32 devices in a mesh: dp: 16 (over z, x, core), tensor: 2 (over y).
Axes of the slice: x: 2, y: 2, z: 4, core: 2. Of those that a mesh axis runs over, the one named last changes fastest.
Arguments:
- inputs: bfloat16 [40960, 1024], P(('dp', 'tensor')), may hold values from -6 to 6
- teacher: bfloat16 [40960, 1024], P(('dp', 'tensor')), may hold values from -6 to 6
- lengths: int32 [128], replicated, may hold values from 200 to 320, as said below
- first_gain: float32 [1024], replicated, may hold values from 0.5 to 1.5
- first_shift: float32 [1024], replicated, may hold values from -0.2 to 0.2
- query_key_value_weight: bfloat16 [3, 1024, 1024], P(None, 'dp', 'tensor'), may hold values from -0.1875 to 0.1875
- heads_bias: float32 [2, 1024], P(None, 'tensor'), may hold values from -0.2 to 0.2
- merge_weight: bfloat16 [1024, 1024], P('dp', 'tensor'), may hold values from -1.5 to 1.5
- merge_bias: float32 [1024], replicated, may hold values from -0.6 to 0.6
- second_gain: float32 [1024], replicated, may hold values from 0.5 to 1.5
- second_shift: float32 [1024], replicated, may hold values from -0.6 to 0.6
- expand_weight: bfloat16 [1024, 4096], P('dp', 'tensor'), may hold values from -0.1875 to 0.1875
- expand_bias: float32 [4096], P('tensor'), may hold values from -0.6 to 0.6
- reduce_weight: bfloat16 [1024, 4096], P('dp', 'tensor'), may hold values from -0.09375 to 0.09375
- reduce_bias: float32 [1024], replicated, may hold values from -0.6 to 0.6
Outputs:
- loss_value: float32 [], replicated
- outputs: bfloat16 [40960, 1024], P(('dp', 'tensor'))
- inputs_grad: float32 [40960, 1024], P(('dp', 'tensor'))
- first_gain_grad: float32 [1024], replicated
- first_shift_grad: float32 [1024], replicated
- heads_weight_grad: float32 [3, 1024, 1024], P(None, 'dp', 'tensor')
- heads_bias_grad: float32 [2, 1024], P(None, 'tensor')
- merge_weight_grad: float32 [1024, 1024], P('dp', 'tensor')
- merge_bias_grad: float32 [1024], replicated
- second_gain_grad: float32 [1024], replicated
- second_shift_grad: float32 [1024], replicated
- expand_weight_grad: float32 [1024, 4096], P('dp', 'tensor')
- expand_bias_grad: float32 [4096], P('tensor')
- reduce_weight_grad: float32 [1024, 4096], P('dp', 'tensor')
- reduce_bias_grad: float32 [1024], replicated
The draws below stay inside these ranges and needn't reach their ends.
Inputs may be any that keep to these rules, and one draw needn't show every extreme that they name: `lengths`: in every draw some image has all 320 slots valid.
All inputs are finite; a program needn't handle non-finite values.
Results may differ from the reference program's by a relative error of at most 0.0095.
Values may be sent and summed in bfloat16 or wider, within the bound.
A program may use at most 320 MiB of HBM per device.

```python
import math
import jax
import jax.numpy as jnp
from jax import lax

D = 1024
HD = 64
FF = 4096
SLOTS = 320
MIN_LEN = 200
IMG_DEV = 8
IMAGES = 128
TOKENS = 40960


def draw_lengths(key, part):
    first_key, second_key = jax.random.split(jax.random.fold_in(key, 17))
    drawn = jax.random.randint(first_key, (IMAGES,), MIN_LEN, SLOTS + 1)
    chosen = jax.random.randint(second_key, (), 0, IMAGES)
    return jnp.where(jnp.arange(IMAGES) == chosen, SLOTS, drawn).astype(jnp.int32)


def block_scale(own_key, dims, pieces, least, high):
    factor_of, own = 1.0, jax.random.fold_in(own_key, 6)
    for dim, parts in pieces:
        heights = jnp.exp(jax.random.uniform(jax.random.fold_in(own, dim), (parts,), jnp.float32, least / len(pieces), high / len(pieces)))
        factor_of = factor_of * jnp.repeat(heights, dims[dim] // parts).reshape([-1 if axis == dim else 1 for axis in range(len(dims))])
    return factor_of


def gaussian(rng, dims, deviation, limit, cuts=(), kind=jnp.bfloat16):
    values = jax.random.normal(rng, dims, jnp.float32) * deviation
    if len(cuts) > 0:
        values = block_scale(rng, dims, cuts, -0.22, 0.18) * values
    return jnp.clip(values, min=-limit, max=limit).astype(kind)


def setup_inputs(seed: int = 0) -> dict:
    key_of = jax.random.split(jax.random.key(seed), 16)
    inputs = gaussian(key_of[0], (TOKENS, D), 1.0, 6.0, ((0, 32),))
    teacher = gaussian(key_of[1], (TOKENS, D), 1.0, 6.0, ((0, 32),))
    lengths = draw_lengths(jax.random.fold_in(key_of[15], 71), 0)
    first_gain = jnp.clip(1.0 + 0.1 * jax.random.normal(key_of[3], (D,), jnp.float32), 0.5, 1.5)
    first_shift = gaussian(key_of[4], (D,), 0.03, 0.2, (), jnp.float32)
    query_key_value_weight = gaussian(key_of[5], (3, D, D), D ** -0.5, 0.1875, ((1, 16), (2, 2)))
    heads_bias = gaussian(key_of[6], (2, D), 0.03, 0.2, ((1, 2),), jnp.float32)
    merge_weight = gaussian(key_of[7], (D, D), (D // 64) ** -0.5, 1.5, ((0, 16), (1, 2)))
    merge_bias = gaussian(key_of[8], (D,), 0.1, 0.6, (), jnp.float32)
    second_gain = jnp.clip(1.0 + 0.1 * jax.random.normal(key_of[9], (D,), jnp.float32), 0.5, 1.5)
    second_shift = gaussian(key_of[10], (D,), 0.1, 0.6, (), jnp.float32)
    expand_weight = gaussian(key_of[11], (D, FF), D ** -0.5, 0.1875, ((0, 16), (1, 2)))
    expand_bias = gaussian(key_of[12], (FF,), 0.1, 0.6, ((0, 2),), jnp.float32)
    reduce_weight = gaussian(key_of[13], (D, FF), FF ** -0.5, 0.09375, ((0, 16), (1, 2)))
    reduce_bias = gaussian(key_of[14], (D,), 0.1, 0.6, (), jnp.float32)
    return {"inputs": inputs, "teacher": teacher, "lengths": lengths, "first_gain": first_gain, "first_shift": first_shift, "query_key_value_weight": query_key_value_weight, "heads_bias": heads_bias, "merge_weight": merge_weight, "merge_bias": merge_bias, "second_gain": second_gain, "second_shift": second_shift, "expand_weight": expand_weight, "expand_bias": expand_bias, "reduce_weight": reduce_weight, "reduce_bias": reduce_bias}


EPSILON = 1e-05
MASKED_SCORE = -1e+30
HIGH_ACCURACY = lax.Precision.HIGHEST

@jax.custom_vjp
def low(v):
    return lax.optimization_barrier(v.astype(jnp.bfloat16)).astype(jnp.float32)

@jax.custom_vjp
def low_back(v):
    return v

def low_keep(v):
    return (low(v), None)

def low_pass(kept, grad):
    return (grad,)

def back_keep(v):
    return (v, None)

def back_low(kept, grad):
    return (low(grad),)
low.defvjp(low_keep, low_pass)
low_back.defvjp(back_keep, back_low)

def layer_norm(rows, gain, shift):
    centre = lax.optimization_barrier(jnp.mean(rows, axis=-1, keepdims=True))
    centred = rows - centre
    spread = lax.optimization_barrier(jnp.mean(centred * centred, axis=-1, keepdims=True))
    return centred * lax.rsqrt(spread + EPSILON) * gain + shift

def layer(params, inputs_f, teacher_f, valid_rows, key_valid, count):
    first_gain, first_shift, query_key_value_weight, heads_bias, merge_weight, merge_bias, second_gain, second_shift, expand_weight, expand_bias, reduce_weight, reduce_bias = params
    group_rows = inputs_f.shape[0]
    images = group_rows // SLOTS
    heads = D // HD
    scale = 1.0 / math.sqrt(HD)
    normalized_rows = low(layer_norm(inputs_f, first_gain, first_shift))
    projected_heads = jnp.einsum('xz,ezi->exi', normalized_rows, query_key_value_weight, precision=HIGH_ACCURACY)
    queries = low(low_back(projected_heads[0] + heads_bias[0]))
    key_rows = low(low_back(projected_heads[1]))
    value_rows = low(low_back(projected_heads[2] + heads_bias[1]))
    query_heads = queries.reshape(images, SLOTS, heads, HD)
    key_heads = key_rows.reshape(images, SLOTS, heads, HD)
    value_heads = value_rows.reshape(images, SLOTS, heads, HD)
    scores = low_back(jnp.einsum('bqhe,bkhe->bhqk', query_heads, key_heads, precision=HIGH_ACCURACY) * scale)
    scores = jnp.where(key_valid[:, None, None, :], scores, MASKED_SCORE)
    attend = low(jax.nn.softmax(scores, axis=-1))
    mixed = jnp.einsum('bhqk,bkhe->bqhe', attend, value_heads, precision=HIGH_ACCURACY).reshape(group_rows, D)
    mixed = low(low_back(mixed))
    branch = low_back(jnp.einsum('rf,df->rd', mixed, merge_weight, precision=HIGH_ACCURACY)) + merge_bias
    hidden_state = inputs_f + branch
    second = low(layer_norm(hidden_state, second_gain, second_shift))
    pre_act = low_back(jnp.dot(second, expand_weight, precision=HIGH_ACCURACY) + expand_bias)
    activ = low(jax.nn.gelu(pre_act, approximate=True))
    feed = low_back(jnp.einsum('rf,df->rd', activ, reduce_weight, precision=HIGH_ACCURACY)) + reduce_bias
    result = (hidden_state + feed) * valid_rows[:, None]
    error = (result - teacher_f) * valid_rows[:, None]
    return (jnp.sum(error * error) / count, result)

def reference(inputs, teacher, lengths, first_gain, first_shift, query_key_value_weight, heads_bias, merge_weight, merge_bias, second_gain, second_shift, expand_weight, expand_bias, reduce_weight, reduce_bias):
    count = jnp.sum(lengths).astype(jnp.float32)
    params = tuple((p.astype(jnp.float32) for p in (first_gain, first_shift, query_key_value_weight, heads_bias, merge_weight, merge_bias, second_gain, second_shift, expand_weight, expand_bias, reduce_weight, reduce_bias)))
    groups = IMAGES // IMG_DEV
    group_rows = IMG_DEV * SLOTS
    slot_valid = jnp.arange(SLOTS, dtype=jnp.int32)[None, :] < lengths[:, None]
    inputs_all = inputs.astype(jnp.float32).reshape(groups, group_rows, D)
    teacher_all = teacher.astype(jnp.float32).reshape(groups, group_rows, D)
    keys_all = slot_valid.reshape(groups, IMG_DEV, SLOTS)
    rows_all = slot_valid.astype(jnp.float32).reshape(groups, group_rows)

    def step(totals, batch_item):
        inputs_g, teacher_g, keys_g, rows_g = batch_item

        def forward(weights, inputs_f):
            return layer(weights, inputs_f, teacher_g, rows_g, keys_g, count)
        loss_part, pullback, result = jax.vjp(forward, params, inputs_g, has_aux=True)
        weight_grads, inputs_g_grad = pullback(jnp.ones_like(loss_part))
        new_totals = (totals[0] + loss_part, jax.tree.map(lambda p, q: p + q, totals[1], weight_grads))
        return (new_totals, (result.astype(jnp.bfloat16), inputs_g_grad))
    start = (jnp.zeros((), jnp.float32), jax.tree.map(jnp.zeros_like, params))
    (loss_value, grads), (results, input_grads) = lax.scan(step, start, (inputs_all, teacher_all, keys_all, rows_all))
    return (loss_value, results.reshape(TOKENS, D), input_grads.reshape(TOKENS, D), grads[0], grads[1], grads[2], grads[3], grads[4], grads[5], grads[6], grads[7], grads[8], grads[9], grads[10], grads[11])
```

```python
from functools import partial

import jax
import jax.numpy as jnp
from jax import lax
from jax.experimental import pallas as pl
from jax.experimental.pallas import tpu as pltpu
from jax.sharding import PartitionSpec as P

HD = 64
SLOTS = 320
PAIR = 2 * HD

EPSILON = 1e-05
MASKED_SCORE = -1e30
F32 = jnp.float32
BF16 = jnp.bfloat16
EVERY = ("tensor", "dp")


def layer_norm(rows, gain, shift):
    centre = jnp.mean(rows, axis=-1, keepdims=True)
    centred = rows - centre
    spread = jnp.mean(centred * centred, axis=-1, keepdims=True)
    return centred * lax.rsqrt(spread + EPSILON) * gain + shift


def two_heads(pair):
    first = lax.broadcasted_iota(jnp.int32, pair.shape, 1) < HD
    zero = jnp.zeros_like(pair)
    return jnp.concatenate([jnp.where(first, pair, zero), jnp.where(first, zero, pair)], axis=0)


def one_pair(stacked):
    first = lax.broadcasted_iota(jnp.int32, (SLOTS, PAIR), 1) < HD
    return jnp.where(first, stacked[:SLOTS], stacked[SLOTS:])


def dot(left, right, left_dim, right_dim):
    return lax.dot_general(
        left, right, (((left_dim,), (right_dim,)), ((), ())), preferred_element_type=F32
    )


def masked_scores(query_stack, keys, length):
    scores = dot(keys, query_stack, 1, 1)
    slot = lax.broadcasted_iota(jnp.int32, scores.shape, 0)
    return jnp.where(slot < length, scores, MASKED_SCORE)


def attend_kernel(lengths_ref, qkv_ref, mixed_ref, log_ref):
    length = lengths_ref[pl.program_id(1)]
    query_stack = two_heads(qkv_ref[0] * 0.125)
    scores = masked_scores(query_stack, qkv_ref[1], length)
    highest = jnp.max(scores, axis=0, keepdims=True)
    expo = jnp.exp(scores - highest)
    totals = jnp.sum(expo, axis=0, keepdims=True)
    mixed = dot(qkv_ref[2], expo.astype(BF16), 0, 0) * (1.0 / totals)
    mixed_ref[...] = one_pair(mixed.T).astype(BF16)
    log_ref[0] = highest + jnp.log(totals)


def attend_back_kernel(lengths_ref, qkv_ref, mixed_grad_ref, log_ref, grad_ref, bias_ref):
    image = pl.program_id(1)
    length = lengths_ref[image]
    query_stack = two_heads(qkv_ref[0] * 0.125)
    keys = qkv_ref[1]
    scores = masked_scores(query_stack, keys, length)
    attend = jnp.exp(scores - log_ref[0])
    grad_stack = two_heads(mixed_grad_ref[...])
    attend_grad = dot(qkv_ref[2], grad_stack, 1, 1)
    value_grad = dot(attend.astype(BF16), grad_stack, 1, 0).astype(BF16)
    centre = jnp.sum(attend * attend_grad, axis=0, keepdims=True)
    score_grad = (attend * (attend_grad - centre)).astype(BF16)
    key_grad = dot(score_grad, query_stack, 1, 0).astype(BF16)
    query_grad = dot(keys, score_grad, 0, 0)
    query_grad = (one_pair(query_grad.T) * 0.125).astype(BF16)
    grad_ref[0] = query_grad
    grad_ref[1] = key_grad
    grad_ref[2] = value_grad

    @pl.when(image == 0)
    def _():
        bias_ref[...] = jnp.zeros_like(bias_ref)

    bias_ref[0, 0:1] += jnp.sum(query_grad.astype(F32), axis=0, keepdims=True)
    bias_ref[0, 1:2] += jnp.sum(value_grad.astype(F32), axis=0, keepdims=True)


def attend(lengths, qkv):
    rows, width = qkv.shape[1:]
    images, pairs = rows // SLOTS, width // PAIR
    return pl.pallas_call(
        attend_kernel,
        grid_spec=pltpu.PrefetchScalarGridSpec(
            num_scalar_prefetch=1,
            grid=(pairs, images),
            in_specs=[pl.BlockSpec((3, SLOTS, PAIR), lambda p, i, s: (0, i, p))],
            out_specs=[
                pl.BlockSpec((SLOTS, PAIR), lambda p, i, s: (i, p)),
                pl.BlockSpec((1, 1, 2 * SLOTS), lambda p, i, s: (p * images + i, 0, 0)),
            ],
        ),
        out_shape=[
            jax.ShapeDtypeStruct((rows, width), BF16),
            jax.ShapeDtypeStruct((pairs * images, 1, 2 * SLOTS), F32),
        ],
        compiler_params=pltpu.CompilerParams(vmem_limit_bytes=48 * 2**20),
        cost_estimate=pl.CostEstimate(
            flops=4 * rows * SLOTS * width * 4, bytes_accessed=8 * rows * width,
            transcendentals=rows * SLOTS * width // HD,
        ),
        name="attend",
    )(lengths, qkv)


def attend_back(lengths, qkv, mixed_grad, log_total):
    rows, width = qkv.shape[1:]
    images, pairs = rows // SLOTS, width // PAIR
    return pl.pallas_call(
        attend_back_kernel,
        grid_spec=pltpu.PrefetchScalarGridSpec(
            num_scalar_prefetch=1,
            grid=(pairs, images),
            in_specs=[
                pl.BlockSpec((3, SLOTS, PAIR), lambda p, i, s: (0, i, p)),
                pl.BlockSpec((SLOTS, PAIR), lambda p, i, s: (i, p)),
                pl.BlockSpec((1, 1, 2 * SLOTS), lambda p, i, s: (p * images + i, 0, 0)),
            ],
            out_specs=[
                pl.BlockSpec((3, SLOTS, PAIR), lambda p, i, s: (0, i, p)),
                pl.BlockSpec((1, 2, PAIR), lambda p, i, s: (p, 0, 0)),
            ],
        ),
        out_shape=[
            jax.ShapeDtypeStruct((3, rows, width), BF16),
            jax.ShapeDtypeStruct((pairs, 2, PAIR), F32),
        ],
        compiler_params=pltpu.CompilerParams(vmem_limit_bytes=48 * 2**20),
        cost_estimate=pl.CostEstimate(
            flops=10 * rows * SLOTS * width * 4, bytes_accessed=14 * rows * width,
            transcendentals=rows * SLOTS * width // HD,
        ),
        name="attend_back",
    )(lengths, qkv, mixed_grad, log_total)


def whole(weight, axis):
    full = lax.all_gather(weight, EVERY, axis=axis, tiled=True)
    halves = lax.axis_size("tensor")
    shape = full.shape
    return full.reshape(*shape[:axis], halves, shape[axis] // halves, *shape[axis + 1 :])


def scatter(grad, axis):
    shape = grad.shape
    flat = grad.reshape(*shape[:axis], shape[axis] * shape[axis + 1], *shape[axis + 2 :])
    return lax.psum_scatter(flat, EVERY, scatter_dimension=axis, tiled=True).astype(F32)


def body(
    inputs,
    teacher,
    lengths,
    first_gain,
    first_shift,
    query_key_value_weight,
    heads_bias,
    merge_weight,
    merge_bias,
    second_gain,
    second_shift,
    expand_weight,
    expand_bias,
    reduce_weight,
    reduce_bias,
):
    rows, width = inputs.shape
    images = rows // SLOTS
    halves = lax.axis_size("tensor")
    hidden = expand_weight.shape[1] * halves
    place = lax.axis_index("dp") * halves + lax.axis_index("tensor")
    mine = lax.dynamic_slice_in_dim(lengths, place * images, images)
    row_valid = (jnp.arange(SLOTS, dtype=jnp.int32)[None, :] < mine[:, None]).reshape(rows, 1)
    row_valid = row_valid.astype(F32)
    count = jnp.sum(lengths).astype(F32)

    heads_bias = lax.all_gather(heads_bias, "tensor", axis=1, tiled=True)
    expand_bias = lax.all_gather(expand_bias, "tensor", axis=0, tiled=True)
    qkv_full = whole(query_key_value_weight, 1)
    merge_full = whole(merge_weight, 0)
    expand_full = whole(expand_weight, 0)
    reduce_full = whole(reduce_weight, 0)

    inputs_f = inputs.astype(F32)
    normed, first_back = jax.vjp(layer_norm, inputs_f, first_gain, first_shift)
    normed = normed.astype(BF16)
    qkv_bias = jnp.stack([heads_bias[0], jnp.zeros_like(heads_bias[0]), heads_bias[1]])
    qkv = jnp.einsum("xz,ejzi->exji", normed, qkv_full, preferred_element_type=F32)
    qkv = (qkv.reshape(3, rows, width) + qkv_bias[:, None, :]).astype(BF16)
    mixed, log_total = attend(mine, qkv)
    branch = jnp.einsum(
        "rjf,jdf->rd", mixed.reshape(rows, halves, -1), merge_full, preferred_element_type=F32
    )
    hidden_state = inputs_f + branch + merge_bias
    second, second_back = jax.vjp(layer_norm, hidden_state, second_gain, second_shift)
    second = second.astype(BF16)
    pre_act = jnp.einsum("rd,jdf->rjf", second, expand_full, preferred_element_type=F32)
    pre_act = pre_act + expand_bias.reshape(halves, -1)
    activ, gelu_back = jax.vjp(partial(jax.nn.gelu, approximate=True), pre_act)
    activ = activ.astype(BF16)
    feed = jnp.einsum("rjf,jdf->rd", activ, reduce_full, preferred_element_type=F32)
    result = (hidden_state + feed + reduce_bias) * row_valid
    error = (result - teacher.astype(F32)) * row_valid
    loss_part = jnp.sum(error * error)
    result_grad = 2.0 * error / count

    result_grad_b = result_grad.astype(BF16)
    reduce_grad = scatter(
        jnp.einsum("rd,rjf->jdf", result_grad_b, activ, preferred_element_type=F32).astype(BF16), 0
    )
    activ_grad = jnp.einsum("rd,jdf->rjf", result_grad_b, reduce_full, preferred_element_type=F32)
    pre_grad = gelu_back(activ_grad)[0].astype(BF16)
    expand_bias_grad = jnp.sum(pre_grad, axis=0, dtype=F32).reshape(hidden)
    expand_grad = scatter(
        jnp.einsum("rd,rjf->jdf", second, pre_grad, preferred_element_type=F32).astype(BF16), 0
    )
    second_grad = jnp.einsum("rjf,jdf->rd", pre_grad, expand_full, preferred_element_type=F32)
    hidden_ln_grad, second_gain_grad, second_shift_grad = second_back(second_grad)
    hidden_grad = result_grad + hidden_ln_grad
    reduce_bias_grad = jnp.sum(result_grad, axis=0)
    merge_bias_grad = jnp.sum(hidden_grad, axis=0)
    hidden_grad_b = hidden_grad.astype(BF16)
    merge_grad = scatter(
        jnp.einsum(
            "rd,rjf->jdf", hidden_grad_b, mixed.reshape(rows, halves, -1), preferred_element_type=F32
        ).astype(BF16),
        0,
    )
    mixed_grad = jnp.einsum("rd,jdf->rjf", hidden_grad_b, merge_full, preferred_element_type=F32)
    mixed_grad = mixed_grad.astype(BF16).reshape(rows, width)
    qkv_grad, bias_grad = attend_back(mine, qkv, mixed_grad, log_total)
    heads_bias_grad = jnp.moveaxis(bias_grad, 1, 0).reshape(2, width)
    qkv_grad = qkv_grad.reshape(3, rows, halves, -1)
    heads_grad = scatter(
        jnp.einsum("rb,mrjx->mjbx", normed, qkv_grad, preferred_element_type=F32).astype(BF16), 1
    )
    normed_grad = jnp.einsum("mejx,mjwx->ew", qkv_grad, qkv_full, preferred_element_type=F32)
    inputs_ln_grad, first_gain_grad, first_shift_grad = first_back(normed_grad)
    inputs_grad = hidden_grad + inputs_ln_grad

    small = jnp.concatenate(
        [
            first_gain_grad,
            first_shift_grad,
            second_gain_grad,
            second_shift_grad,
            merge_bias_grad,
            reduce_bias_grad,
            heads_bias_grad.reshape(-1),
            expand_bias_grad,
            loss_part.reshape(1),
        ]
    )
    small = lax.psum(small, EVERY)
    vectors = small[: 6 * width].reshape(6, width)
    tensor = lax.axis_index("tensor")
    heads_bias_sum = lax.dynamic_slice_in_dim(
        small[6 * width : 8 * width].reshape(2, width), tensor * (width // halves), width // halves, 1
    )
    expand_bias_sum = lax.dynamic_slice_in_dim(
        small, 8 * width + tensor * (hidden // halves), hidden // halves
    )
    return (
        small[-1] / count,
        result.astype(BF16),
        inputs_grad,
        vectors[0],
        vectors[1],
        heads_grad,
        heads_bias_sum,
        merge_grad,
        vectors[4],
        vectors[2],
        vectors[3],
        expand_grad,
        expand_bias_sum,
        reduce_grad,
        vectors[5],
    )


def solution(mesh):
    return jax.shard_map(
        body,
        mesh=mesh,
        in_specs=(
            P(("dp", "tensor"), None),
            P(("dp", "tensor"), None),
            P(),
            P(),
            P(),
            P(None, "dp", "tensor"),
            P(None, "tensor"),
            P("dp", "tensor"),
            P(),
            P(),
            P(),
            P("dp", "tensor"),
            P("tensor"),
            P("dp", "tensor"),
            P(),
        ),
        out_specs=(
            P(),
            P(("dp", "tensor"), None),
            P(("dp", "tensor"), None),
            P(),
            P(),
            P(None, "dp", "tensor"),
            P(None, "tensor"),
            P("dp", "tensor"),
            P(),
            P(),
            P(),
            P("dp", "tensor"),
            P("tensor"),
            P("dp", "tensor"),
            P(),
        ),
        check_vma=False,
    )
```

```python
from functools import partial
import math

import jax
import jax.numpy as jnp
from jax import lax
from jax.experimental import pallas as pl
from jax.experimental.pallas import tpu as pltpu
from jax.sharding import PartitionSpec as P

HD = 64
SLOTS = 320
PAIR = 2 * HD

EPSILON = 1e-05
MASKED_SCORE = -1e30
F32 = jnp.float32
BF16 = jnp.bfloat16
EVERY = ("tensor", "dp")
CORES = 2
LINE = 4


def layer_norm(rows, gain, shift):
    centre = jnp.mean(rows, axis=-1, keepdims=True)
    centred = rows - centre
    spread = jnp.mean(centred * centred, axis=-1, keepdims=True)
    return centred * lax.rsqrt(spread + EPSILON) * gain + shift


def two_heads(pair):
    first = lax.broadcasted_iota(jnp.int32, pair.shape, 1) < HD
    zero = jnp.zeros_like(pair)
    return jnp.concatenate([jnp.where(first, pair, zero), jnp.where(first, zero, pair)], axis=0)


def one_pair(stacked):
    first = lax.broadcasted_iota(jnp.int32, (SLOTS, PAIR), 1) < HD
    return jnp.where(first, stacked[:SLOTS], stacked[SLOTS:])


def dot(left, right, left_dim, right_dim):
    return lax.dot_general(
        left, right, (((left_dim,), (right_dim,)), ((), ())), preferred_element_type=F32
    )


def masked_scores(query_stack, keys, length):
    scores = dot(keys, query_stack, 1, 1)
    slot = lax.broadcasted_iota(jnp.int32, scores.shape, 0)
    return jnp.where(slot < length, scores, MASKED_SCORE)


def attend_kernel(lengths_ref, qkv_ref, mixed_ref, log_ref):
    length = lengths_ref[pl.program_id(1)]
    query_stack = two_heads(qkv_ref[0] * 0.125)
    scores = masked_scores(query_stack, qkv_ref[1], length)
    highest = jnp.max(scores, axis=0, keepdims=True)
    expo = jnp.exp(scores - highest)
    totals = jnp.sum(expo, axis=0, keepdims=True)
    mixed = dot(qkv_ref[2], expo.astype(BF16), 0, 0) * (1.0 / totals)
    mixed_ref[...] = one_pair(mixed.T).astype(BF16)
    log_ref[0] = highest + jnp.log(totals)


def attend_back_kernel(lengths_ref, qkv_ref, mixed_grad_ref, log_ref, grad_ref, bias_ref):
    image = pl.program_id(1)
    length = lengths_ref[image]
    query_stack = two_heads(qkv_ref[0] * 0.125)
    keys = qkv_ref[1]
    scores = masked_scores(query_stack, keys, length)
    attend = jnp.exp(scores - log_ref[0])
    grad_stack = two_heads(mixed_grad_ref[...])
    attend_grad = dot(qkv_ref[2], grad_stack, 1, 1)
    value_grad = dot(attend.astype(BF16), grad_stack, 1, 0).astype(BF16)
    centre = jnp.sum(attend * attend_grad, axis=0, keepdims=True)
    score_grad = (attend * (attend_grad - centre)).astype(BF16)
    key_grad = dot(score_grad, query_stack, 1, 0).astype(BF16)
    query_grad = dot(keys, score_grad, 0, 0)
    query_grad = (one_pair(query_grad.T) * 0.125).astype(BF16)
    grad_ref[0] = query_grad
    grad_ref[1] = key_grad
    grad_ref[2] = value_grad

    @pl.when(image == 0)
    def _():
        bias_ref[...] = jnp.zeros_like(bias_ref)

    bias_ref[0, 0:1] += jnp.sum(query_grad.astype(F32), axis=0, keepdims=True)
    bias_ref[0, 1:2] += jnp.sum(value_grad.astype(F32), axis=0, keepdims=True)


def attend(lengths, qkv):
    rows, width = qkv.shape[1:]
    images, pairs = rows // SLOTS, width // PAIR
    return pl.pallas_call(
        attend_kernel,
        grid_spec=pltpu.PrefetchScalarGridSpec(
            num_scalar_prefetch=1,
            grid=(pairs, images),
            in_specs=[pl.BlockSpec((3, SLOTS, PAIR), lambda p, i, s: (0, i, p))],
            out_specs=[
                pl.BlockSpec((SLOTS, PAIR), lambda p, i, s: (i, p)),
                pl.BlockSpec((1, 1, 2 * SLOTS), lambda p, i, s: (p * images + i, 0, 0)),
            ],
        ),
        out_shape=[
            jax.ShapeDtypeStruct((rows, width), BF16),
            jax.ShapeDtypeStruct((pairs * images, 1, 2 * SLOTS), F32),
        ],
        compiler_params=pltpu.CompilerParams(vmem_limit_bytes=48 * 2**20),
        cost_estimate=pl.CostEstimate(
            flops=4 * rows * SLOTS * width * 4, bytes_accessed=8 * rows * width,
            transcendentals=rows * SLOTS * width // HD,
        ),
        name="attend",
    )(lengths, qkv)


def attend_back(lengths, qkv, mixed_grad, log_total):
    rows, width = qkv.shape[1:]
    images, pairs = rows // SLOTS, width // PAIR
    return pl.pallas_call(
        attend_back_kernel,
        grid_spec=pltpu.PrefetchScalarGridSpec(
            num_scalar_prefetch=1,
            grid=(pairs, images),
            in_specs=[
                pl.BlockSpec((3, SLOTS, PAIR), lambda p, i, s: (0, i, p)),
                pl.BlockSpec((SLOTS, PAIR), lambda p, i, s: (i, p)),
                pl.BlockSpec((1, 1, 2 * SLOTS), lambda p, i, s: (p * images + i, 0, 0)),
            ],
            out_specs=[
                pl.BlockSpec((3, SLOTS, PAIR), lambda p, i, s: (0, i, p)),
                pl.BlockSpec((1, 2, PAIR), lambda p, i, s: (p, 0, 0)),
            ],
        ),
        out_shape=[
            jax.ShapeDtypeStruct((3, rows, width), BF16),
            jax.ShapeDtypeStruct((pairs, 2, PAIR), F32),
        ],
        compiler_params=pltpu.CompilerParams(vmem_limit_bytes=48 * 2**20),
        cost_estimate=pl.CostEstimate(
            flops=10 * rows * SLOTS * width * 4, bytes_accessed=14 * rows * width,
            transcendentals=rows * SLOTS * width // HD,
        ),
        name="attend_back",
    )(lengths, qkv, mixed_grad, log_total)


AXES = ("tensor", "line", "row", "core")
MESH = pl.DeviceIdType.MESH
GATHER_ORDERS = (
    (("line", "tensor", "row"), ("line", "row", "tensor")),
    (("tensor", "row", "line"), ("row", "tensor", "line")),
)


def sizes():
    return {"tensor": lax.axis_size("tensor"), "line": LINE, "row": lax.axis_size("dp") // (LINE * CORES), "core": CORES}


class Place:
    def __init__(self):
        self.size = sizes()
        index = lax.axis_index("dp")
        self.at = {
            "tensor": lax.axis_index("tensor"),
            "core": lax.rem(index, CORES),
            "row": lax.rem(lax.div(index, CORES), self.size["row"]),
            "line": lax.div(index, CORES * self.size["row"]),
        }

    def steps(self, axis):
        return range(1, self.size[axis])

    def peer(self, axis, step):
        return lax.rem(self.at[axis] + step, self.size[axis])

    def device(self, axis, place):
        at = {**self.at, axis: place}
        return {"dp": (at["line"] * self.size["row"] + at["row"]) * CORES + at["core"], "tensor": at["tensor"]}

    def greet(self):
        barrier = pltpu.get_barrier_semaphore()
        count = 0
        for axis in AXES:
            for step in self.steps(axis):
                pl.semaphore_signal(barrier, inc=1, device_id=self.device(axis, self.peer(axis, step)), device_id_type=MESH)
                count += 1
        pl.semaphore_wait(barrier, count)


def pieces_of(shards, width):
    out = []
    for a, shard in enumerate(shards):
        for lead in range(shard.shape[0]) if len(shard.shape) == 3 else (None,):
            for col in range(shard.shape[-1] // width):
                out.append((a, lead, col))
    return out


def piece(refs, which, width):
    a, lead, col = which
    ref = refs[a] if lead is None else refs[a].at[lead]
    spare = (slice(None),) * (len(ref.shape) - 1)
    return ref.at[(*spare, pl.ds(col * width, width))]


def gather_kernel(pieces, width, orders, lag, n_weights, n_biases, *refs):
    n_in = n_weights + n_biases
    ins, outs = refs[:n_in], refs[n_in : 2 * n_in]
    send_sem, recv_sem, own_sem, bias_send, bias_recv, bias_own = refs[2 * n_in :]
    here = Place()
    here.greet()
    half = ins[0].shape[-2] // 2
    count = len(pieces)

    def region(n, h, stage, axis=None, place=None):
        order = (*orders[n][h], "core")
        index = [
            slice(None) if a in order[:stage] else place if a == axis else here.at[a] for a in AXES
        ]
        return piece(outs, pieces[n], width).at[(*index, pl.ds(h * half, half))]

    def remote(n, h, stage, step, coming=False):
        axis = (*orders[n][h], "core")[stage]
        slot = (n, h, stage, step - 1)
        to = region(n, h, stage)
        source = piece(ins, pieces[n], width).at[pl.ds(h * half, half)] if stage == 0 else to
        if coming:
            to = region(n, h, stage, axis, here.peer(axis, here.size[axis] - step))
        return pltpu.make_async_remote_copy(
            src_ref=source, dst_ref=to, send_sem=send_sem.at[slot], recv_sem=recv_sem.at[slot],
            device_id=here.device(axis, here.peer(axis, step)), device_id_type=MESH,
        )

    def every(n, stage, act):
        for h in range(2):
            for step in here.steps((*orders[n][h], "core")[stage]):
                act(n, h, stage, step)

    def own(n):
        place = tuple(here.at[a] for a in AXES)
        return pltpu.make_async_copy(
            piece(ins, pieces[n], width), piece(outs, pieces[n], width).at[place], own_sem.at[n]
        )

    def bias(b, step, coming=False):
        ref, out = ins[n_weights + b], outs[n_weights + b]
        place = here.peer("tensor", here.size["tensor"] - step) if coming else here.at["tensor"]
        return pltpu.make_async_remote_copy(
            src_ref=ref, dst_ref=out.at[place], send_sem=bias_send.at[b, step - 1],
            recv_sem=bias_recv.at[b, step - 1],
            device_id=here.device("tensor", here.peer("tensor", step)), device_id_type=MESH,
        )

    def own_bias(b):
        return pltpu.make_async_copy(
            ins[n_weights + b], outs[n_weights + b].at[here.at["tensor"]], bias_own.at[b]
        )

    start = lambda *k: remote(*k).start()
    arrived = lambda *k: remote(*k, coming=True).wait_recv()
    sent = lambda *k: remote(*k).wait_send()
    for n in range(count):
        every(n, 0, start)
        own(n).start()
    for b in range(n_biases):
        own_bias(b).start()
        for step in here.steps("tensor"):
            bias(b, step).start()
    for tick in range(count + 3 * lag):
        for stage in range(1, 4):
            n = tick - lag * (stage - 1)
            if 0 <= n < count:
                if stage == 1:
                    own(n).wait()
                every(n, stage - 1, arrived)
                every(n, stage, start)
    for n in range(count):
        every(n, 3, arrived)
        for stage in range(4):
            every(n, stage, sent)
    for b in range(n_biases):
        own_bias(b).wait()
        for step in here.steps("tensor"):
            bias(b, step, coming=True).wait_recv()
            bias(b, step).wait_send()


def gather(weights, biases, collective_id, width, third=(), lag=2):
    size = sizes()
    lead = tuple(size[a] for a in AXES)
    outs = [jax.ShapeDtypeStruct((*w.shape[:-2], *lead, *w.shape[-2:]), w.dtype) for w in weights]
    outs += [jax.ShapeDtypeStruct((size["tensor"], *b.shape), b.dtype) for b in biases]
    pieces = pieces_of(weights, width)
    count, most, total = len(pieces), max(size.values()) - 1, len(weights) + len(biases)
    orders = [GATHER_ORDERS[n in third] for n in range(count)]
    few = max(len(biases), 1)
    return pl.pallas_call(
        partial(gather_kernel, pieces, width, orders, lag, len(weights), len(biases)),
        out_shape=outs,
        in_specs=[pl.BlockSpec(memory_space=pl.ANY)] * total,
        out_specs=[pl.BlockSpec(memory_space=pl.ANY)] * total,
        scratch_shapes=[
            pltpu.SemaphoreType.DMA((count, 2, 4, most)),
            pltpu.SemaphoreType.DMA((count, 2, 4, most)),
            pltpu.SemaphoreType.DMA((count,)),
            pltpu.SemaphoreType.DMA((few, size["tensor"])),
            pltpu.SemaphoreType.DMA((few, size["tensor"])),
            pltpu.SemaphoreType.DMA((few,)),
        ],
        compiler_params=pltpu.CompilerParams(collective_id=collective_id, has_side_effects=True),
        name="gather",
    )(*weights, *biases)


SCATTER_ORDERS = (
    (("tensor", "row", "line"), ("row", "tensor", "line")),
    (("line", "tensor", "row"), ("line", "row", "tensor")),
)
SUM_AXES = ("core", "tensor", "row", "line")


def scatter_kernel(pieces, width, orders, lag, n_grads, *refs):
    ins, small = refs[:n_grads], refs[n_grads]
    outs, small_out = refs[n_grads + 1 : 2 * n_grads + 1], refs[2 * n_grads + 1]
    own_buf, first_buf, *rest = refs[2 * n_grads + 2 :]
    count = len(pieces)
    late = {(n, h, s): rest[(n * 2 + h) * 3 + s - 1] for n in range(count) for h in range(2) for s in (1, 2, 3)}
    small_bufs = rest[6 * count : 6 * count + 4]
    send_sem, recv_sem, own_sem, small_send, small_recv = rest[6 * count + 4 :]
    here = Place()
    here.greet()
    half = own_buf.shape[-2] // 2
    three = AXES[:3]

    def own(n):
        source = piece(ins, pieces[n], width).at[:, :, :, here.at["core"]]
        return pltpu.make_async_copy(source, own_buf.at[n], own_sem.at[n])

    def to_core(n):
        other = here.peer("core", 1)
        return pltpu.make_async_remote_copy(
            src_ref=piece(ins, pieces[n], width).at[:, :, :, other], dst_ref=first_buf.at[n],
            send_sem=send_sem.at[n, 0, 0, 0], recv_sem=recv_sem.at[n, 0, 0, 0],
            device_id=here.device("core", other), device_id_type=MESH,
        )

    def remote(n, h, stage, step):
        order = orders[n][h]
        axis = order[stage - 1]
        to = here.peer(axis, step)
        index = [
            here.at[a] if a in order[: stage - 1] else to if a == axis else slice(None) for a in three
        ]
        slot = (n, h, stage, step - 1)
        return pltpu.make_async_remote_copy(
            src_ref=own_buf.at[(n, *index, pl.ds(h * half, half))],
            dst_ref=late[n, h, stage].at[step - 1],
            send_sem=send_sem.at[slot], recv_sem=recv_sem.at[slot],
            device_id=here.device(axis, to), device_id_type=MESH,
        )

    def every(n, stage, act):
        for h in range(2):
            for step in here.steps(orders[n][h][stage - 1]):
                act(remote(n, h, stage, step))

    def add_core(n):
        def one(i, _):
            first, left = lax.div(i, here.size["row"]), lax.rem(i, here.size["row"])
            at = (n, lax.div(first, LINE), lax.rem(first, LINE), left)
            own_buf[at] = (own_buf[at].astype(F32) + first_buf[at].astype(F32)).astype(BF16)
            return 0

        lax.fori_loop(0, math.prod(here.size[a] for a in three), one, 0)

    def add(n, h, stage):
        order = orders[n][h]
        buf, steps = late[n, h, stage], here.size[order[stage - 1]] - 1
        free = [a for a in three if a not in order[:stage]]
        rows = pl.ds(h * half, half)

        def one(i, _):
            at, left = dict(here.at), i
            for a in reversed(free):
                at[a] = lax.rem(left, here.size[a])
                left = lax.div(left, here.size[a])
            mine = (n, *(at[a] for a in three), rows)
            total = own_buf[mine].astype(F32)
            for s in range(steps):
                total += buf[(s, *(at[a] for a in free))].astype(F32)
            if stage == 3:
                out = piece(outs, pieces[n], width)
                out[rows, :] = total
            else:
                own_buf[mine] = total.astype(BF16)
            return 0

        if free:
            lax.fori_loop(0, math.prod(here.size[a] for a in free), one, 0)
        else:
            one(0, 0)

    def small_copy(stage, step, coming=False):
        axis = SUM_AXES[stage]
        place = here.peer(axis, here.size[axis] - step) if coming else here.at[axis]
        buf = small_bufs[stage]
        return pltpu.make_async_remote_copy(
            src_ref=buf.at[here.at[axis]], dst_ref=buf.at[place],
            send_sem=small_send.at[stage, step - 1], recv_sem=small_recv.at[stage, step - 1],
            device_id=here.device(axis, here.peer(axis, step)), device_id_type=MESH,
        )

    def small_start(stage, value):
        axis = SUM_AXES[stage]
        small_bufs[stage][here.at[axis]] = value
        for step in here.steps(axis):
            small_copy(stage, step).start()

    def small_end(stage):
        axis = SUM_AXES[stage]
        for step in here.steps(axis):
            small_copy(stage, step, coming=True).wait_recv()
            small_copy(stage, step).wait_send()
        total = small_bufs[stage][0]
        for place in range(1, here.size[axis]):
            total += small_bufs[stage][place]
        return total

    for n in range(count):
        to_core(n).start()
        own(n).start()
    small_start(0, small[...])
    for tick in range(max(count + 3 * lag, 5)):
        if 1 <= tick <= 4:
            total = small_end(tick - 1)
            if tick < 4:
                small_start(tick, total)
            else:
                small_out[...] = total
        for stage in range(4):
            n = tick - lag * stage
            if not 0 <= n < count:
                continue
            if stage == 0:
                own(n).wait()
                to_core(n).wait_recv()
                add_core(n)
            else:
                every(n, stage, lambda copy: copy.wait_recv())
                for h in range(2):
                    add(n, h, stage)
            if stage < 3:
                every(n, stage + 1, lambda copy: copy.start())
    for n in range(count):
        to_core(n).wait_send()
        for stage in (1, 2, 3):
            every(n, stage, lambda copy: copy.wait_send())


def scatter(grads, small, collective_id, width, third=(), lag=2):
    size = sizes()
    shards = [jax.ShapeDtypeStruct((*g.shape[:-6], *g.shape[-2:]), F32) for g in grads]
    pieces = pieces_of(shards, width)
    count, most = len(pieces), max(size.values()) - 1
    orders = [SCATTER_ORDERS[n in third] for n in range(count)]
    rows = grads[0].shape[-2]
    three = AXES[:3]
    whole = (count, *(size[a] for a in three), rows, width)
    late = []
    for n in range(count):
        for h in range(2):
            for s in (1, 2, 3):
                order = orders[n][h]
                free = [size[a] for a in three if a not in order[:s]]
                late.append(pltpu.VMEM((size[order[s - 1]] - 1, *free, rows // 2, width), BF16))
    vmem = pl.BlockSpec(memory_space=pltpu.VMEM)
    return pl.pallas_call(
        partial(scatter_kernel, pieces, width, orders, lag, len(grads)),
        out_shape=[*shards, jax.ShapeDtypeStruct(small.shape, small.dtype)],
        in_specs=[*[pl.BlockSpec(memory_space=pl.ANY)] * len(grads), vmem],
        out_specs=[vmem] * (len(grads) + 1),
        scratch_shapes=[
            pltpu.VMEM(whole, BF16),
            pltpu.VMEM(whole, BF16),
            *late,
            *[pltpu.VMEM((size[a], *small.shape), F32) for a in SUM_AXES],
            pltpu.SemaphoreType.DMA((count, 2, 4, most)),
            pltpu.SemaphoreType.DMA((count, 2, 4, most)),
            pltpu.SemaphoreType.DMA((count,)),
            pltpu.SemaphoreType.DMA((4, most)),
            pltpu.SemaphoreType.DMA((4, most)),
        ],
        compiler_params=pltpu.CompilerParams(
            collective_id=collective_id, has_side_effects=True, vmem_limit_bytes=60 * 2**20
        ),
        name="scatter",
    )(*grads, small)


def body(
    inputs,
    teacher,
    lengths,
    first_gain,
    first_shift,
    query_key_value_weight,
    heads_bias,
    merge_weight,
    merge_bias,
    second_gain,
    second_shift,
    expand_weight,
    expand_bias,
    reduce_weight,
    reduce_bias,
):
    rows, width = inputs.shape
    images = rows // SLOTS
    halves = lax.axis_size("tensor")
    hidden = expand_weight.shape[1] * halves
    place = lax.axis_index("dp") * halves + lax.axis_index("tensor")
    mine = lax.dynamic_slice_in_dim(lengths, place * images, images)
    row_valid = (jnp.arange(SLOTS, dtype=jnp.int32)[None, :] < mine[:, None]).reshape(rows, 1)
    row_valid = row_valid.astype(F32)
    count = jnp.sum(lengths).astype(F32)

    weights = [query_key_value_weight, merge_weight, expand_weight]
    piece_width = query_key_value_weight.shape[-1]
    qkv_full, merge_full, expand_full, heads_bias, expand_bias = gather(
        weights, [heads_bias, expand_bias.reshape(1, -1)], 0, piece_width, (4,), 1
    )
    qkv_full = qkv_full.reshape(3, halves, width, -1)
    merge_full = merge_full.reshape(halves, width, -1)
    expand_full = expand_full.reshape(halves, width, -1)
    heads_bias = jnp.moveaxis(heads_bias, 0, 1).reshape(2, width)
    reduce_full = lax.all_gather(reduce_weight, EVERY, axis=0, tiled=True).reshape(halves, width, -1)

    inputs_f = inputs.astype(F32)
    normed, first_back = jax.vjp(layer_norm, inputs_f, first_gain, first_shift)
    normed = normed.astype(BF16)
    qkv_bias = jnp.stack([heads_bias[0], jnp.zeros_like(heads_bias[0]), heads_bias[1]])
    qkv = jnp.einsum("xz,ejzi->exji", normed, qkv_full, preferred_element_type=F32)
    qkv = (qkv.reshape(3, rows, width) + qkv_bias[:, None, :]).astype(BF16)
    mixed, log_total = attend(mine, qkv)
    branch = jnp.einsum(
        "rjf,jdf->rd", mixed.reshape(rows, halves, -1), merge_full, preferred_element_type=F32
    )
    hidden_state = inputs_f + branch + merge_bias
    second, second_back = jax.vjp(layer_norm, hidden_state, second_gain, second_shift)
    second = second.astype(BF16)
    pre_act = jnp.einsum("rd,jdf->rjf", second, expand_full, preferred_element_type=F32)
    pre_act = pre_act + expand_bias.reshape(halves, -1)
    activ, gelu_back = jax.vjp(partial(jax.nn.gelu, approximate=True), pre_act)
    activ = activ.astype(BF16)
    feed = jnp.einsum("rjf,jdf->rd", activ, reduce_full, preferred_element_type=F32)
    result = (hidden_state + feed + reduce_bias) * row_valid
    error = (result - teacher.astype(F32)) * row_valid
    loss_part = jnp.sum(error * error)
    result_grad = 2.0 * error / count

    result_grad_b = result_grad.astype(BF16)
    reduce_grad = jnp.einsum("rd,rjf->jdf", result_grad_b, activ, preferred_element_type=F32)
    reduce_grad = lax.psum_scatter(
        reduce_grad.astype(BF16).reshape(halves * width, -1), EVERY, scatter_dimension=0, tiled=True
    ).astype(F32)
    activ_grad = jnp.einsum("rd,jdf->rjf", result_grad_b, reduce_full, preferred_element_type=F32)
    pre_grad = gelu_back(activ_grad)[0].astype(BF16)
    expand_bias_grad = jnp.sum(pre_grad, axis=0, dtype=F32).reshape(hidden)
    expand_grad = jnp.einsum("rd,rjf->jdf", second, pre_grad, preferred_element_type=F32).astype(BF16)
    second_grad = jnp.einsum("rjf,jdf->rd", pre_grad, expand_full, preferred_element_type=F32)
    hidden_ln_grad, second_gain_grad, second_shift_grad = second_back(second_grad)
    hidden_grad = result_grad + hidden_ln_grad
    reduce_bias_grad = jnp.sum(result_grad, axis=0)
    merge_bias_grad = jnp.sum(hidden_grad, axis=0)
    hidden_grad_b = hidden_grad.astype(BF16)
    merge_grad = jnp.einsum(
        "rd,rjf->jdf", hidden_grad_b, mixed.reshape(rows, halves, -1), preferred_element_type=F32
    ).astype(BF16)
    mixed_grad = jnp.einsum("rd,jdf->rjf", hidden_grad_b, merge_full, preferred_element_type=F32)
    mixed_grad = mixed_grad.astype(BF16).reshape(rows, width)
    qkv_grad, bias_grad = attend_back(mine, qkv, mixed_grad, log_total)
    heads_bias_grad = jnp.moveaxis(bias_grad, 1, 0).reshape(2, width)
    qkv_grad = qkv_grad.reshape(3, rows, halves, -1)
    heads_grad = jnp.einsum("rb,mrjx->mjbx", normed, qkv_grad, preferred_element_type=F32).astype(BF16)
    normed_grad = jnp.einsum("mejx,mjwx->ew", qkv_grad, qkv_full, preferred_element_type=F32)
    inputs_ln_grad, first_gain_grad, first_shift_grad = first_back(normed_grad)
    inputs_grad = hidden_grad + inputs_ln_grad

    small = jnp.concatenate(
        [
            first_gain_grad,
            first_shift_grad,
            second_gain_grad,
            second_shift_grad,
            merge_bias_grad,
            reduce_bias_grad,
            heads_bias_grad.reshape(-1),
            expand_bias_grad,
            loss_part.reshape(1),
        ]
    )
    length = small.shape[0]
    small = jnp.pad(small, (0, -length % 1024)).reshape(-1, 128)
    size = sizes()
    places = tuple(size[a] for a in AXES)
    heads_grad, merge_grad, expand_grad, small = scatter(
        [
            heads_grad.reshape(3, *places, -1, piece_width),
            merge_grad.reshape(*places, -1, piece_width),
            expand_grad.reshape(*places, -1, hidden // halves),
        ],
        small, 1, piece_width, (), 1,
    )
    small = small.reshape(-1)
    vectors = small[: 6 * width].reshape(6, width)
    tensor = lax.axis_index("tensor")
    heads_bias_sum = lax.dynamic_slice_in_dim(
        small[6 * width : 8 * width].reshape(2, width), tensor * (width // halves), width // halves, 1
    )
    expand_bias_sum = lax.dynamic_slice_in_dim(
        small, 8 * width + tensor * (hidden // halves), hidden // halves
    )
    return (
        small[length - 1] / count,
        result.astype(BF16),
        inputs_grad,
        vectors[0],
        vectors[1],
        heads_grad,
        heads_bias_sum,
        merge_grad,
        vectors[4],
        vectors[2],
        vectors[3],
        expand_grad,
        expand_bias_sum,
        reduce_grad,
        vectors[5],
    )


def solution(mesh):
    return jax.shard_map(
        body,
        mesh=mesh,
        in_specs=(
            P(("dp", "tensor"), None),
            P(("dp", "tensor"), None),
            P(),
            P(),
            P(),
            P(None, "dp", "tensor"),
            P(None, "tensor"),
            P("dp", "tensor"),
            P(),
            P(),
            P(),
            P("dp", "tensor"),
            P("tensor"),
            P("dp", "tensor"),
            P(),
        ),
        out_specs=(
            P(),
            P(("dp", "tensor"), None),
            P(("dp", "tensor"), None),
            P(),
            P(),
            P(None, "dp", "tensor"),
            P(None, "tensor"),
            P("dp", "tensor"),
            P(),
            P(),
            P(),
            P("dp", "tensor"),
            P("tensor"),
            P("dp", "tensor"),
            P(),
        ),
        check_vma=False,
    )
```

```python
from functools import partial
import math

import jax
import jax.numpy as jnp
from jax import lax
from jax.experimental import pallas as pl
from jax.experimental.pallas import tpu as pltpu
from jax.sharding import PartitionSpec as P

HD = 64
SLOTS = 320
PAIR = 2 * HD

EPSILON = 1e-05
MASKED_SCORE = -1e30
F32 = jnp.float32
BF16 = jnp.bfloat16
EVERY = ("tensor", "dp")
CORES = 2
LINE = 4


AXES = ("tensor", "line", "row", "core")
MESH = pl.DeviceIdType.MESH
GATHER_ORDERS = (("line", "tensor", "row", "core"), ("line", "row", "tensor", "core"))


def sizes():
    dp = lax.axis_size("dp")
    return {"tensor": lax.axis_size("tensor"), "line": LINE, "row": dp // (LINE * CORES), "core": CORES}


class Place:
    def __init__(self):
        self.size = sizes()
        index = lax.axis_index("dp")
        self.at = {
            "tensor": lax.axis_index("tensor"),
            "core": lax.rem(index, CORES),
            "row": lax.rem(lax.div(index, CORES), self.size["row"]),
            "line": lax.div(index, CORES * self.size["row"]),
        }

    def steps(self, axis):
        return range(1, self.size[axis])

    def peer(self, axis, step):
        return lax.rem(self.at[axis] + step, self.size[axis])

    def device(self, axis, place):
        at = {**self.at, axis: place}
        return {"dp": (at["line"] * self.size["row"] + at["row"]) * CORES + at["core"], "tensor": at["tensor"]}

    def greet(self):
        barrier = pltpu.get_barrier_semaphore()
        count = 0
        for axis in AXES:
            for step in self.steps(axis):
                pl.semaphore_signal(
                    barrier, inc=1, device_id=self.device(axis, self.peer(axis, step)), device_id_type=MESH
                )
                count += 1
        pl.semaphore_wait(barrier, count)


def pieces_of(shards, width):
    out = []
    for a, shard in enumerate(shards):
        for lead in range(shard.shape[0]) if len(shard.shape) == 3 else (None,):
            for col in range(shard.shape[-1] // width):
                out.append((a, lead, col))
    return out


def piece(refs, which, width):
    a, lead, col = which
    ref = refs[a] if lead is None else refs[a].at[lead]
    spare = (slice(None),) * (len(ref.shape) - 1)
    return ref.at[(*spare, pl.ds(col * width, width))]


def whole_shape(weight):
    size = sizes()
    return (*weight.shape[:-2], *(size[a] for a in AXES), *weight.shape[-2:])


class Gather:
    def __init__(self, pieces, width, offsets, ins, outs, sems):
        self.here = Place()
        self.pieces, self.width, self.offsets, self.ins, self.outs = pieces, width, offsets, ins, outs
        self.send_sem, self.recv_sem, self.own_sem = sems
        self.half = ins[0].shape[-2] // 2
        self.count = len(pieces)

    def region(self, n, h, stage, axis=None, place=None):
        order = GATHER_ORDERS[h]
        index = [
            slice(None) if a in order[:stage] else place if a == axis else self.here.at[a] for a in AXES
        ]
        return piece(self.outs, self.pieces[n], self.width).at[(*index, pl.ds(h * self.half, self.half))]

    def remote(self, n, h, stage, step, coming=False):
        here, axis = self.here, GATHER_ORDERS[h][stage]
        slot = (n, h, stage, step - 1)
        to = source = self.region(n, h, stage)
        if stage == 0:
            source = piece(self.ins, self.pieces[n], self.width).at[pl.ds(h * self.half, self.half)]
        if coming:
            to = self.region(n, h, stage, axis, here.peer(axis, here.size[axis] - step))
        return pltpu.make_async_remote_copy(
            src_ref=source, dst_ref=to, send_sem=self.send_sem.at[slot], recv_sem=self.recv_sem.at[slot],
            device_id=here.device(axis, here.peer(axis, step)), device_id_type=MESH,
        )

    def every(self, n, stage):
        return [(n, h, stage, step) for h in range(2) for step in self.here.steps(GATHER_ORDERS[h][stage])]

    def start(self, n, stage):
        for slot in self.every(n, stage):
            self.remote(*slot).start()

    def arrived(self, n, stage=3):
        for slot in self.every(n, stage):
            self.remote(*slot, coming=True).wait_recv()

    def own(self, n):
        place = tuple(self.here.at[a] for a in AXES)
        return pltpu.make_async_copy(
            piece(self.ins, self.pieces[n], self.width),
            piece(self.outs, self.pieces[n], self.width).at[place], self.own_sem.at[n],
        )

    def begin(self):
        self.here.greet()
        for n in range(self.count):
            self.start(n, 0)
            self.own(n).start()

    def ticks(self):
        return self.count + self.offsets[-1]

    def tick(self, k):
        for stage, offset in enumerate(self.offsets, 1):
            n = k - offset
            if 0 <= n < self.count:
                if stage == 1:
                    self.own(n).wait()
                self.arrived(n, stage - 1)
                self.start(n, stage)

    def end(self):
        for n in range(self.count):
            for stage in range(4):
                for slot in self.every(n, stage):
                    self.remote(*slot).wait_send()


class Share:
    def __init__(self, here, source, target, sems):
        self.here, self.source, self.target = here, source, target
        self.send_sem, self.recv_sem, self.own_sem = sems

    def remote(self, step, coming=False):
        here = self.here
        place = here.peer("tensor", here.size["tensor"] - step) if coming else here.at["tensor"]
        return pltpu.make_async_remote_copy(
            src_ref=self.source, dst_ref=self.target.at[place],
            send_sem=self.send_sem.at[step - 1], recv_sem=self.recv_sem.at[step - 1],
            device_id=here.device("tensor", here.peer("tensor", step)), device_id_type=MESH,
        )

    def own(self):
        return pltpu.make_async_copy(self.source, self.target.at[self.here.at["tensor"]], self.own_sem)

    def begin(self):
        self.own().start()
        for step in self.here.steps("tensor"):
            self.remote(step).start()

    def arrived(self):
        self.own().wait()
        for step in self.here.steps("tensor"):
            self.remote(step, coming=True).wait_recv()

    def end(self):
        for step in self.here.steps("tensor"):
            self.remote(step).wait_send()


SCATTER_ORDERS = (
    (("tensor", "row", "line"), ("row", "tensor", "line")),
    (("line", "tensor", "row"), ("line", "row", "tensor")),
)
SUM_AXES = ("core", "tensor", "row", "line")


def scatter_kernel(pieces, width, orders, lag, n_grads, *refs):
    ins, small = refs[:n_grads], refs[n_grads]
    outs, small_out = refs[n_grads + 1 : 2 * n_grads + 1], refs[2 * n_grads + 1]
    own_buf, first_buf, *rest = refs[2 * n_grads + 2 :]
    count = len(pieces)
    late = {(n, h, s): rest[(n * 2 + h) * 3 + s - 1] for n in range(count) for h in range(2) for s in (1, 2, 3)}
    small_bufs = rest[6 * count : 6 * count + 4]
    send_sem, recv_sem, own_sem, small_send, small_recv = rest[6 * count + 4 :]
    here = Place()
    here.greet()
    half = own_buf.shape[-2] // 2
    three = AXES[:3]

    def own(n):
        source = piece(ins, pieces[n], width).at[:, :, :, here.at["core"]]
        return pltpu.make_async_copy(source, own_buf.at[n], own_sem.at[n])

    def to_core(n):
        other = here.peer("core", 1)
        return pltpu.make_async_remote_copy(
            src_ref=piece(ins, pieces[n], width).at[:, :, :, other], dst_ref=first_buf.at[n],
            send_sem=send_sem.at[n, 0, 0, 0], recv_sem=recv_sem.at[n, 0, 0, 0],
            device_id=here.device("core", other), device_id_type=MESH,
        )

    def remote(n, h, stage, step):
        order = orders[n][h]
        axis = order[stage - 1]
        to = here.peer(axis, step)
        index = [
            here.at[a] if a in order[: stage - 1] else to if a == axis else slice(None) for a in three
        ]
        slot = (n, h, stage, step - 1)
        return pltpu.make_async_remote_copy(
            src_ref=own_buf.at[(n, *index, pl.ds(h * half, half))],
            dst_ref=late[n, h, stage].at[step - 1],
            send_sem=send_sem.at[slot], recv_sem=recv_sem.at[slot],
            device_id=here.device(axis, to), device_id_type=MESH,
        )

    def every(n, stage, act):
        for h in range(2):
            for step in here.steps(orders[n][h][stage - 1]):
                act(remote(n, h, stage, step))

    def add_core(n):
        def one(i, _):
            first, left = lax.div(i, here.size["row"]), lax.rem(i, here.size["row"])
            at = (n, lax.div(first, LINE), lax.rem(first, LINE), left)
            own_buf[at] = (own_buf[at].astype(F32) + first_buf[at].astype(F32)).astype(BF16)
            return 0

        lax.fori_loop(0, math.prod(here.size[a] for a in three), one, 0)

    def add(n, h, stage):
        order = orders[n][h]
        buf, steps = late[n, h, stage], here.size[order[stage - 1]] - 1
        free = [a for a in three if a not in order[:stage]]
        rows = pl.ds(h * half, half)

        def one(i, _):
            at, left = dict(here.at), i
            for a in reversed(free):
                at[a] = lax.rem(left, here.size[a])
                left = lax.div(left, here.size[a])
            mine = (n, *(at[a] for a in three), rows)
            total = own_buf[mine].astype(F32)
            for s in range(steps):
                total += buf[(s, *(at[a] for a in free))].astype(F32)
            if stage == 3:
                out = piece(outs, pieces[n], width)
                out[rows, :] = total
            else:
                own_buf[mine] = total.astype(BF16)
            return 0

        if free:
            lax.fori_loop(0, math.prod(here.size[a] for a in free), one, 0)
        else:
            one(0, 0)

    def small_copy(stage, step, coming=False):
        axis = SUM_AXES[stage]
        place = here.peer(axis, here.size[axis] - step) if coming else here.at[axis]
        buf = small_bufs[stage]
        return pltpu.make_async_remote_copy(
            src_ref=buf.at[here.at[axis]], dst_ref=buf.at[place],
            send_sem=small_send.at[stage, step - 1], recv_sem=small_recv.at[stage, step - 1],
            device_id=here.device(axis, here.peer(axis, step)), device_id_type=MESH,
        )

    def small_start(stage, value):
        axis = SUM_AXES[stage]
        small_bufs[stage][here.at[axis]] = value
        for step in here.steps(axis):
            small_copy(stage, step).start()

    def small_end(stage):
        axis = SUM_AXES[stage]
        for step in here.steps(axis):
            small_copy(stage, step, coming=True).wait_recv()
            small_copy(stage, step).wait_send()
        total = small_bufs[stage][0]
        for place in range(1, here.size[axis]):
            total += small_bufs[stage][place]
        return total

    for n in range(count):
        to_core(n).start()
        own(n).start()
    small_start(0, small[...])
    for tick in range(max(count + 3 * lag, 5)):
        if 1 <= tick <= 4:
            total = small_end(tick - 1)
            if tick < 4:
                small_start(tick, total)
            else:
                small_out[...] = total
        for stage in range(4):
            n = tick - lag * stage
            if not 0 <= n < count:
                continue
            if stage == 0:
                own(n).wait()
                to_core(n).wait_recv()
                add_core(n)
            else:
                every(n, stage, lambda copy: copy.wait_recv())
                for h in range(2):
                    add(n, h, stage)
            if stage < 3:
                every(n, stage + 1, lambda copy: copy.start())
    for n in range(count):
        to_core(n).wait_send()
        for stage in (1, 2, 3):
            every(n, stage, lambda copy: copy.wait_send())


def scatter(grads, small, collective_id, width, third=(), lag=2):
    size = sizes()
    shards = [jax.ShapeDtypeStruct((*g.shape[:-6], *g.shape[-2:]), F32) for g in grads]
    pieces = pieces_of(shards, width)
    count, most = len(pieces), max(size.values()) - 1
    orders = [SCATTER_ORDERS[n in third] for n in range(count)]
    rows = grads[0].shape[-2]
    three = AXES[:3]
    whole = (count, *(size[a] for a in three), rows, width)
    late = []
    for n in range(count):
        for h in range(2):
            for s in (1, 2, 3):
                order = orders[n][h]
                free = [size[a] for a in three if a not in order[:s]]
                late.append(pltpu.VMEM((size[order[s - 1]] - 1, *free, rows // 2, width), BF16))
    vmem = pl.BlockSpec(memory_space=pltpu.VMEM)
    return pl.pallas_call(
        partial(scatter_kernel, pieces, width, orders, lag, len(grads)),
        out_shape=[*shards, jax.ShapeDtypeStruct(small.shape, small.dtype)],
        in_specs=[*[pl.BlockSpec(memory_space=pl.ANY)] * len(grads), vmem],
        out_specs=[vmem] * (len(grads) + 1),
        scratch_shapes=[
            pltpu.VMEM(whole, BF16),
            pltpu.VMEM(whole, BF16),
            *late,
            *[pltpu.VMEM((size[a], *small.shape), F32) for a in SUM_AXES],
            pltpu.SemaphoreType.DMA((count, 2, 4, most)),
            pltpu.SemaphoreType.DMA((count, 2, 4, most)),
            pltpu.SemaphoreType.DMA((count,)),
            pltpu.SemaphoreType.DMA((4, most)),
            pltpu.SemaphoreType.DMA((4, most)),
        ],
        compiler_params=pltpu.CompilerParams(
            collective_id=collective_id, has_side_effects=True, vmem_limit_bytes=60 * 2**20
        ),
        name="scatter",
    )(*grads, small)


def dot(left, right, left_dim=1, right_dim=0):
    return lax.dot_general(
        left, right, (((left_dim,), (right_dim,)), ((), ())), preferred_element_type=F32
    )


def side_by_side(ref, *lead):
    return jnp.concatenate([ref[(*lead, t)] for t in range(ref.shape[-3])], axis=-1)


def centred(rows):
    off = rows - jnp.mean(rows, axis=-1, keepdims=True)
    inverse = lax.rsqrt(jnp.mean(off * off, axis=-1, keepdims=True) + EPSILON)
    return off * inverse, inverse


def norm_back(grad, hat, inverse, gain):
    scaled = grad * gain
    along = jnp.mean(scaled * hat, axis=-1, keepdims=True)
    return inverse * (scaled - jnp.mean(scaled, axis=-1, keepdims=True) - hat * along)


def fold(rows):
    return jnp.sum(rows.reshape(-1, 8, rows.shape[-1]), axis=0)


def row_blocks(rows, size, one):
    def step(i, _):
        one(i, pl.ds(pl.multiple_of(i * size, size), size))
        return 0

    lax.fori_loop(0, rows // size, step, 0)


def transpose_into(source, target):
    rows = source.shape[0]
    for first in range(0, rows, 128):
        size = min(128, rows - first)
        target[:, first : first + size] = source[first : first + size, :].astype(F32).T.astype(BF16)


def two_heads(pair):
    first = lax.broadcasted_iota(jnp.int32, pair.shape, 1) < HD
    zero = jnp.zeros_like(pair)
    return jnp.concatenate([jnp.where(first, pair, zero), jnp.where(first, zero, pair)], axis=0)


def one_pair(stacked):
    first = lax.broadcasted_iota(jnp.int32, (SLOTS, PAIR), 1) < HD
    return jnp.where(first, stacked[:SLOTS], stacked[SLOTS:])


def masked_scores(query_stack, keys, length):
    scores = dot(keys, query_stack, 1, 1)
    slot = lax.broadcasted_iota(jnp.int32, scores.shape, 0)
    return jnp.where(slot < length, scores, MASKED_SCORE)


def group_weight(qkv_held, columns):
    parts = [qkv_held[e, t, ..., columns] for t in range(qkv_held.shape[1]) for e in range(3)]
    return jnp.concatenate([part.reshape(-1, PAIR) for part in parts], axis=-1)


def merge_tile(merge_held, columns):
    parts = [merge_held[t, ..., columns] for t in range(merge_held.shape[0])]
    return jnp.concatenate([part.reshape(-1, PAIR) for part in parts], axis=-1)


def schedule(ticks, last_piece, needed, steps):
    at = []
    first = needed.index(next(s for s in needed if s > 0), 0) if any(needed) else len(needed)
    early = first + last_piece
    for k in range(ticks):
        piece_done = k - last_piece
        even = 0 if k < early else 1 + (k - early) * (steps - 1) // (ticks - early)
        at.append(min(even, needed[max(piece_done, 0)]))
    for k in range(ticks - 2, -1, -1):
        at[k] = min(at[k], at[k + 1])
    return at


def forward_kernel(
    width_of_piece, offsets, feed_columns,
    lengths, x_ref, gain, shift, merge_bias, gain_2, shift_2, heads_bias, expand_bias,
    qkv_part, merge_part, expand_part, reduce_part,
    a_turned, qkv_ref, mixed_ref, log_ref, hidden_ref, second_ref, second_turned, activ, slope,
    qkv_full, merge_full, expand_full, reduce_full,
    a_ref, qkv_held, merge_held, tiles, heads_bias_all, expand_bias_all,
    send_sem, recv_sem, own_sem, share_send, share_recv, share_own, held_sem, tile_sem,
):
    now = pl.program_id(0)
    rows = x_ref.shape[0]
    images = rows // SLOTS
    halves = qkv_held.shape[1]
    groups = width_of_piece // PAIR
    attention_steps = groups * images
    feed_steps = expand_part.shape[1] // feed_columns
    steps = attention_steps + feed_steps
    parts = [qkv_part, merge_part, expand_part, reduce_part]
    pieces = pieces_of(parts, width_of_piece)
    gather = Gather(
        pieces, width_of_piece, offsets, parts, [qkv_full, merge_full, expand_full, reduce_full],
        (send_sem, recv_sem, own_sem),
    )
    shares = [
        Share(gather.here, source, target, (share_send.at[n], share_recv.at[n], share_own.at[n]))
        for n, (source, target) in enumerate([(heads_bias, heads_bias_all), (expand_bias, expand_bias_all)])
    ]
    tiles_of_piece = width_of_piece // feed_columns
    needed = [
        0 if a == 0 else images - 1 if a == 1
        else max(attention_steps + col * tiles_of_piece - 1, 0) if a == 2 else steps - 1
        for a, _, col in pieces
    ]
    when = schedule(gather.ticks(), offsets[-1], needed, steps)
    image = lax.rem(now, images)
    group = lax.min(lax.div(now, images), groups - 1)
    columns = pl.ds(pl.multiple_of(group * PAIR, PAIR), PAIR)

    def hold(n):
        a, lead, _ = pieces[n]
        source, target = (qkv_full.at[lead], qkv_held.at[lead]) if a == 0 else (merge_full, merge_held)
        return pltpu.make_async_copy(source, target, held_sem.at[n])

    def tile_copy(j):
        block = pl.ds(j * feed_columns, feed_columns)
        return pltpu.make_async_copy(
            expand_full.at[:, :, :, :, :, block], tiles.at[j % 2], tile_sem.at[j % 2]
        )

    def fetch_tile(j):
        if j % tiles_of_piece == 0:
            gather.arrived(4 + j // tiles_of_piece)
        tile_copy(j).start()

    @pl.when(now == 0)
    def _():
        gather.begin()
        for share in shares:
            share.begin()
        early = [k for k in range(gather.ticks()) if when[k] == 0]
        blocks = rows // 32
        per = -(-blocks // max(len(early), 1))

        def norm(i, _):
            at = pl.ds(pl.multiple_of(i * 32, 32), 32)
            x = x_ref[at, :].astype(F32)
            hidden_ref[at, :] = x + merge_bias[...]
            a_ref[at, :] = (centred(x)[0] * gain[...] + shift[...]).astype(BF16)
            return 0

        done = 0
        for k in early:
            lax.fori_loop(done, min(done + per, blocks), norm, 0)
            done = min(done + per, blocks)
            gather.tick(k)
            n = k - offsets[-1] - 1
            if 0 <= n < 3:
                gather.arrived(n)
                hold(n).start()
        lax.fori_loop(done, blocks, norm, 0)
        transpose_into(a_ref, a_turned)
        for n in range(max(len(early) - offsets[-1] - 1, 0), 3):
            gather.arrived(n)
            hold(n).start()
        for share in shares:
            share.arrived()
        for n in range(3):
            hold(n).wait()

    for k in range(gather.ticks()):
        if when[k] > 0:
            pl.when(now == when[k])(partial(gather.tick, k))

    @pl.when((now < attention_steps) & (image == 0))
    def _():
        weight = group_weight(qkv_held, columns)
        bias = []
        for t in range(halves):
            query = heads_bias_all[t, 0:1, columns]
            bias += [query, jnp.zeros_like(query), heads_bias_all[t, 1:2, columns]]
        bias = jnp.concatenate(bias, axis=-1)
        for i in range(images):
            at = slice(i * SLOTS, (i + 1) * SLOTS)
            out = (dot(a_ref[at, :], weight) + bias).astype(BF16)
            for t in range(halves):
                query = slice(t * 3 * PAIR, (t * 3 + 1) * PAIR)
                qkv_ref[0, at, query] = out[:, query] * 0.125
                rest = slice((t * 3 + 1) * PAIR, (t * 3 + 3) * PAIR)
                qkv_ref[0, at, rest] = out[:, rest]

    @pl.when(now < attention_steps)
    def _():
        length = lengths[image]
        at = pl.ds(pl.multiple_of(image * SLOTS, SLOTS), SLOTS)
        for t in range(halves):
            first = t * 3 * PAIR
            query_stack = two_heads(qkv_ref[0, at, first : first + PAIR])
            scores = masked_scores(query_stack, qkv_ref[0, at, first + PAIR : first + 2 * PAIR], length)
            highest = jnp.max(scores, axis=0, keepdims=True)
            expo = jnp.exp(scores - highest)
            totals = jnp.sum(expo, axis=0, keepdims=True)
            values = qkv_ref[0, at, first + 2 * PAIR : first + 3 * PAIR]
            mixed = dot(values, expo.astype(BF16), 0, 0) * (1.0 / totals)
            mixed_ref[0, at, t * PAIR : (t + 1) * PAIR] = one_pair(mixed.T).astype(BF16)
            log_ref[0, 0, t : t + 1] = highest + jnp.log(totals)

    @pl.when(now == images - 1)
    def _():
        gather.arrived(3)
        hold(3).start()
        hold(3).wait()

    @pl.when((now < attention_steps) & (image == images - 1))
    def _():
        weight = merge_tile(merge_held, columns)
        for i in range(images):
            part = slice(i * SLOTS, (i + 1) * SLOTS)
            hidden_ref[part, :] += dot(mixed_ref[0, part, :], weight, 1, 1)

    @pl.when(now == attention_steps - 1)
    def _():
        fetch_tile(0)

        def norm(_, at):
            hat, _ = centred(hidden_ref[at, :])
            second_ref[at, :] = (hat * gain_2[...] + shift_2[...]).astype(BF16)

        row_blocks(rows, 32, norm)
        transpose_into(second_ref, second_turned)

    for j in range(feed_steps):

        @pl.when(now == attention_steps + j)
        def _(j=j):
            tile_copy(j).wait()
            if j + 1 < feed_steps:
                fetch_tile(j + 1)

    @pl.when(now >= attention_steps)
    def _():
        j = now - attention_steps
        block = pl.ds(pl.multiple_of(j * feed_columns, feed_columns), feed_columns)
        slot = lax.rem(j, 2)
        weight = jnp.concatenate(
            [tiles[slot, t].reshape(-1, feed_columns) for t in range(halves)], axis=-1
        )
        bias = jnp.concatenate([expand_bias_all[t, :, block] for t in range(halves)], axis=-1)
        for i in range(images):
            at = slice(i * SLOTS, (i + 1) * SLOTS)
            z = dot(second_ref[at, :], weight) + bias
            square = z * z
            bend = jnp.tanh(0.7978845608 * z * (1.0 + 0.044715 * square))
            half = 0.5 + 0.5 * bend
            activ[0, at, :] = (z * half).astype(BF16)
            inner = 0.7978845608 * z * (1.0 + (3 * 0.044715) * square)
            slope[0, at, :] = (half + 0.5 * inner * (1.0 - bend * bend)).astype(BF16)

    @pl.when(now == steps - 1)
    def _():
        for n in range(8, gather.count):
            gather.arrived(n)
        gather.end()
        for share in shares:
            share.end()


def feed_kernel(
    lengths, count, activ, hidden, reduce, reduce_bias, teacher,
    out, grad, grad_b, grad_turned, bias_grad, loss, total,
):
    step = pl.program_id(0)
    rows = hidden.shape[0]
    reduce_tile = side_by_side(reduce)

    @pl.when(step == 0)
    def _():
        total[...] = jnp.zeros_like(total)

    for i in range(rows // SLOTS):
        at = slice(i * SLOTS, (i + 1) * SLOTS)
        total[at, :] += dot(activ[0, at, :], reduce_tile, 1, 1)

    @pl.when(step == pl.num_programs(0) - 1)
    def _():
        bias_grad[...] = jnp.zeros_like(bias_grad)
        loss[...] = jnp.zeros_like(loss)

        def end(i, at):
            image, block = lax.div(i, SLOTS // 32), lax.rem(i, SLOTS // 32)
            slot = block * 32 + lax.broadcasted_iota(jnp.int32, (32, 1), 0)
            valid = slot < lengths[image]
            result = jnp.where(valid, hidden[at, :] + total[at, :] + reduce_bias[...], 0.0)
            out[at, :] = result.astype(BF16)
            error = jnp.where(valid, result - teacher[at, :].astype(F32), 0.0)
            loss[...] += fold(error * error)
            back = 2.0 * error / count[0]
            bias_grad[...] += fold(back)
            grad[at, :] = back
            grad_b[at, :] = back.astype(BF16)

        row_blocks(rows, 32, end)
        transpose_into(grad_b, grad_turned)


def feed_back_kernel(
    result_b, result_turned, second_turned, expand, reduce, activ, slope, hidden, result_grad, gain,
    reduce_grad, expand_grad, expand_bias_grad, hidden_grad, hidden_b, hidden_turned, sums, total,
):
    step = pl.program_id(0)
    rows = result_b.shape[0]
    halves, width, columns = expand.shape
    expand_tile, reduce_tile = side_by_side(expand), side_by_side(reduce)

    @pl.when(step == 0)
    def _():
        total[...] = jnp.zeros_like(total)

    reduce_part = dot(result_turned[...], activ[0])
    for t in range(halves):
        reduce_grad[t] = reduce_part[:, t * columns : (t + 1) * columns].astype(BF16)
    bias = jnp.zeros((8, halves * columns), F32)
    parts = []
    for i in range(rows // SLOTS):
        at = slice(i * SLOTS, (i + 1) * SLOTS)
        z_grad = (dot(result_b[at, :], reduce_tile) * slope[0, at, :].astype(F32)).astype(BF16)
        bias += fold(z_grad.astype(F32))
        parts.append(z_grad)
        total[at, :] += dot(z_grad, expand_tile, 1, 1)
    expand_bias_grad[0] = jnp.sum(bias, axis=0, keepdims=True)
    expand_part = dot(second_turned[...], jnp.concatenate(parts, axis=0))
    for t in range(halves):
        expand_grad[t] = expand_part[:, t * columns : (t + 1) * columns].astype(BF16)

    @pl.when(step == pl.num_programs(0) - 1)
    def _():
        sums[...] = jnp.zeros_like(sums)

        def end(_, at):
            hat, inverse = centred(hidden[at, :])
            second_grad = total[at, :]
            back = result_grad[at, :] + norm_back(second_grad, hat, inverse, gain[...])
            sums[0] += fold(second_grad * hat)
            sums[1] += fold(second_grad)
            sums[2] += fold(back)
            hidden_grad[at, :] = back
            hidden_b[at, :] = back.astype(BF16)

        row_blocks(rows, 32, end)
        transpose_into(hidden_b, hidden_turned)


def attend_back_kernel(
    lengths, a_turned, hidden_b, hidden_turned, qkv_ref, mixed_ref, log_ref, x_ref, hidden_grad, gain,
    qkv_weight, merge_weight,
    merge_grad, qkv_grad, bias_grad, inputs_grad, sums,
    mixed_grad, heads_grad, total, qkv_held, merge_held, sem,
):
    group, image = pl.program_id(0), pl.program_id(1)
    rows = x_ref.shape[0]
    halves = qkv_held.shape[1]
    columns = pl.ds(pl.multiple_of(group * PAIR, PAIR), PAIR)

    @pl.when((group == 0) & (image == 0))
    def _():
        copies = [
            pltpu.make_async_copy(merge_weight, merge_held, sem.at[1]),
            pltpu.make_async_copy(qkv_weight, qkv_held, sem.at[0]),
        ]
        for copy in copies:
            copy.start()
        total[...] = jnp.zeros_like(total)
        for copy in copies:
            copy.wait()

    @pl.when(image == 0)
    def _():
        weight = merge_tile(merge_held, columns)
        for i in range(rows // SLOTS):
            part = slice(i * SLOTS, (i + 1) * SLOTS)
            mixed_grad[part, :] = dot(hidden_b[part, :], weight).astype(BF16)
        part = dot(hidden_turned[...], mixed_ref[0]).astype(BF16)
        for t in range(halves):
            merge_grad[t] = part[:, t * PAIR : (t + 1) * PAIR]

    length = lengths[image]
    at = pl.ds(pl.multiple_of(image * SLOTS, SLOTS), SLOTS)
    for t in range(halves):
        first = t * 3 * PAIR
        query_stack = two_heads(qkv_ref[0, at, first : first + PAIR])
        keys = qkv_ref[0, at, first + PAIR : first + 2 * PAIR]
        values = qkv_ref[0, at, first + 2 * PAIR : first + 3 * PAIR]
        scores = masked_scores(query_stack, keys, length)
        attend = jnp.exp(scores - log_ref[0, 0, t : t + 1])
        grad_stack = two_heads(mixed_grad[at, t * PAIR : (t + 1) * PAIR])
        attend_grad = dot(values, grad_stack, 1, 1)
        value_grad = dot(attend.astype(BF16), grad_stack).astype(BF16)
        centre = jnp.sum(attend * attend_grad, axis=0, keepdims=True)
        score_grad = (attend * (attend_grad - centre)).astype(BF16)
        key_grad = dot(score_grad, query_stack).astype(BF16)
        query_grad = dot(keys, score_grad, 0, 0)
        query_grad = (one_pair(query_grad.T) * 0.125).astype(BF16)
        heads_grad[at, first : first + PAIR] = query_grad
        heads_grad[at, first + PAIR : first + 2 * PAIR] = key_grad
        heads_grad[at, first + 2 * PAIR : first + 3 * PAIR] = value_grad

    @pl.when(image == pl.num_programs(1) - 1)
    def _():
        weight = group_weight(qkv_held, columns)
        bias = jnp.zeros((8, halves * 3 * PAIR), F32)
        for i in range(rows // SLOTS):
            part = slice(i * SLOTS, (i + 1) * SLOTS)
            total[part, :] += dot(heads_grad[part, :], weight, 1, 1)
            bias += fold(heads_grad[part, :].astype(F32))
        bias_grad[0] = jnp.sum(bias, axis=0, keepdims=True)
        part = dot(a_turned[...], heads_grad[...]).astype(BF16)
        for t in range(halves):
            for e in range(3):
                first = (t * 3 + e) * PAIR
                qkv_grad[e, t] = part[:, first : first + PAIR]

    @pl.when((image == pl.num_programs(1) - 1) & (group == pl.num_programs(0) - 1))
    def _():
        sums[...] = jnp.zeros_like(sums)

        def end(_, at):
            hat, inverse = centred(x_ref[at, :].astype(F32))
            grad = total[at, :]
            sums[0] += fold(grad * hat)
            sums[1] += fold(grad)
            inputs_grad[at, :] = hidden_grad[at, :] + norm_back(grad, hat, inverse, gain[...])

        row_blocks(rows, 32, end)


def shape(dims, kind=BF16):
    return jax.ShapeDtypeStruct(dims, kind)


def once(dims):
    return pl.BlockSpec(dims, lambda *_: (0,) * len(dims), pipeline_mode=pl.Buffered(1))


ELSEWHERE = pl.BlockSpec(memory_space=pl.ANY)
SCALARS = pl.BlockSpec(memory_space=pltpu.SMEM)
LIMIT = 63 * 2**20


OFFSETS = (0, 1, 2)


def feed_width(halves):
    return max(PAIR, 512 // halves)


def forward(lengths, x, gain, shift, merge_bias, gain_2, shift_2, heads_bias, expand_bias, parts):
    rows, width = x.shape
    halves, columns = lax.axis_size("tensor"), parts[0].shape[2]
    groups, images = columns // PAIR, rows // SLOTS
    attention_steps = groups * images
    feed_columns = feed_width(halves)
    feed_steps = parts[2].shape[1] // feed_columns
    pieces = len(pieces_of(parts, columns))
    most = max(sizes().values()) - 1
    line = once((1, width))
    group_at = lambda s: lax.min(lax.div(s, images), groups - 1)
    feed_at = lambda s: lax.max(s - attention_steps, 0)
    wholes = [whole_shape(part) for part in parts]
    saved = pl.BlockSpec((1, rows, halves * feed_columns), lambda s: (feed_at(s), 0, 0))
    return pl.pallas_call(
        partial(forward_kernel, columns, OFFSETS, feed_columns),
        grid=(attention_steps + feed_steps,),
        in_specs=[SCALARS, once((rows, width)), *[line] * 5, *[ELSEWHERE] * 6],
        out_specs=[
            once((width, rows)),
            pl.BlockSpec((1, rows, halves * 3 * PAIR), lambda s: (group_at(s), 0, 0)),
            pl.BlockSpec((1, rows, halves * PAIR), lambda s: (group_at(s), 0, 0)),
            pl.BlockSpec(
                (1, 1, halves, 2 * SLOTS),
                lambda s: (group_at(s), jnp.where(s < attention_steps, lax.rem(s, images), images - 1), 0, 0),
            ),
            once((rows, width)), once((rows, width)), once((width, rows)), saved, saved,
            *[ELSEWHERE] * 4,
        ],
        out_shape=[
            shape((width, rows)),
            shape((groups, rows, halves * 3 * PAIR)),
            shape((groups, rows, halves * PAIR)),
            shape((groups, images, halves, 2 * SLOTS), F32),
            shape((rows, width), F32), shape((rows, width)), shape((width, rows)),
            *[shape((feed_steps, rows, halves * feed_columns))] * 2,
            *[shape(dims) for dims in wholes],
        ],
        scratch_shapes=[
            pltpu.VMEM((rows, width), BF16),
            pltpu.VMEM(wholes[0], BF16),
            pltpu.VMEM(wholes[1], BF16),
            pltpu.VMEM((2, *wholes[2][:-1], feed_columns), BF16),
            pltpu.VMEM((halves, *heads_bias.shape), F32),
            pltpu.VMEM((halves, *expand_bias.shape), F32),
            pltpu.SemaphoreType.DMA((pieces, 2, 4, most)),
            pltpu.SemaphoreType.DMA((pieces, 2, 4, most)),
            pltpu.SemaphoreType.DMA((pieces,)),
            pltpu.SemaphoreType.DMA((2, halves)),
            pltpu.SemaphoreType.DMA((2, halves)),
            pltpu.SemaphoreType.DMA((2,)),
            pltpu.SemaphoreType.DMA((4,)),
            pltpu.SemaphoreType.DMA((2,)),
        ],
        compiler_params=pltpu.CompilerParams(
            vmem_limit_bytes=LIMIT, collective_id=0, has_side_effects=True
        ),
        name="forward",
    )(lengths, x, gain, shift, merge_bias, gain_2, shift_2, heads_bias, expand_bias, *parts)


def feed(lengths, count, activ, hidden, reduce, reduce_bias, teacher):
    rows, width = hidden.shape
    halves, _, wide = reduce.shape
    steps, columns = activ.shape[0], activ.shape[2] // halves
    whole = once((rows, width))
    return pl.pallas_call(
        feed_kernel,
        grid=(steps,),
        in_specs=[
            SCALARS, SCALARS, pl.BlockSpec((1, rows, halves * columns), lambda j: (j, 0, 0)), whole,
            pl.BlockSpec((halves, width, columns), lambda j: (0, 0, j)), once((1, width)), whole,
        ],
        out_specs=[whole, whole, whole, once((width, rows)), once((8, width)), once((8, width))],
        out_shape=[
            shape((rows, width)), shape((rows, width), F32), shape((rows, width)), shape((width, rows)),
            shape((8, width), F32), shape((8, width), F32),
        ],
        scratch_shapes=[pltpu.VMEM((rows, width), F32)],
        compiler_params=pltpu.CompilerParams(vmem_limit_bytes=LIMIT),
        cost_estimate=pl.CostEstimate(
            flops=2 * rows * width * halves * wide,
            bytes_accessed=2 * rows * halves * wide + 2 * width * halves * wide + 20 * rows * width,
            transcendentals=0,
        ),
        name="feed",
    )(lengths, count, activ, hidden, reduce, reduce_bias, teacher)


def feed_back(result_b, result_turned, second_turned, expand, reduce, activ, slope, hidden, result_grad, gain):
    rows, width = result_b.shape
    halves, _, wide = expand.shape
    steps, columns = activ.shape[0], activ.shape[2] // halves
    tile = pl.BlockSpec((halves, width, columns), lambda j: (0, 0, j))
    saved = pl.BlockSpec((1, rows, halves * columns), lambda j: (j, 0, 0))
    whole, turned = once((rows, width)), once((width, rows))
    return pl.pallas_call(
        feed_back_kernel,
        grid=(steps,),
        in_specs=[whole, turned, turned, tile, tile, saved, saved, whole, whole, once((1, width))],
        out_specs=[
            tile, tile, pl.BlockSpec((1, 1, halves * columns), lambda j: (j, 0, 0)),
            whole, whole, turned, once((3, 8, width)),
        ],
        out_shape=[
            shape(expand.shape), shape(expand.shape), shape((steps, 1, halves * columns), F32),
            shape((rows, width), F32), shape((rows, width)), shape((width, rows)), shape((3, 8, width), F32),
        ],
        scratch_shapes=[pltpu.VMEM((rows, width), F32)],
        compiler_params=pltpu.CompilerParams(vmem_limit_bytes=LIMIT),
        cost_estimate=pl.CostEstimate(
            flops=8 * rows * width * halves * wide,
            bytes_accessed=4 * rows * halves * wide + 8 * width * halves * wide, transcendentals=0,
        ),
        name="feed_back",
    )(result_b, result_turned, second_turned, expand, reduce, activ, slope, hidden, result_grad, gain)


def attend_back(
    lengths, a_turned, hidden_b, hidden_turned, qkv, mixed, log_total, x, hidden_grad, gain,
    qkv_weight, merge_weight,
):
    rows, width = x.shape
    halves, columns = qkv_weight.shape[1], qkv_weight.shape[3]
    groups, images = columns // PAIR, rows // SLOTS
    whole, turned = once((rows, width)), once((width, rows))
    return pl.pallas_call(
        attend_back_kernel,
        grid=(groups, images),
        in_specs=[
            SCALARS, turned, whole, turned,
            pl.BlockSpec((1, rows, halves * 3 * PAIR), lambda c, i: (c, 0, 0)),
            pl.BlockSpec((1, rows, halves * PAIR), lambda c, i: (c, 0, 0)),
            pl.BlockSpec((1, 1, halves, 2 * SLOTS), lambda c, i: (c, i, 0, 0)),
            whole, whole, once((1, width)), ELSEWHERE, ELSEWHERE,
        ],
        out_specs=[
            pl.BlockSpec((halves, width, PAIR), lambda c, i: (0, 0, c)),
            pl.BlockSpec((3, halves, width, PAIR), lambda c, i: (0, 0, 0, c)),
            pl.BlockSpec((1, 1, halves * 3 * PAIR), lambda c, i: (c, 0, 0)),
            whole, once((2, 8, width)),
        ],
        out_shape=[
            shape(merge_weight.shape), shape(qkv_weight.shape),
            shape((groups, 1, halves * 3 * PAIR), F32), shape((rows, width), F32), shape((2, 8, width), F32),
        ],
        scratch_shapes=[
            pltpu.VMEM((rows, halves * PAIR), BF16),
            pltpu.VMEM((rows, halves * 3 * PAIR), BF16),
            pltpu.VMEM((rows, width), F32),
            pltpu.VMEM(qkv_weight.shape, BF16),
            pltpu.VMEM(merge_weight.shape, BF16),
            pltpu.SemaphoreType.DMA((2,)),
        ],
        compiler_params=pltpu.CompilerParams(vmem_limit_bytes=LIMIT),
        cost_estimate=pl.CostEstimate(
            flops=16 * rows * width * width + 40 * rows * SLOTS * width,
            bytes_accessed=40 * rows * width, transcendentals=rows * SLOTS * width // HD,
        ),
        name="attend_back",
    )(lengths, a_turned, hidden_b, hidden_turned, qkv, mixed, log_total, x, hidden_grad, gain,
      qkv_weight, merge_weight)


def body(
    inputs,
    teacher,
    lengths,
    first_gain,
    first_shift,
    query_key_value_weight,
    heads_bias,
    merge_weight,
    merge_bias,
    second_gain,
    second_shift,
    expand_weight,
    expand_bias,
    reduce_weight,
    reduce_bias,
):
    rows, width = inputs.shape
    images = rows // SLOTS
    halves = lax.axis_size("tensor")
    tensor = lax.axis_index("tensor")
    hidden = expand_weight.shape[1] * halves
    piece_width = query_key_value_weight.shape[-1]
    groups = piece_width // PAIR
    place = lax.axis_index("dp") * halves + tensor
    mine = lax.dynamic_slice_in_dim(lengths, place * images, images)
    count = jnp.sum(lengths).astype(F32)
    line = lambda vector: vector.reshape(1, width)

    a_turned, qkv, mixed, log_total, hidden_state, _, second_turned, activ, slope, *wholes = forward(
        mine, inputs, line(first_gain), line(first_shift), line(merge_bias), line(second_gain),
        line(second_shift), heads_bias, expand_bias.reshape(1, -1),
        [query_key_value_weight, merge_weight, expand_weight, reduce_weight],
    )
    qkv_full = wholes[0].reshape(3, halves, width, -1)
    merge_full, expand_full, reduce_full = (whole.reshape(halves, width, -1) for whole in wholes[1:])
    columns = feed_width(halves)
    steps = hidden // halves // columns
    outputs, result_grad, result_b, result_turned, reduce_bias_grad, loss = feed(
        mine, count.reshape(1), activ, hidden_state, reduce_full, line(reduce_bias), teacher
    )
    reduce_grad, expand_grad, expand_bias_grad, hidden_grad, hidden_b, hidden_turned, second_sums = feed_back(
        result_b, result_turned, second_turned, expand_full, reduce_full, activ, slope, hidden_state,
        result_grad, line(second_gain),
    )
    reduce_grad = lax.psum_scatter(
        reduce_grad.reshape(halves * width, -1), EVERY, scatter_dimension=0, tiled=True
    ).astype(F32)
    merge_grad, heads_grad, bias_grad, inputs_grad, first_sums = attend_back(
        mine, a_turned, hidden_b, hidden_turned, qkv, mixed, log_total, inputs, hidden_grad,
        line(first_gain), qkv_full, merge_full,
    )
    bias_grad = jnp.moveaxis(bias_grad.reshape(groups, halves, 3, PAIR), 0, 2).reshape(halves, 3, -1)
    expand_bias_grad = jnp.moveaxis(expand_bias_grad.reshape(steps, halves, columns), 0, 1)
    sums = jnp.sum(jnp.concatenate([first_sums, second_sums, reduce_bias_grad[None]]), axis=1)
    small = jnp.concatenate(
        [
            sums.reshape(-1),
            bias_grad[:, 0].reshape(-1),
            bias_grad[:, 2].reshape(-1),
            expand_bias_grad.reshape(-1),
            jnp.sum(loss).reshape(1),
        ]
    )
    length = small.shape[0]
    small = jnp.pad(small, (0, -length % 1024)).reshape(-1, 128)
    size = sizes()
    places = tuple(size[a] for a in AXES)
    heads_grad, merge_grad, expand_grad, small = scatter(
        [
            heads_grad.reshape(3, *places, -1, piece_width),
            merge_grad.reshape(*places, -1, piece_width),
            expand_grad.reshape(*places, -1, hidden // halves),
        ],
        small, 1, piece_width, (), 1,
    )
    small = small.reshape(-1)
    vectors = small[: 6 * width].reshape(6, width)
    heads_bias_sum = lax.dynamic_slice_in_dim(
        small[6 * width : 8 * width].reshape(2, width), tensor * piece_width, piece_width, 1
    )
    expand_bias_sum = lax.dynamic_slice_in_dim(
        small, 8 * width + tensor * (hidden // halves), hidden // halves
    )
    return (
        small[length - 1] / count,
        outputs,
        inputs_grad,
        vectors[0],
        vectors[1],
        heads_grad,
        heads_bias_sum,
        merge_grad,
        vectors[4],
        vectors[2],
        vectors[3],
        expand_grad,
        expand_bias_sum,
        reduce_grad,
        vectors[5],
    )


def solution(mesh):
    return jax.shard_map(
        body,
        mesh=mesh,
        in_specs=(
            P(("dp", "tensor"), None),
            P(("dp", "tensor"), None),
            P(),
            P(),
            P(),
            P(None, "dp", "tensor"),
            P(None, "tensor"),
            P("dp", "tensor"),
            P(),
            P(),
            P(),
            P("dp", "tensor"),
            P("tensor"),
            P("dp", "tensor"),
            P(),
        ),
        out_specs=(
            P(),
            P(("dp", "tensor"), None),
            P(("dp", "tensor"), None),
            P(),
            P(),
            P(None, "dp", "tensor"),
            P(None, "tensor"),
            P("dp", "tensor"),
            P(),
            P(),
            P(),
            P("dp", "tensor"),
            P("tensor"),
            P("dp", "tensor"),
            P(),
        ),
        check_vma=False,
    )
```

```python
from functools import partial
import math

import jax
import jax.numpy as jnp
import numpy as np
from jax import lax
from jax.experimental import pallas as pl
from jax.experimental.pallas import tpu as pltpu
from jax.sharding import PartitionSpec as P

HD = 64
SLOTS = 320
PAIR = 2 * HD

EPSILON = 1e-05
MASKED_SCORE = -1e30
F32 = jnp.float32
BF16 = jnp.bfloat16
CORES = 2
LINE = 4


AXES = ("tensor", "line", "row", "core")
MESH = pl.DeviceIdType.MESH
GATHER_ORDERS = (("line", "tensor", "row", "core"), ("line", "row", "tensor", "core"))


def sizes():
    dp = lax.axis_size("dp")
    return {"tensor": lax.axis_size("tensor"), "line": LINE, "row": dp // (LINE * CORES), "core": CORES}


class Place:
    def __init__(self):
        self.size = sizes()
        index = lax.axis_index("dp")
        self.at = {
            "tensor": lax.axis_index("tensor"),
            "core": lax.rem(index, CORES),
            "row": lax.rem(lax.div(index, CORES), self.size["row"]),
            "line": lax.div(index, CORES * self.size["row"]),
        }

    def steps(self, axis):
        return range(1, self.size[axis])

    def peer(self, axis, step):
        return lax.rem(self.at[axis] + step, self.size[axis])

    def device(self, axis, place):
        at = {**self.at, axis: place}
        return {"dp": (at["line"] * self.size["row"] + at["row"]) * CORES + at["core"], "tensor": at["tensor"]}

    def greet(self):
        barrier = pltpu.get_barrier_semaphore()
        count = 0
        for axis in AXES:
            for step in self.steps(axis):
                pl.semaphore_signal(
                    barrier, inc=1, device_id=self.device(axis, self.peer(axis, step)), device_id_type=MESH
                )
                count += 1
        pl.semaphore_wait(barrier, count)


def pieces_of(shards, width):
    out = []
    for a, shard in enumerate(shards):
        for lead in range(shard.shape[0]) if len(shard.shape) == 3 else (None,):
            for col in range(shard.shape[-1] // width):
                out.append((a, lead, col))
    return out


def piece(refs, which, width):
    a, lead, col = which
    ref = refs[a] if lead is None else refs[a].at[lead]
    spare = (slice(None),) * (len(ref.shape) - 1)
    return ref.at[(*spare, pl.ds(col * width, width))]


def whole_shape(weight):
    size = sizes()
    return (*weight.shape[:-2], *(size[a] for a in AXES), *weight.shape[-2:])


class Gather:
    def __init__(self, pieces, width, offsets, ins, outs, sems):
        self.here = Place()
        self.pieces, self.width, self.offsets, self.ins, self.outs = pieces, width, offsets, ins, outs
        self.send_sem, self.recv_sem, self.own_sem = sems
        self.half = ins[0].shape[-2] // 2
        self.count = len(pieces)

    def region(self, n, h, stage, axis=None, place=None):
        order = GATHER_ORDERS[h]
        index = [
            slice(None) if a in order[:stage] else place if a == axis else self.here.at[a] for a in AXES
        ]
        return piece(self.outs, self.pieces[n], self.width).at[(*index, pl.ds(h * self.half, self.half))]

    def remote(self, n, h, stage, step, coming=False):
        here, axis = self.here, GATHER_ORDERS[h][stage]
        slot = (n, h, stage, step - 1)
        to = source = self.region(n, h, stage)
        if stage == 0:
            source = piece(self.ins, self.pieces[n], self.width).at[pl.ds(h * self.half, self.half)]
        if coming:
            to = self.region(n, h, stage, axis, here.peer(axis, here.size[axis] - step))
        return pltpu.make_async_remote_copy(
            src_ref=source, dst_ref=to, send_sem=self.send_sem.at[slot], recv_sem=self.recv_sem.at[slot],
            device_id=here.device(axis, here.peer(axis, step)), device_id_type=MESH,
        )

    def every(self, n, stage):
        return [(n, h, stage, step) for h in range(2) for step in self.here.steps(GATHER_ORDERS[h][stage])]

    def start(self, n, stage):
        for slot in self.every(n, stage):
            self.remote(*slot).start()

    def arrived(self, n, stage=3):
        for slot in self.every(n, stage):
            self.remote(*slot, coming=True).wait_recv()

    def own(self, n):
        place = tuple(self.here.at[a] for a in AXES)
        return pltpu.make_async_copy(
            piece(self.ins, self.pieces[n], self.width),
            piece(self.outs, self.pieces[n], self.width).at[place], self.own_sem.at[n],
        )

    def begin(self):
        self.here.greet()
        for n in range(self.count):
            self.start(n, 0)
            self.own(n).start()

    def ticks(self):
        return self.count + self.offsets[-1]

    def tick(self, k):
        for stage, offset in enumerate(self.offsets, 1):
            n = k - offset
            if 0 <= n < self.count:
                if stage == 1:
                    self.own(n).wait()
                self.arrived(n, stage - 1)
                self.start(n, stage)

    def end(self):
        for n in range(self.count):
            for stage in range(4):
                for slot in self.every(n, stage):
                    self.remote(*slot).wait_send()


class Share:
    def __init__(self, here, source, target, sems):
        self.here, self.source, self.target = here, source, target
        self.send_sem, self.recv_sem, self.own_sem = sems

    def remote(self, step, coming=False):
        here = self.here
        place = here.peer("tensor", here.size["tensor"] - step) if coming else here.at["tensor"]
        return pltpu.make_async_remote_copy(
            src_ref=self.source, dst_ref=self.target.at[place],
            send_sem=self.send_sem.at[step - 1], recv_sem=self.recv_sem.at[step - 1],
            device_id=here.device("tensor", here.peer("tensor", step)), device_id_type=MESH,
        )

    def own(self):
        return pltpu.make_async_copy(self.source, self.target.at[self.here.at["tensor"]], self.own_sem)

    def begin(self):
        self.own().start()
        for step in self.here.steps("tensor"):
            self.remote(step).start()

    def arrived(self):
        self.own().wait()
        for step in self.here.steps("tensor"):
            self.remote(step, coming=True).wait_recv()

    def end(self):
        for step in self.here.steps("tensor"):
            self.remote(step).wait_send()


SCATTER_ORDERS = (("tensor", "row", "line"), ("row", "tensor", "line"))
THREE = AXES[:3]


def late_shapes(count, rows, columns):
    size, out = sizes(), []
    for order in SCATTER_ORDERS:
        for stage in (1, 2, 3):
            free = [size[a] for a in THREE if a not in order[:stage]]
            out.append((count, size[order[stage - 1]] - 1, *free, rows // 2, columns))
    return out


def scatter_scratch(count, rows, columns):
    size = sizes()
    most = max(size.values()) - 1
    half_piece = (count, *(size[a] for a in THREE), rows, columns)
    return [
        pltpu.VMEM(half_piece, BF16),
        pltpu.VMEM(half_piece, BF16),
        *[pltpu.VMEM(dims, BF16) for dims in late_shapes(count, rows, columns)],
        pltpu.SemaphoreType.DMA((count, 2, 4, most)),
        pltpu.SemaphoreType.DMA((count, 2, 4, most)),
    ]


SCATTER_REFS = 10


def plus(terms):
    if len(terms) == 2:
        return terms[0] + terms[1]
    return sum(term.astype(F32) for term in terms).astype(BF16)


class Scatter:
    def __init__(self, here, staging, out, refs):
        self.here, self.staging, self.out = here, staging, out
        self.own, self.first, *late, self.send_sem, self.recv_sem = refs
        self.late = {(h, s): late[h * 3 + s - 1] for h in range(2) for s in (1, 2, 3)}
        self.half = self.own.shape[-2] // 2

    def to_core(self, n):
        here = self.here
        other = here.peer("core", 1)
        return pltpu.make_async_remote_copy(
            src_ref=self.staging(n).at[:, :, :, other], dst_ref=self.first.at[n],
            send_sem=self.send_sem.at[n, 0, 0, 0], recv_sem=self.recv_sem.at[n, 0, 0, 0],
            device_id=here.device("core", other), device_id_type=MESH,
        )

    def remote(self, n, h, stage, step):
        here, order = self.here, SCATTER_ORDERS[h]
        axis = order[stage - 1]
        to = here.peer(axis, step)
        index = [
            here.at[a] if a in order[: stage - 1] else to if a == axis else slice(None) for a in THREE
        ]
        slot = (n, h, stage, step - 1)
        return pltpu.make_async_remote_copy(
            src_ref=self.own.at[(n, *index, pl.ds(h * self.half, self.half))],
            dst_ref=self.late[h, stage].at[n, step - 1],
            send_sem=self.send_sem.at[slot], recv_sem=self.recv_sem.at[slot],
            device_id=here.device(axis, to), device_id_type=MESH,
        )

    def every(self, n, stage):
        return [
            self.remote(n, h, stage, step)
            for h in range(2)
            for step in self.here.steps(SCATTER_ORDERS[h][stage - 1])
        ]

    def add_core(self, n):
        source, core = self.staging(n), self.here.at["core"]
        for at in np.ndindex(self.own.shape[1:3]):
            self.own[(n, *at)] = plus([source[(*at, slice(None), core)], self.first[(n, *at)]])

    def add(self, n, h, stage):
        here, order = self.here, SCATTER_ORDERS[h]
        buf, steps = self.late[h, stage], here.size[order[stage - 1]] - 1
        free = [a for a in THREE if a not in order[:stage]]
        rows = pl.ds(h * self.half, self.half)
        for free_at in np.ndindex(*(here.size[a] for a in free)):
            at = {**here.at, **dict(zip(free, free_at, strict=True))}
            mine = (n, *(at[a] for a in THREE), rows)
            terms = [self.own[mine]] + [buf[(n, s, *free_at)] for s in range(steps)]
            if stage == 3:
                self.out(n)[rows, :] = sum(term.astype(F32) for term in terms)
            else:
                self.own[mine] = plus(terms)

    def begin(self, n):
        self.to_core(n).start()

    def tick(self, n, stage):
        if stage == 0:
            copy = self.to_core(n)
            copy.wait_recv()
            copy.wait_send()
            self.add_core(n)
        else:
            for copy in self.every(n, stage):
                copy.wait_recv()
            for h in range(2):
                self.add(n, h, stage)
        if stage < 3:
            for copy in self.every(n, stage + 1):
                copy.start()

    def end(self, count):
        def one(n, _):
            for stage in (1, 2, 3):
                for copy in self.every(n, stage):
                    copy.wait_send()
            return 0

        lax.fori_loop(0, count, one, 0)


SUM_AXES = ("core", "tensor", "row", "line")


class SmallSum:
    def __init__(self, here, refs):
        self.here = here
        *self.bufs, self.send_sem, self.recv_sem = refs

    @staticmethod
    def scratch(dims):
        size = sizes()
        most = max(size.values()) - 1
        return [
            *[pltpu.VMEM((size[a], *dims), F32) for a in SUM_AXES],
            pltpu.SemaphoreType.DMA((4, most)),
            pltpu.SemaphoreType.DMA((4, most)),
        ]

    def remote(self, stage, step, coming=False):
        here, axis, buf = self.here, SUM_AXES[stage], self.bufs[stage]
        place = here.peer(axis, here.size[axis] - step) if coming else here.at[axis]
        return pltpu.make_async_remote_copy(
            src_ref=buf.at[here.at[axis]], dst_ref=buf.at[place],
            send_sem=self.send_sem.at[stage, step - 1], recv_sem=self.recv_sem.at[stage, step - 1],
            device_id=here.device(axis, here.peer(axis, step)), device_id_type=MESH,
        )

    def start(self, stage, value):
        self.bufs[stage][self.here.at[SUM_AXES[stage]]] = value
        self.send(stage)

    def send(self, stage):
        for step in self.here.steps(SUM_AXES[stage]):
            self.remote(stage, step).start()

    def finish(self, stage):
        axis = SUM_AXES[stage]
        for step in self.here.steps(axis):
            self.remote(stage, step, coming=True).wait_recv()
            self.remote(stage, step).wait_send()
        total = self.bufs[stage][0]
        for place in range(1, self.here.size[axis]):
            total += self.bufs[stage][place]
        return total

    def tick(self, stage, target):
        total = self.finish(stage)
        if stage < 3:
            self.start(stage + 1, total)
        else:
            target[...] = total


SMALL_REFS = 6


def dot(left, right, left_dim=1, right_dim=0):
    return lax.dot_general(
        left, right, (((left_dim,), (right_dim,)), ((), ())), preferred_element_type=F32
    )


def side_by_side(ref, *lead):
    return jnp.concatenate([ref[(*lead, t)] for t in range(ref.shape[-3])], axis=-1)


def centred(rows):
    off = rows - jnp.mean(rows, axis=-1, keepdims=True)
    inverse = lax.rsqrt(jnp.mean(off * off, axis=-1, keepdims=True) + EPSILON)
    return off * inverse, inverse


def norm_back(grad, hat, inverse, gain):
    scaled = grad * gain
    along = jnp.mean(scaled * hat, axis=-1, keepdims=True)
    return inverse * (scaled - jnp.mean(scaled, axis=-1, keepdims=True) - hat * along)


def fold(rows):
    return jnp.sum(rows.reshape(-1, 8, rows.shape[-1]), axis=0)


def row_blocks(rows, size, one):
    def step(i, _):
        one(i, pl.ds(pl.multiple_of(i * size, size), size))
        return 0

    lax.fori_loop(0, rows // size, step, 0)


def transpose_into(source, target):
    rows = source.shape[0]
    for first in range(0, rows, 128):
        size = min(128, rows - first)
        target[:, first : first + size] = source[first : first + size, :].astype(F32).T.astype(BF16)


def two_heads(pair):
    first = lax.broadcasted_iota(jnp.int32, pair.shape, 1) < HD
    zero = jnp.zeros_like(pair)
    return jnp.concatenate([jnp.where(first, pair, zero), jnp.where(first, zero, pair)], axis=0)


def one_pair(stacked):
    first = lax.broadcasted_iota(jnp.int32, (SLOTS, PAIR), 1) < HD
    return jnp.where(first, stacked[:SLOTS], stacked[SLOTS:])


def masked_scores(query_stack, keys, length):
    scores = dot(keys, query_stack, 1, 1)
    slot = lax.broadcasted_iota(jnp.int32, scores.shape, 0)
    return jnp.where(slot < length, scores, MASKED_SCORE)


def group_weight(qkv_held, columns):
    parts = [qkv_held[e, t, ..., columns] for t in range(qkv_held.shape[1]) for e in range(3)]
    return jnp.concatenate([part.reshape(-1, PAIR) for part in parts], axis=-1)


def merge_tile(merge_held, columns):
    parts = [merge_held[t, ..., columns] for t in range(merge_held.shape[0])]
    return jnp.concatenate([part.reshape(-1, PAIR) for part in parts], axis=-1)


def schedule(ticks, last_piece, needed, steps):
    at = []
    first = needed.index(next(s for s in needed if s > 0), 0) if any(needed) else len(needed)
    early = first + last_piece
    for k in range(ticks):
        piece_done = k - last_piece
        even = 0 if k < early else 1 + (k - early) * (steps - 1) // (ticks - early)
        at.append(min(even, needed[max(piece_done, 0)]))
    for k in range(ticks - 2, -1, -1):
        at[k] = min(at[k], at[k + 1])
    return at


def forward_kernel(
    width_of_piece, offsets, feed_columns,
    lengths, x_ref, gain, shift, merge_bias, gain_2, shift_2, heads_bias, expand_bias,
    qkv_part, merge_part, expand_part, reduce_part,
    a_turned, qkv_ref, mixed_ref, log_ref, hidden_ref, second_ref, second_turned, activ, slope,
    qkv_full, merge_full, expand_full, reduce_full,
    a_ref, qkv_held, merge_held, tiles, heads_bias_all, expand_bias_all,
    send_sem, recv_sem, own_sem, share_send, share_recv, share_own, held_sem, tile_sem,
):
    now = pl.program_id(0)
    rows = x_ref.shape[0]
    images = rows // SLOTS
    halves = qkv_held.shape[1]
    groups = width_of_piece // PAIR
    attention_steps = groups * images
    feed_steps = expand_part.shape[1] // feed_columns
    steps = attention_steps + feed_steps
    parts = [qkv_part, merge_part, expand_part, reduce_part]
    pieces = pieces_of(parts, width_of_piece)
    gather = Gather(
        pieces, width_of_piece, offsets, parts, [qkv_full, merge_full, expand_full, reduce_full],
        (send_sem, recv_sem, own_sem),
    )
    shares = [
        Share(gather.here, source, target, (share_send.at[n], share_recv.at[n], share_own.at[n]))
        for n, (source, target) in enumerate([(heads_bias, heads_bias_all), (expand_bias, expand_bias_all)])
    ]
    tiles_of_piece = width_of_piece // feed_columns
    needed = [
        0 if a == 0 else images - 1 if a == 1
        else max(attention_steps + col * tiles_of_piece - 1, 0) if a == 2 else steps - 1
        for a, _, col in pieces
    ]
    when = schedule(gather.ticks(), offsets[-1], needed, steps)
    image = lax.rem(now, images)
    group = lax.min(lax.div(now, images), groups - 1)
    columns = pl.ds(pl.multiple_of(group * PAIR, PAIR), PAIR)

    def hold(n):
        a, lead, _ = pieces[n]
        source, target = (qkv_full.at[lead], qkv_held.at[lead]) if a == 0 else (merge_full, merge_held)
        return pltpu.make_async_copy(source, target, held_sem.at[n])

    def tile_copy(j):
        block = pl.ds(j * feed_columns, feed_columns)
        return pltpu.make_async_copy(
            expand_full.at[:, :, :, :, :, block], tiles.at[j % 2], tile_sem.at[j % 2]
        )

    def fetch_tile(j):
        if j % tiles_of_piece == 0:
            gather.arrived(4 + j // tiles_of_piece)
        tile_copy(j).start()

    @pl.when(now == 0)
    def _():
        gather.begin()
        for share in shares:
            share.begin()
        early = [k for k in range(gather.ticks()) if when[k] == 0]
        blocks = rows // 32
        per = -(-blocks // max(len(early), 1))

        def norm(i, _):
            at = pl.ds(pl.multiple_of(i * 32, 32), 32)
            x = x_ref[at, :].astype(F32)
            hidden_ref[at, :] = x + merge_bias[...]
            a_ref[at, :] = (centred(x)[0] * gain[...] + shift[...]).astype(BF16)
            return 0

        done = 0
        for k in early:
            lax.fori_loop(done, min(done + per, blocks), norm, 0)
            done = min(done + per, blocks)
            gather.tick(k)
            n = k - offsets[-1] - 1
            if 0 <= n < 3:
                gather.arrived(n)
                hold(n).start()
        lax.fori_loop(done, blocks, norm, 0)
        transpose_into(a_ref, a_turned)
        for n in range(max(len(early) - offsets[-1] - 1, 0), 3):
            gather.arrived(n)
            hold(n).start()
        for share in shares:
            share.arrived()
        for n in range(3):
            hold(n).wait()

    for k in range(gather.ticks()):
        if when[k] > 0:
            pl.when(now == when[k])(partial(gather.tick, k))

    @pl.when((now < attention_steps) & (image == 0))
    def _():
        weight = group_weight(qkv_held, columns)
        bias = []
        for t in range(halves):
            query = heads_bias_all[t, 0:1, columns]
            bias += [query, jnp.zeros_like(query), heads_bias_all[t, 1:2, columns]]
        bias = jnp.concatenate(bias, axis=-1)
        for i in range(images):
            at = slice(i * SLOTS, (i + 1) * SLOTS)
            out = (dot(a_ref[at, :], weight) + bias).astype(BF16)
            for t in range(halves):
                query = slice(t * 3 * PAIR, (t * 3 + 1) * PAIR)
                qkv_ref[0, at, query] = out[:, query] * 0.125
                rest = slice((t * 3 + 1) * PAIR, (t * 3 + 3) * PAIR)
                qkv_ref[0, at, rest] = out[:, rest]

    @pl.when(now < attention_steps)
    def _():
        length = lengths[image]
        at = pl.ds(pl.multiple_of(image * SLOTS, SLOTS), SLOTS)
        for t in range(halves):
            first = t * 3 * PAIR
            query_stack = two_heads(qkv_ref[0, at, first : first + PAIR])
            scores = masked_scores(query_stack, qkv_ref[0, at, first + PAIR : first + 2 * PAIR], length)
            highest = jnp.max(scores, axis=0, keepdims=True)
            expo = jnp.exp(scores - highest)
            totals = jnp.sum(expo, axis=0, keepdims=True)
            values = qkv_ref[0, at, first + 2 * PAIR : first + 3 * PAIR]
            mixed = dot(values, expo.astype(BF16), 0, 0) * (1.0 / totals)
            mixed_ref[0, at, t * PAIR : (t + 1) * PAIR] = one_pair(mixed.T).astype(BF16)
            log_ref[0, 0, t : t + 1] = highest + jnp.log(totals)

    @pl.when(now == images - 1)
    def _():
        gather.arrived(3)
        hold(3).start()
        hold(3).wait()

    @pl.when((now < attention_steps) & (image == images - 1))
    def _():
        weight = merge_tile(merge_held, columns)
        for i in range(images):
            part = slice(i * SLOTS, (i + 1) * SLOTS)
            hidden_ref[part, :] += dot(mixed_ref[0, part, :], weight, 1, 1)

    @pl.when(now == attention_steps - 1)
    def _():
        fetch_tile(0)

        def norm(_, at):
            hat, _ = centred(hidden_ref[at, :])
            second_ref[at, :] = (hat * gain_2[...] + shift_2[...]).astype(BF16)

        row_blocks(rows, 32, norm)
        transpose_into(second_ref, second_turned)

    for j in range(feed_steps):

        @pl.when(now == attention_steps + j)
        def _(j=j):
            tile_copy(j).wait()
            if j + 1 < feed_steps:
                fetch_tile(j + 1)

    @pl.when(now >= attention_steps)
    def _():
        j = now - attention_steps
        block = pl.ds(pl.multiple_of(j * feed_columns, feed_columns), feed_columns)
        slot = lax.rem(j, 2)
        weight = jnp.concatenate(
            [tiles[slot, t].reshape(-1, feed_columns) for t in range(halves)], axis=-1
        )
        bias = jnp.concatenate([expand_bias_all[t, :, block] for t in range(halves)], axis=-1)
        for i in range(images):
            at = slice(i * SLOTS, (i + 1) * SLOTS)
            z = dot(second_ref[at, :], weight) + bias
            square = z * z
            bend = jnp.tanh(0.7978845608 * z * (1.0 + 0.044715 * square))
            half = 0.5 + 0.5 * bend
            activ[0, at, :] = (z * half).astype(BF16)
            inner = 0.7978845608 * z * (1.0 + (3 * 0.044715) * square)
            slope[0, at, :] = (half + 0.5 * inner * (1.0 - bend * bend)).astype(BF16)

    @pl.when(now == steps - 1)
    def _():
        for n in range(8, gather.count):
            gather.arrived(n)
        gather.end()
        for share in shares:
            share.end()


def feed_kernel(
    lengths, count, activ, hidden, reduce, reduce_bias, teacher,
    out, grad, grad_b, grad_turned, bias_grad, loss, total,
):
    step = pl.program_id(0)
    rows = hidden.shape[0]
    reduce_tile = side_by_side(reduce)

    @pl.when(step == 0)
    def _():
        total[...] = jnp.zeros_like(total)

    for i in range(rows // SLOTS):
        at = slice(i * SLOTS, (i + 1) * SLOTS)
        total[at, :] += dot(activ[0, at, :], reduce_tile, 1, 1)

    @pl.when(step == pl.num_programs(0) - 1)
    def _():
        bias_grad[...] = jnp.zeros_like(bias_grad)
        loss[...] = jnp.zeros_like(loss)

        def end(i, at):
            image, block = lax.div(i, SLOTS // 32), lax.rem(i, SLOTS // 32)
            slot = block * 32 + lax.broadcasted_iota(jnp.int32, (32, 1), 0)
            valid = slot < lengths[image]
            result = jnp.where(valid, hidden[at, :] + total[at, :] + reduce_bias[...], 0.0)
            out[at, :] = result.astype(BF16)
            error = jnp.where(valid, result - teacher[at, :].astype(F32), 0.0)
            loss[0] += fold(error * error)
            back = 2.0 * error / count[0]
            bias_grad[0] += fold(back)
            grad[at, :] = back
            grad_b[at, :] = back.astype(BF16)

        row_blocks(rows, 32, end)
        transpose_into(grad_b, grad_turned)


def feed_back_kernel(
    result_b, result_turned, second_turned, expand, reduce, activ, slope, hidden, result_grad, gain,
    reduce_grad, expand_grad, expand_bias_grad, hidden_grad, hidden_b, hidden_turned, sums,
    total, staging, *scatter_refs,
):
    step, steps = pl.program_id(0), reduce_grad.shape[1] // expand.shape[-1]
    rows, width = result_b.shape
    halves, _, columns = expand.shape
    expand_tile, reduce_tile = side_by_side(expand), side_by_side(reduce)

    scatters = []
    here = Place()
    for p, target in enumerate((reduce_grad, expand_grad)):
        slot = lambda j, p=p: staging.at[lax.rem(j, 2), p]
        part = lambda j, target=target: target.at[:, pl.ds(pl.multiple_of(j * columns, columns), columns)]
        scatters.append(Scatter(here, slot, part, scatter_refs[p * SCATTER_REFS : (p + 1) * SCATTER_REFS]))

    @pl.when(step == 0)
    def _():
        here.greet()
        total[...] = jnp.zeros_like(total)

    for stage in range(3, -1, -1):

        @pl.when(step >= stage + 1)
        def _(stage=stage):
            for scatter in scatters:
                scatter.tick(step - 1 - stage, stage)

    def stage_out(p, part):
        for t in range(halves):
            block = part[:, t * columns : (t + 1) * columns].astype(BF16)
            staging[lax.rem(step, 2), p, t] = block.reshape(staging.shape[3:])
        scatters[p].begin(step)

    stage_out(0, dot(result_turned[...], activ[0]))
    bias = jnp.zeros((8, halves * columns), F32)
    parts = []
    for i in range(rows // SLOTS):
        at = slice(i * SLOTS, (i + 1) * SLOTS)
        z_grad = (dot(result_b[at, :], reduce_tile) * slope[0, at, :].astype(F32)).astype(BF16)
        bias += fold(z_grad.astype(F32))
        parts.append(z_grad)
        total[at, :] += dot(z_grad, expand_tile, 1, 1)
    expand_bias_grad[0] = jnp.sum(bias, axis=0, keepdims=True)
    stage_out(1, dot(second_turned[...], jnp.concatenate(parts, axis=0)))

    @pl.when(step == steps - 1)
    def _():
        sums[...] = jnp.zeros_like(sums)
        size = 128 if rows % 128 == 0 else rows
        blocks = rows // size

        def end(first, h_ref, g_ref, back_ref, back_b_ref, turned_ref):
            block = pl.program_id(0) + first
            for k in range(0, size, 32):
                at = slice(k, k + 32)
                hat, inverse = centred(h_ref[at, :])
                second_grad = total[pl.ds(pl.multiple_of(block * size + k, 32), 32), :]
                back = g_ref[at, :] + norm_back(second_grad, hat, inverse, gain[...])
                sums[0] += fold(second_grad * hat)
                sums[1] += fold(second_grad)
                sums[2] += fold(back)
                back_ref[at, :] = back
                back_b_ref[at, :] = back.astype(BF16)
            turned_ref[...] = back_ref[...].T.astype(BF16)

        def some(first, last):
            row_block = pl.BlockSpec((size, width), lambda i: (i + first, 0))
            pltpu.emit_pipeline(
                partial(end, first),
                grid=(last - first,),
                in_specs=[row_block, row_block],
                out_specs=[row_block, row_block, pl.BlockSpec((width, size), lambda i: (0, i + first))],
            )(hidden, result_grad, hidden_grad, hidden_b, hidden_turned)

        bounds = [blocks * k // 3 for k in range(4)]
        for drain in range(4):
            for stage in range(3, -1, -1):
                for scatter in scatters:
                    if stage >= drain and steps + drain - 1 - stage >= 0:
                        scatter.tick(steps + drain - 1 - stage, stage)
            if drain < 3 and bounds[drain + 1] > bounds[drain]:
                some(bounds[drain], bounds[drain + 1])
        for scatter in scatters:
            scatter.end(steps)


def attend_back_kernel(
    lengths, a_turned, hidden_b, hidden_turned, qkv_ref, mixed_ref, log_ref, x_ref, hidden_grad, gain,
    qkv_weight, merge_weight, second_sums, reduce_bias_grad, loss, expand_bias_grad,
    merge_grad, qkv_grad, inputs_grad, early_out, expand_out, late_out, heads_out,
    mixed_grad, heads_grad, total, qkv_held, merge_held, sem, merge_staging, qkv_staging, sums, bias_grad,
    *comm,
):
    now = pl.program_id(0)
    rows = x_ref.shape[0]
    images = rows // SLOTS
    halves = qkv_held.shape[1]
    groups = merge_grad.shape[1] // PAIR
    steps = groups * images
    group, image = lax.div(now, images), lax.rem(now, images)
    here = Place()
    block = lambda c: pl.ds(pl.multiple_of(c * PAIR, PAIR), PAIR)
    merge_scatter = Scatter(here, lambda n: merge_staging, lambda n: merge_grad.at[:, block(n)], comm[:SCATTER_REFS])
    qkv_scatter = Scatter(
        here, lambda n: qkv_staging.at[lax.rem(n, 3)],
        lambda n: qkv_grad.at[lax.rem(n, 3), :, block(lax.div(n, 3))], comm[SCATTER_REFS : 2 * SCATTER_REFS],
    )
    early, expand_sum, late, heads_sum = (
        SmallSum(here, comm[2 * SCATTER_REFS + k * SMALL_REFS :][:SMALL_REFS]) for k in range(4)
    )

    def merge_tick(c, stage):
        merge_scatter.tick(c, stage)

    def qkv_tick(c, stage):
        for e in range(3):
            qkv_scatter.tick(3 * c + e, stage)
    columns = pl.ds(pl.multiple_of(group * PAIR, PAIR), PAIR)

    @pl.when(now == 0)
    def _():
        copies = [
            pltpu.make_async_copy(merge_weight, merge_held, sem.at[1]),
            pltpu.make_async_copy(qkv_weight, qkv_held, sem.at[0]),
        ]
        for copy in copies:
            copy.start()
        here.greet()
        total[...] = jnp.zeros_like(total)
        rowsum = lambda ref, k: jnp.sum(ref[k], axis=0, keepdims=True)
        vectors = [rowsum(second_sums, k) for k in range(3)] + [rowsum(reduce_bias_grad, 0)]
        lost = jnp.sum(rowsum(loss, 0), axis=1, keepdims=True)
        vectors.append(jnp.broadcast_to(lost, vectors[0].shape))
        early.start(0, jnp.concatenate(vectors, axis=0))
        expand_sum.start(0, expand_bias_grad[:, 0])
        for copy in copies:
            copy.wait()

    for stage in range(4):

        @pl.when(now == min(stage + 1, steps - 1))
        def _(stage=stage):
            early.tick(stage, early_out)
            expand_sum.tick(stage, expand_out)

    for stage in range(3, -1, -1):
        for ready, tick in ((0, merge_tick), (images - 1, qkv_tick)):
            since = now - 1 - stage - ready

            @pl.when((since >= 0) & (lax.rem(since, images) == 0))
            def _(stage=stage, tick=tick, since=since):
                tick(lax.div(since, images), stage)

    @pl.when(image == 0)
    def _():
        weight = merge_tile(merge_held, columns)
        for i in range(rows // SLOTS):
            part = slice(i * SLOTS, (i + 1) * SLOTS)
            mixed_grad[part, :] = dot(hidden_b[part, :], weight).astype(BF16)
        part = dot(hidden_turned[...], mixed_ref[0]).astype(BF16)
        for t in range(halves):
            merge_staging[t] = part[:, t * PAIR : (t + 1) * PAIR].reshape(merge_staging.shape[1:])
        merge_scatter.begin(group)

    length = lengths[image]
    at = pl.ds(pl.multiple_of(image * SLOTS, SLOTS), SLOTS)
    for t in range(halves):
        first = t * 3 * PAIR
        query_stack = two_heads(qkv_ref[0, at, first : first + PAIR])
        keys = qkv_ref[0, at, first + PAIR : first + 2 * PAIR]
        values = qkv_ref[0, at, first + 2 * PAIR : first + 3 * PAIR]
        scores = masked_scores(query_stack, keys, length)
        attend = jnp.exp(scores - log_ref[0, 0, t : t + 1])
        grad_stack = two_heads(mixed_grad[at, t * PAIR : (t + 1) * PAIR])
        attend_grad = dot(values, grad_stack, 1, 1)
        value_grad = dot(attend.astype(BF16), grad_stack).astype(BF16)
        centre = jnp.sum(attend * attend_grad, axis=0, keepdims=True)
        score_grad = (attend * (attend_grad - centre)).astype(BF16)
        key_grad = dot(score_grad, query_stack).astype(BF16)
        query_grad = dot(keys, score_grad, 0, 0)
        query_grad = (one_pair(query_grad.T) * 0.125).astype(BF16)
        heads_grad[at, first : first + PAIR] = query_grad
        heads_grad[at, first + PAIR : first + 2 * PAIR] = key_grad
        heads_grad[at, first + 2 * PAIR : first + 3 * PAIR] = value_grad

    @pl.when(image == images - 1)
    def _():
        weight = group_weight(qkv_held, columns)
        bias = jnp.zeros((8, halves * 3 * PAIR), F32)
        for i in range(rows // SLOTS):
            part = slice(i * SLOTS, (i + 1) * SLOTS)
            bias += fold(heads_grad[part, :].astype(F32))
        bias_grad[pl.ds(group, 1), :] = jnp.sum(bias, axis=0, keepdims=True)
        part = dot(a_turned[...], heads_grad[...]).astype(BF16)
        for t in range(halves):
            for e in range(3):
                first = (t * 3 + e) * PAIR
                qkv_staging[e, t] = part[:, first : first + PAIR].reshape(qkv_staging.shape[2:])
        for e in range(3):
            qkv_scatter.begin(3 * group + e)
        for i in range(rows // SLOTS):
            part = slice(i * SLOTS, (i + 1) * SLOTS)
            total[part, :] += dot(heads_grad[part, :], weight, 1, 1)

    @pl.when(now == steps - 1)
    def _():
        heads_sum.start(0, bias_grad[...])
        sums[...] = jnp.zeros_like(sums)

        def end(i, _):
            at = pl.ds(pl.multiple_of(i * 32, 32), 32)
            hat, inverse = centred(x_ref[at, :].astype(F32))
            grad = total[at, :]
            sums[0] += fold(grad * hat)
            sums[1] += fold(grad)
            inputs_grad[at, :] = hidden_grad[at, :] + norm_back(grad, hat, inverse, gain[...])
            return 0

        blocks = rows // 32

        def drain(d):
            for stage in range(3, -1, -1):
                for ready, tick in ((0, merge_tick), (images - 1, qkv_tick)):
                    since = steps + d - 1 - stage - ready
                    if stage >= d and since >= 0 and since % images == 0 and since // images < groups:
                        tick(since // images, stage)

        drain(0)
        heads_sum.tick(0, heads_out)
        lax.fori_loop(0, blocks // 2, end, 0)
        drain(1)
        heads_sum.tick(1, heads_out)
        lax.fori_loop(blocks // 2, blocks, end, 0)
        late.start(0, jnp.sum(sums[...], axis=1))
        drain(2)
        heads_sum.tick(2, heads_out)
        late.tick(0, late_out)
        drain(3)
        heads_sum.tick(3, heads_out)
        for stage in range(1, 4):
            late.tick(stage, late_out)
        merge_scatter.end(groups)
        qkv_scatter.end(3 * groups)


def shape(dims, kind=BF16):
    return jax.ShapeDtypeStruct(dims, kind)


def once(dims):
    return pl.BlockSpec(dims, lambda *_: (0,) * len(dims), pipeline_mode=pl.Buffered(1))


ELSEWHERE = pl.BlockSpec(memory_space=pl.ANY)
SCALARS = pl.BlockSpec(memory_space=pltpu.SMEM)
LIMIT = 63 * 2**20


OFFSETS = (0, 1, 2)


def feed_width(halves):
    return max(PAIR, 512 // halves)


def forward(lengths, x, gain, shift, merge_bias, gain_2, shift_2, heads_bias, expand_bias, parts):
    rows, width = x.shape
    halves, columns = lax.axis_size("tensor"), parts[0].shape[2]
    groups, images = columns // PAIR, rows // SLOTS
    attention_steps = groups * images
    feed_columns = feed_width(halves)
    feed_steps = parts[2].shape[1] // feed_columns
    pieces = len(pieces_of(parts, columns))
    most = max(sizes().values()) - 1
    line = once((1, width))
    group_at = lambda s: lax.min(lax.div(s, images), groups - 1)
    feed_at = lambda s: lax.max(s - attention_steps, 0)
    wholes = [whole_shape(part) for part in parts]
    saved = pl.BlockSpec((1, rows, halves * feed_columns), lambda s: (feed_at(s), 0, 0))
    return pl.pallas_call(
        partial(forward_kernel, columns, OFFSETS, feed_columns),
        grid=(attention_steps + feed_steps,),
        in_specs=[SCALARS, once((rows, width)), *[line] * 5, *[ELSEWHERE] * 6],
        out_specs=[
            once((width, rows)),
            pl.BlockSpec((1, rows, halves * 3 * PAIR), lambda s: (group_at(s), 0, 0)),
            pl.BlockSpec((1, rows, halves * PAIR), lambda s: (group_at(s), 0, 0)),
            pl.BlockSpec(
                (1, 1, halves, 2 * SLOTS),
                lambda s: (group_at(s), jnp.where(s < attention_steps, lax.rem(s, images), images - 1), 0, 0),
            ),
            once((rows, width)), once((rows, width)), once((width, rows)), saved, saved,
            *[ELSEWHERE] * 4,
        ],
        out_shape=[
            shape((width, rows)),
            shape((groups, rows, halves * 3 * PAIR)),
            shape((groups, rows, halves * PAIR)),
            shape((groups, images, halves, 2 * SLOTS), F32),
            shape((rows, width), F32), shape((rows, width)), shape((width, rows)),
            *[shape((feed_steps, rows, halves * feed_columns))] * 2,
            *[shape(dims) for dims in wholes],
        ],
        scratch_shapes=[
            pltpu.VMEM((rows, width), BF16),
            pltpu.VMEM(wholes[0], BF16),
            pltpu.VMEM(wholes[1], BF16),
            pltpu.VMEM((2, *wholes[2][:-1], feed_columns), BF16),
            pltpu.VMEM((halves, *heads_bias.shape), F32),
            pltpu.VMEM((halves, *expand_bias.shape), F32),
            pltpu.SemaphoreType.DMA((pieces, 2, 4, most)),
            pltpu.SemaphoreType.DMA((pieces, 2, 4, most)),
            pltpu.SemaphoreType.DMA((pieces,)),
            pltpu.SemaphoreType.DMA((2, halves)),
            pltpu.SemaphoreType.DMA((2, halves)),
            pltpu.SemaphoreType.DMA((2,)),
            pltpu.SemaphoreType.DMA((4,)),
            pltpu.SemaphoreType.DMA((2,)),
        ],
        compiler_params=pltpu.CompilerParams(
            vmem_limit_bytes=LIMIT, collective_id=0, has_side_effects=True
        ),
        name="forward",
    )(lengths, x, gain, shift, merge_bias, gain_2, shift_2, heads_bias, expand_bias, *parts)


def feed(lengths, count, activ, hidden, reduce, reduce_bias, teacher):
    rows, width = hidden.shape
    halves, _, wide = reduce.shape
    steps, columns = activ.shape[0], activ.shape[2] // halves
    whole = once((rows, width))
    return pl.pallas_call(
        feed_kernel,
        grid=(steps,),
        in_specs=[
            SCALARS, SCALARS, pl.BlockSpec((1, rows, halves * columns), lambda j: (j, 0, 0)), whole,
            pl.BlockSpec((halves, width, columns), lambda j: (0, 0, j)), once((1, width)), whole,
        ],
        out_specs=[whole, whole, whole, once((width, rows)), once((1, 8, width)), once((1, 8, width))],
        out_shape=[
            shape((rows, width)), shape((rows, width), F32), shape((rows, width)), shape((width, rows)),
            shape((1, 8, width), F32), shape((1, 8, width), F32),
        ],
        scratch_shapes=[pltpu.VMEM((rows, width), F32)],
        compiler_params=pltpu.CompilerParams(vmem_limit_bytes=LIMIT),
        cost_estimate=pl.CostEstimate(
            flops=2 * rows * width * halves * wide,
            bytes_accessed=2 * rows * halves * wide + 2 * width * halves * wide + 20 * rows * width,
            transcendentals=0,
        ),
        name="feed",
    )(lengths, count, activ, hidden, reduce, reduce_bias, teacher)


def feed_back(result_b, result_turned, second_turned, expand, reduce, activ, slope, hidden, result_grad, gain):
    rows, width = result_b.shape
    halves, _, wide = expand.shape
    steps, columns = activ.shape[0], activ.shape[2] // halves
    size = sizes()
    part_rows = width // math.prod(size[a] for a in ("line", "row", "core"))
    tile = pl.BlockSpec((halves, width, columns), lambda j: (0, 0, j))
    saved = pl.BlockSpec((1, rows, halves * columns), lambda j: (j, 0, 0))
    whole, turned, part = once((rows, width)), once((width, rows)), once((part_rows, wide))
    return pl.pallas_call(
        feed_back_kernel,
        grid=(steps,),
        in_specs=[whole, turned, turned, tile, tile, saved, saved, ELSEWHERE, ELSEWHERE, once((1, width))],
        out_specs=[
            part, part, pl.BlockSpec((1, 1, halves * columns), lambda j: (j, 0, 0)),
            ELSEWHERE, ELSEWHERE, ELSEWHERE, once((3, 8, width)),
        ],
        out_shape=[
            shape((part_rows, wide), F32), shape((part_rows, wide), F32),
            shape((steps, 1, halves * columns), F32),
            shape((rows, width), F32), shape((rows, width)), shape((width, rows)), shape((3, 8, width), F32),
        ],
        scratch_shapes=[
            pltpu.VMEM((rows, width), F32),
            pltpu.VMEM((2, 2, *(size[a] for a in AXES), part_rows, columns), BF16),
            *scatter_scratch(steps, part_rows, columns),
            *scatter_scratch(steps, part_rows, columns),
        ],
        compiler_params=pltpu.CompilerParams(
            vmem_limit_bytes=LIMIT, collective_id=1, has_side_effects=True
        ),
        name="feed_back",
    )(result_b, result_turned, second_turned, expand, reduce, activ, slope, hidden, result_grad, gain)


def attend_back(
    lengths, a_turned, hidden_b, hidden_turned, qkv, mixed, log_total, x, hidden_grad, gain,
    qkv_whole, merge_whole, second_sums, reduce_bias_grad, loss, expand_bias_grad,
):
    rows, width = x.shape
    halves, (part_rows, columns) = qkv_whole.shape[1], qkv_whole.shape[-2:]
    groups, images = columns // PAIR, rows // SLOTS
    whole, turned = once((rows, width)), once((width, rows))
    group_at = lambda s: lax.div(s, images)
    size = sizes()
    staging = (*(size[a] for a in AXES), part_rows, PAIR)
    small = [(5, width), (expand_bias_grad.shape[0], expand_bias_grad.shape[2]), (2, width), (groups, halves * 3 * PAIR)]
    vmem = lambda array: once(array.shape)
    return pl.pallas_call(
        attend_back_kernel,
        grid=(groups * images,),
        in_specs=[
            SCALARS, turned, whole, turned,
            pl.BlockSpec((1, rows, halves * 3 * PAIR), lambda s: (group_at(s), 0, 0)),
            pl.BlockSpec((1, rows, halves * PAIR), lambda s: (group_at(s), 0, 0)),
            pl.BlockSpec((1, 1, halves, 2 * SLOTS), lambda s: (group_at(s), lax.rem(s, images), 0, 0)),
            whole, whole, once((1, width)), ELSEWHERE, ELSEWHERE,
            vmem(second_sums), vmem(reduce_bias_grad), vmem(loss), vmem(expand_bias_grad),
        ],
        out_specs=[
            once((part_rows, columns)), once((3, part_rows, columns)), whole, *[once(dims) for dims in small]
        ],
        out_shape=[
            shape((part_rows, columns), F32), shape((3, part_rows, columns), F32), shape((rows, width), F32),
            *[shape(dims, F32) for dims in small],
        ],
        scratch_shapes=[
            pltpu.VMEM((rows, halves * PAIR), BF16),
            pltpu.VMEM((rows, halves * 3 * PAIR), BF16),
            pltpu.VMEM((rows, width), F32),
            pltpu.VMEM(qkv_whole.shape, BF16),
            pltpu.VMEM(merge_whole.shape, BF16),
            pltpu.SemaphoreType.DMA((2,)),
            pltpu.VMEM(staging, BF16),
            pltpu.VMEM((3, *staging), BF16),
            pltpu.VMEM((2, 8, width), F32),
            pltpu.VMEM((groups, halves * 3 * PAIR), F32),
            *scatter_scratch(groups, part_rows, PAIR),
            *scatter_scratch(3 * groups, part_rows, PAIR),
            *[ref for dims in small for ref in SmallSum.scratch(dims)],
        ],
        compiler_params=pltpu.CompilerParams(
            vmem_limit_bytes=LIMIT, collective_id=2, has_side_effects=True
        ),
        name="attend_back",
    )(
        lengths, a_turned, hidden_b, hidden_turned, qkv, mixed, log_total, x, hidden_grad, gain,
        qkv_whole, merge_whole, second_sums, reduce_bias_grad, loss, expand_bias_grad,
    )


def body(
    inputs,
    teacher,
    lengths,
    first_gain,
    first_shift,
    query_key_value_weight,
    heads_bias,
    merge_weight,
    merge_bias,
    second_gain,
    second_shift,
    expand_weight,
    expand_bias,
    reduce_weight,
    reduce_bias,
):
    rows, width = inputs.shape
    images = rows // SLOTS
    halves = lax.axis_size("tensor")
    tensor = lax.axis_index("tensor")
    hidden = expand_weight.shape[1] * halves
    piece_width = query_key_value_weight.shape[-1]
    groups = piece_width // PAIR
    place = lax.axis_index("dp") * halves + tensor
    mine = lax.dynamic_slice_in_dim(lengths, place * images, images)
    count = jnp.sum(lengths).astype(F32)
    line = lambda vector: vector.reshape(1, width)

    a_turned, qkv, mixed, log_total, hidden_state, _, second_turned, activ, slope, *wholes = forward(
        mine, inputs, line(first_gain), line(first_shift), line(merge_bias), line(second_gain),
        line(second_shift), heads_bias, expand_bias.reshape(1, -1),
        [query_key_value_weight, merge_weight, expand_weight, reduce_weight],
    )
    expand_full, reduce_full = (whole.reshape(halves, width, -1) for whole in wholes[2:])
    columns = feed_width(halves)
    steps = hidden // halves // columns
    outputs, result_grad, result_b, result_turned, reduce_bias_grad, loss = feed(
        mine, count.reshape(1), activ, hidden_state, reduce_full, line(reduce_bias), teacher
    )
    reduce_grad, expand_grad, expand_bias_grad, hidden_grad, hidden_b, hidden_turned, second_sums = feed_back(
        result_b, result_turned, second_turned, expand_full, reduce_full, activ, slope, hidden_state,
        result_grad, line(second_gain),
    )
    merge_grad, heads_grad, inputs_grad, early, expand_sum, late, heads_sum = attend_back(
        mine, a_turned, hidden_b, hidden_turned, qkv, mixed, log_total, inputs, hidden_grad,
        line(first_gain), wholes[0], wholes[1], second_sums, reduce_bias_grad, loss, expand_bias_grad,
    )
    heads_sum = jnp.moveaxis(heads_sum.reshape(groups, halves, 3, PAIR), 0, 2)
    heads_sum = lax.dynamic_index_in_dim(heads_sum, tensor, 0, False).reshape(3, piece_width)
    expand_sum = jnp.moveaxis(expand_sum.reshape(steps, halves, columns), 0, 1)
    expand_sum = lax.dynamic_index_in_dim(expand_sum, tensor, 0, False).reshape(-1)
    return (
        early[4, 0] / count,
        outputs,
        inputs_grad,
        late[0],
        late[1],
        heads_grad,
        heads_sum[::2],
        merge_grad,
        early[2],
        early[0],
        early[1],
        expand_grad,
        expand_sum,
        reduce_grad,
        early[3],
    )


def solution(mesh):
    return jax.shard_map(
        body,
        mesh=mesh,
        in_specs=(
            P(("dp", "tensor"), None),
            P(("dp", "tensor"), None),
            P(),
            P(),
            P(),
            P(None, "dp", "tensor"),
            P(None, "tensor"),
            P("dp", "tensor"),
            P(),
            P(),
            P(),
            P("dp", "tensor"),
            P("tensor"),
            P("dp", "tensor"),
            P(),
        ),
        out_specs=(
            P(),
            P(("dp", "tensor"), None),
            P(("dp", "tensor"), None),
            P(),
            P(),
            P(None, "dp", "tensor"),
            P(None, "tensor"),
            P("dp", "tensor"),
            P(),
            P(),
            P(),
            P("dp", "tensor"),
            P("tensor"),
            P("dp", "tensor"),
            P(),
        ),
        check_vma=False,
    )
```

```python
from functools import partial
import math

import jax
import jax.numpy as jnp
import numpy as np
from jax import lax
from jax.experimental import pallas as pl
from jax.experimental.pallas import tpu as pltpu
from jax.sharding import PartitionSpec as P

HD = 64
SLOTS = 320
PAIR = 2 * HD
BLOCK = SLOTS // 2

EPSILON = 1e-05
MASKED_SCORE = -1e30
F32 = jnp.float32
BF16 = jnp.bfloat16
CORES = 2
LINE = 4


AXES = ("tensor", "line", "row", "core")
MESH = pl.DeviceIdType.MESH
GATHER_ORDERS = (("line", "tensor", "row", "core"), ("line", "row", "tensor", "core"))


def sizes():
    dp = lax.axis_size("dp")
    return {"tensor": lax.axis_size("tensor"), "line": LINE, "row": dp // (LINE * CORES), "core": CORES}


class Place:
    def __init__(self):
        self.size = sizes()
        index = lax.axis_index("dp")
        self.at = {
            "tensor": lax.axis_index("tensor"),
            "core": lax.rem(index, CORES),
            "row": lax.rem(lax.div(index, CORES), self.size["row"]),
            "line": lax.div(index, CORES * self.size["row"]),
        }

    def steps(self, axis):
        return range(1, self.size[axis])

    def peer(self, axis, step):
        return lax.rem(self.at[axis] + step, self.size[axis])

    def device(self, axis, place):
        at = {**self.at, axis: place}
        return {"dp": (at["line"] * self.size["row"] + at["row"]) * CORES + at["core"], "tensor": at["tensor"]}

    def greet(self):
        barrier = pltpu.get_barrier_semaphore()
        count = 0
        for axis in AXES:
            for step in self.steps(axis):
                pl.semaphore_signal(
                    barrier, inc=1, device_id=self.device(axis, self.peer(axis, step)), device_id_type=MESH
                )
                count += 1
        pl.semaphore_wait(barrier, count)


def pieces_of(shards, width):
    out = []
    for a, shard in enumerate(shards):
        for lead in range(shard.shape[0]) if len(shard.shape) == 3 else (None,):
            for col in range(shard.shape[-1] // width):
                out.append((a, lead, col))
    return out


def piece(refs, which, width):
    a, lead, col = which
    ref = refs[a] if lead is None else refs[a].at[lead]
    spare = (slice(None),) * (len(ref.shape) - 1)
    return ref.at[(*spare, pl.ds(col * width, width))]


def whole_shape(weight):
    size = sizes()
    return (*weight.shape[:-2], *(size[a] for a in AXES), *weight.shape[-2:])


class Gather:
    def __init__(self, pieces, width, offsets, ins, outs, sems):
        self.here = Place()
        self.pieces, self.width, self.offsets, self.ins, self.outs = pieces, width, offsets, ins, outs
        self.send_sem, self.recv_sem, self.own_sem = sems
        self.half = ins[0].shape[-2] // 2
        self.count = len(pieces)

    def region(self, n, h, stage, axis=None, place=None):
        order = GATHER_ORDERS[h]
        index = [
            slice(None) if a in order[:stage] else place if a == axis else self.here.at[a] for a in AXES
        ]
        return piece(self.outs, self.pieces[n], self.width).at[(*index, pl.ds(h * self.half, self.half))]

    def remote(self, n, h, stage, step, coming=False):
        here, axis = self.here, GATHER_ORDERS[h][stage]
        slot = (n, h, stage, step - 1)
        to = source = self.region(n, h, stage)
        if stage == 0:
            source = piece(self.ins, self.pieces[n], self.width).at[pl.ds(h * self.half, self.half)]
        if coming:
            to = self.region(n, h, stage, axis, here.peer(axis, here.size[axis] - step))
        return pltpu.make_async_remote_copy(
            src_ref=source, dst_ref=to, send_sem=self.send_sem.at[slot], recv_sem=self.recv_sem.at[slot],
            device_id=here.device(axis, here.peer(axis, step)), device_id_type=MESH,
        )

    def every(self, n, stage):
        return [(n, h, stage, step) for h in range(2) for step in self.here.steps(GATHER_ORDERS[h][stage])]

    def start(self, n, stage):
        for slot in self.every(n, stage):
            self.remote(*slot).start()

    def arrived(self, n, stage=3):
        for slot in self.every(n, stage):
            self.remote(*slot, coming=True).wait_recv()

    def own(self, n):
        place = tuple(self.here.at[a] for a in AXES)
        return pltpu.make_async_copy(
            piece(self.ins, self.pieces[n], self.width),
            piece(self.outs, self.pieces[n], self.width).at[place], self.own_sem.at[n],
        )

    def begin(self):
        self.here.greet()
        for n in range(self.count):
            self.start(n, 0)
            self.own(n).start()

    def ticks(self):
        return self.count + self.offsets[-1]

    def tick(self, k):
        for stage, offset in enumerate(self.offsets, 1):
            n = k - offset
            if 0 <= n < self.count:
                if stage == 1:
                    self.own(n).wait()
                self.arrived(n, stage - 1)
                self.start(n, stage)

    def end(self):
        for n in range(self.count):
            for stage in range(4):
                for slot in self.every(n, stage):
                    self.remote(*slot).wait_send()


class Share:
    def __init__(self, here, source, target, sems):
        self.here, self.source, self.target = here, source, target
        self.send_sem, self.recv_sem, self.own_sem = sems

    def remote(self, step, coming=False):
        here = self.here
        place = here.peer("tensor", here.size["tensor"] - step) if coming else here.at["tensor"]
        return pltpu.make_async_remote_copy(
            src_ref=self.source, dst_ref=self.target.at[place],
            send_sem=self.send_sem.at[step - 1], recv_sem=self.recv_sem.at[step - 1],
            device_id=here.device("tensor", here.peer("tensor", step)), device_id_type=MESH,
        )

    def own(self):
        return pltpu.make_async_copy(self.source, self.target.at[self.here.at["tensor"]], self.own_sem)

    def begin(self):
        self.own().start()
        for step in self.here.steps("tensor"):
            self.remote(step).start()

    def arrived(self):
        self.own().wait()
        for step in self.here.steps("tensor"):
            self.remote(step, coming=True).wait_recv()

    def end(self):
        for step in self.here.steps("tensor"):
            self.remote(step).wait_send()


SCATTER_ORDERS = (("tensor", "row", "line"), ("row", "tensor", "line"))
THREE = AXES[:3]


def late_shapes(count, rows, columns):
    size, out = sizes(), []
    for order in SCATTER_ORDERS:
        for stage in (1, 2, 3):
            free = [size[a] for a in THREE if a not in order[:stage]]
            out.append((count, size[order[stage - 1]] - 1, *free, rows // 2, columns))
    return out


def scatter_scratch(count, rows, columns):
    size = sizes()
    most = max(size.values()) - 1
    half_piece = (count, *(size[a] for a in THREE), rows, columns)
    return [
        pltpu.VMEM(half_piece, BF16),
        pltpu.VMEM(half_piece, BF16),
        *[pltpu.VMEM(dims, BF16) for dims in late_shapes(count, rows, columns)],
        pltpu.SemaphoreType.DMA((count, 2, 4, most)),
        pltpu.SemaphoreType.DMA((count, 2, 4, most)),
    ]


SCATTER_REFS = 10


def plus(terms):
    if len(terms) == 2:
        return terms[0] + terms[1]
    return sum(term.astype(F32) for term in terms).astype(BF16)


class Scatter:
    def __init__(self, here, staging, out, refs):
        self.here, self.staging, self.out = here, staging, out
        self.own, self.first, *late, self.send_sem, self.recv_sem = refs
        self.late = {(h, s): late[h * 3 + s - 1] for h in range(2) for s in (1, 2, 3)}
        self.half = self.own.shape[-2] // 2

    def to_core(self, n):
        here = self.here
        other = here.peer("core", 1)
        return pltpu.make_async_remote_copy(
            src_ref=self.staging(n).at[:, :, :, other], dst_ref=self.first.at[n],
            send_sem=self.send_sem.at[n, 0, 0, 0], recv_sem=self.recv_sem.at[n, 0, 0, 0],
            device_id=here.device("core", other), device_id_type=MESH,
        )

    def remote(self, n, h, stage, step):
        here, order = self.here, SCATTER_ORDERS[h]
        axis = order[stage - 1]
        to = here.peer(axis, step)
        index = [
            here.at[a] if a in order[: stage - 1] else to if a == axis else slice(None) for a in THREE
        ]
        slot = (n, h, stage, step - 1)
        return pltpu.make_async_remote_copy(
            src_ref=self.own.at[(n, *index, pl.ds(h * self.half, self.half))],
            dst_ref=self.late[h, stage].at[n, step - 1],
            send_sem=self.send_sem.at[slot], recv_sem=self.recv_sem.at[slot],
            device_id=here.device(axis, to), device_id_type=MESH,
        )

    def every(self, n, stage):
        return [
            self.remote(n, h, stage, step)
            for h in range(2)
            for step in self.here.steps(SCATTER_ORDERS[h][stage - 1])
        ]

    def add_core(self, n):
        source, core = self.staging(n), self.here.at["core"]
        for at in np.ndindex(self.own.shape[1:3]):
            self.own[(n, *at)] = plus([source[(*at, slice(None), core)], self.first[(n, *at)]])

    def add(self, n, h, stage):
        here, order = self.here, SCATTER_ORDERS[h]
        buf, steps = self.late[h, stage], here.size[order[stage - 1]] - 1
        free = [a for a in THREE if a not in order[:stage]]
        rows = pl.ds(h * self.half, self.half)
        for free_at in np.ndindex(*(here.size[a] for a in free)):
            at = {**here.at, **dict(zip(free, free_at, strict=True))}
            mine = (n, *(at[a] for a in THREE), rows)
            terms = [self.own[mine]] + [buf[(n, s, *free_at)] for s in range(steps)]
            if stage == 3:
                self.out(n)[rows, :] = sum(term.astype(F32) for term in terms)
            else:
                self.own[mine] = plus(terms)

    def begin(self, n):
        self.to_core(n).start()

    def tick(self, n, stage):
        if stage == 0:
            copy = self.to_core(n)
            copy.wait_recv()
            copy.wait_send()
            self.add_core(n)
        else:
            for copy in self.every(n, stage):
                copy.wait_recv()
            for h in range(2):
                self.add(n, h, stage)
        if stage < 3:
            for copy in self.every(n, stage + 1):
                copy.start()

    def end(self, count):
        def one(n, _):
            for stage in (1, 2, 3):
                for copy in self.every(n, stage):
                    copy.wait_send()
            return 0

        lax.fori_loop(0, count, one, 0)


SUM_AXES = ("core", "tensor", "row", "line")


class SmallSum:
    def __init__(self, here, refs):
        self.here = here
        *self.bufs, self.send_sem, self.recv_sem = refs

    @staticmethod
    def scratch(dims):
        size = sizes()
        most = max(size.values()) - 1
        return [
            *[pltpu.VMEM((size[a], *dims), F32) for a in SUM_AXES],
            pltpu.SemaphoreType.DMA((4, most)),
            pltpu.SemaphoreType.DMA((4, most)),
        ]

    def remote(self, stage, step, coming=False):
        here, axis, buf = self.here, SUM_AXES[stage], self.bufs[stage]
        place = here.peer(axis, here.size[axis] - step) if coming else here.at[axis]
        return pltpu.make_async_remote_copy(
            src_ref=buf.at[here.at[axis]], dst_ref=buf.at[place],
            send_sem=self.send_sem.at[stage, step - 1], recv_sem=self.recv_sem.at[stage, step - 1],
            device_id=here.device(axis, here.peer(axis, step)), device_id_type=MESH,
        )

    def start(self, stage, value):
        self.bufs[stage][self.here.at[SUM_AXES[stage]]] = value
        self.send(stage)

    def send(self, stage):
        for step in self.here.steps(SUM_AXES[stage]):
            self.remote(stage, step).start()

    def finish(self, stage):
        axis = SUM_AXES[stage]
        for step in self.here.steps(axis):
            self.remote(stage, step, coming=True).wait_recv()
            self.remote(stage, step).wait_send()
        total = self.bufs[stage][0]
        for place in range(1, self.here.size[axis]):
            total += self.bufs[stage][place]
        return total

    def tick(self, stage, target):
        total = self.finish(stage)
        if stage < 3:
            self.start(stage + 1, total)
        else:
            target[...] = total


SMALL_REFS = 6


def dot(left, right, left_dim=1, right_dim=0):
    return lax.dot_general(
        left, right, (((left_dim,), (right_dim,)), ((), ())), preferred_element_type=F32
    )


def side_by_side(ref, *lead):
    return jnp.concatenate([ref[(*lead, t)] for t in range(ref.shape[-3])], axis=-1)


def centred(rows):
    off = rows - jnp.mean(rows, axis=-1, keepdims=True)
    inverse = lax.rsqrt(jnp.mean(off * off, axis=-1, keepdims=True) + EPSILON)
    return off * inverse, inverse


def norm_back(grad, hat, inverse, gain):
    scaled = grad * gain
    along = jnp.mean(scaled * hat, axis=-1, keepdims=True)
    return inverse * (scaled - jnp.mean(scaled, axis=-1, keepdims=True) - hat * along)


def fold(rows):
    return jnp.sum(rows.reshape(-1, 8, rows.shape[-1]), axis=0)


def row_blocks(rows, size, one):
    def step(i, _):
        one(i, pl.ds(pl.multiple_of(i * size, size), size))
        return 0

    lax.fori_loop(0, rows // size, step, 0)


def transpose_into(source, target):
    rows = source.shape[0]
    for first in range(0, rows, 128):
        size = min(128, rows - first)
        target[:, first : first + size] = source[first : first + size, :].astype(F32).T.astype(BF16)


def two_heads(pair):
    first = lax.broadcasted_iota(jnp.int32, pair.shape, 1) < HD
    zero = jnp.zeros_like(pair)
    return jnp.concatenate([jnp.where(first, pair, zero), jnp.where(first, zero, pair)], axis=0)


def one_pair(stacked):
    first = lax.broadcasted_iota(jnp.int32, (SLOTS, PAIR), 1) < HD
    return jnp.where(first, stacked[:SLOTS], stacked[SLOTS:])


def masked_scores(query_stack, keys, length):
    scores = dot(keys, query_stack, 1, 1)
    slot = lax.broadcasted_iota(jnp.int32, scores.shape, 0)
    return jnp.where(slot < length, scores, MASKED_SCORE)


def group_weight(qkv_held, columns):
    parts = [qkv_held[e, t, ..., columns] for t in range(qkv_held.shape[1]) for e in range(3)]
    return jnp.concatenate([part.reshape(-1, PAIR) for part in parts], axis=-1)


def merge_tile(merge_held, columns):
    parts = [merge_held[t, ..., columns] for t in range(merge_held.shape[0])]
    return jnp.concatenate([part.reshape(-1, PAIR) for part in parts], axis=-1)


def schedule(ticks, last_piece, needed, steps):
    at = []
    first = needed.index(next(s for s in needed if s > 0), 0) if any(needed) else len(needed)
    early = first + last_piece
    for k in range(ticks):
        piece_done = k - last_piece
        even = 0 if k < early else 1 + (k - early) * (steps - 1) // (ticks - early)
        at.append(min(even, needed[max(piece_done, 0)]))
    for k in range(ticks - 2, -1, -1):
        at[k] = min(at[k], at[k + 1])
    return at


def forward_pieces(parts, width):
    pieces = pieces_of(parts, width)
    return sorted(pieces, key=lambda which: (max(which[0], 0) if which[0] < 2 else 2, which[2], which[0]))


def forward_kernel(
    width_of_piece, offsets, feed_columns,
    lengths, count, x_ref, teacher, gain, shift, merge_bias, gain_2, shift_2, reduce_bias,
    heads_bias, expand_bias, qkv_part, merge_part, expand_part, reduce_part,
    a_turned, qkv_ref, mixed_ref, log_ref, second_turned, activ, slope,
    out, grad_b, grad_turned, bias_grad, loss,
    hidden, grad, qkv_full, merge_full, expand_full, reduce_full,
    hidden_ref, second_ref, a_ref, qkv_held, merge_held, tiles, heads_bias_all, expand_bias_all,
    send_sem, recv_sem, own_sem, share_send, share_recv, share_own, held_sem, tile_sem, keep_sem,
):
    now = pl.program_id(0)
    rows = x_ref.shape[0]
    images = rows // SLOTS
    halves = qkv_held.shape[1]
    groups = width_of_piece // PAIR
    attention_steps = groups * images
    feed_steps = expand_part.shape[1] // feed_columns
    steps = attention_steps + feed_steps
    parts = [qkv_part, merge_part, expand_part, reduce_part]
    pieces = forward_pieces(parts, width_of_piece)
    gather = Gather(
        pieces, width_of_piece, offsets, parts, [qkv_full, merge_full, expand_full, reduce_full],
        (send_sem, recv_sem, own_sem),
    )
    shares = [
        Share(gather.here, source, target, (share_send.at[n], share_recv.at[n], share_own.at[n]))
        for n, (source, target) in enumerate([(heads_bias, heads_bias_all), (expand_bias, expand_bias_all)])
    ]
    tiles_of_piece = width_of_piece // feed_columns
    needed = [
        0 if a == 0 else images - 1 if a == 1 else max(attention_steps + col * tiles_of_piece - 1, 0)
        for a, _, col in pieces
    ]
    when = schedule(gather.ticks(), offsets[-1], needed, steps)
    image = lax.rem(now, images)
    group = lax.min(lax.div(now, images), groups - 1)
    columns = pl.ds(pl.multiple_of(group * PAIR, PAIR), PAIR)

    def hold(n):
        a, lead, _ = pieces[n]
        source, target = (qkv_full.at[lead], qkv_held.at[lead]) if a == 0 else (merge_full, merge_held)
        return pltpu.make_async_copy(source, target, held_sem.at[n])

    def tile_copies(j):
        block = pl.ds(j * feed_columns, feed_columns)
        return [
            pltpu.make_async_copy(
                full.at[:, :, :, :, :, block], tiles.at[j % 2, kind], tile_sem.at[j % 2, kind]
            )
            for kind, full in enumerate((expand_full, reduce_full))
        ]

    def fetch_tiles(j):
        for kind, copy in enumerate(tile_copies(j)):
            if j % tiles_of_piece == 0:
                gather.arrived(4 + 2 * (j // tiles_of_piece) + kind)
            copy.start()

    def keep_hidden():
        return pltpu.make_async_copy(hidden_ref, hidden, keep_sem)

    @pl.when(now == 0)
    def _():
        gather.begin()
        for share in shares:
            share.begin()
        early = [k for k in range(gather.ticks()) if when[k] == 0]
        blocks = rows // BLOCK
        per = -(-blocks // max(len(early), 1))

        def norm(i, _):
            at = pl.ds(pl.multiple_of(i * BLOCK, BLOCK), BLOCK)
            x = x_ref[at, :].astype(F32)
            hidden_ref[at, :] = x + merge_bias[...]
            a_ref[at, :] = (centred(x)[0] * gain[...] + shift[...]).astype(BF16)
            return 0

        done = 0
        for k in early:
            lax.fori_loop(done, min(done + per, blocks), norm, 0)
            done = min(done + per, blocks)
            gather.tick(k)
            n = k - offsets[-1] - 1
            if 0 <= n < 3:
                gather.arrived(n)
                hold(n).start()
        lax.fori_loop(done, blocks, norm, 0)
        transpose_into(a_ref, a_turned)
        for n in range(max(len(early) - offsets[-1] - 1, 0), 3):
            gather.arrived(n)
            hold(n).start()
        for share in shares:
            share.arrived()
        for n in range(3):
            hold(n).wait()

    for k in range(gather.ticks()):
        if when[k] > 0:
            pl.when(now == when[k])(partial(gather.tick, k))

    @pl.when((now < attention_steps) & (image == 0))
    def _():
        weight = group_weight(qkv_held, columns)
        bias = []
        for t in range(halves):
            query = heads_bias_all[t, 0:1, columns]
            bias += [query, jnp.zeros_like(query), heads_bias_all[t, 1:2, columns]]
        bias = jnp.concatenate(bias, axis=-1)
        for i in range(images):
            at = slice(i * SLOTS, (i + 1) * SLOTS)
            out = (dot(a_ref[at, :], weight) + bias).astype(BF16)
            for t in range(halves):
                query = slice(t * 3 * PAIR, (t * 3 + 1) * PAIR)
                qkv_ref[0, at, query] = out[:, query] * 0.125
                rest = slice((t * 3 + 1) * PAIR, (t * 3 + 3) * PAIR)
                qkv_ref[0, at, rest] = out[:, rest]

    @pl.when(now < attention_steps)
    def _():
        length = lengths[image]
        at = pl.ds(pl.multiple_of(image * SLOTS, SLOTS), SLOTS)
        for t in range(halves):
            first = t * 3 * PAIR
            query_stack = two_heads(qkv_ref[0, at, first : first + PAIR])
            scores = masked_scores(query_stack, qkv_ref[0, at, first + PAIR : first + 2 * PAIR], length)
            highest = jnp.max(scores, axis=0, keepdims=True)
            expo = jnp.exp(scores - highest)
            totals = jnp.sum(expo, axis=0, keepdims=True)
            values = qkv_ref[0, at, first + 2 * PAIR : first + 3 * PAIR]
            mixed = dot(values, expo.astype(BF16), 0, 0) * (1.0 / totals)
            mixed_ref[0, at, t * PAIR : (t + 1) * PAIR] = one_pair(mixed.T).astype(BF16)
            log_ref[0, 0, t : t + 1] = highest + jnp.log(totals)

    @pl.when(now == images - 1)
    def _():
        gather.arrived(3)
        hold(3).start()
        hold(3).wait()

    @pl.when((now < attention_steps) & (image == images - 1))
    def _():
        weight = merge_tile(merge_held, columns)
        for i in range(images):
            part = slice(i * SLOTS, (i + 1) * SLOTS)
            hidden_ref[part, :] += dot(mixed_ref[0, part, :], weight, 1, 1)

    @pl.when(now == attention_steps - 1)
    def _():
        keep_hidden().start()
        fetch_tiles(0)

        def norm(_, at):
            hat, _ = centred(hidden_ref[at, :])
            second_ref[at, :] = (hat * gain_2[...] + shift_2[...]).astype(BF16)

        row_blocks(rows, BLOCK, norm)
        transpose_into(second_ref, second_turned)

    for j in range(feed_steps):

        @pl.when(now == attention_steps + j)
        def _(j=j):
            if j == 0:
                keep_hidden().wait()
            for copy in tile_copies(j):
                copy.wait()
            if j + 1 < feed_steps:
                fetch_tiles(j + 1)

    @pl.when(now >= attention_steps)
    def _():
        j = now - attention_steps
        block = pl.ds(pl.multiple_of(j * feed_columns, feed_columns), feed_columns)
        slot = lax.rem(j, 2)
        weight, reduce_tile = (
            jnp.concatenate([tiles[slot, kind, t].reshape(-1, feed_columns) for t in range(halves)], axis=-1)
            for kind in range(2)
        )
        bias = jnp.concatenate([expand_bias_all[t, :, block] for t in range(halves)], axis=-1)
        for i in range(images):
            at = slice(i * SLOTS, (i + 1) * SLOTS)
            z = dot(second_ref[at, :], weight) + bias
            square = z * z
            bend = jnp.tanh(0.7978845608 * z * (1.0 + 0.044715 * square))
            half = 0.5 + 0.5 * bend
            act = (z * half).astype(BF16)
            activ[0, at, :] = act
            inner = 0.7978845608 * z * (1.0 + (3 * 0.044715) * square)
            slope[0, at, :] = (half + 0.5 * inner * (1.0 - bend * bend)).astype(BF16)
            hidden_ref[at, :] += dot(act, reduce_tile, 1, 1)

    @pl.when(now == steps - 1)
    def _():
        bias_grad[...] = jnp.zeros_like(bias_grad)
        loss[...] = jnp.zeros_like(loss)

        def end(i, at):
            image, block = lax.div(i, SLOTS // BLOCK), lax.rem(i, SLOTS // BLOCK)
            slot = block * BLOCK + lax.broadcasted_iota(jnp.int32, (BLOCK, 1), 0)
            valid = slot < lengths[image]
            result = jnp.where(valid, hidden_ref[at, :] + reduce_bias[...], 0.0)
            out[at, :] = result.astype(BF16)
            error = jnp.where(valid, result - teacher[at, :].astype(F32), 0.0)
            loss[0] += fold(error * error)
            back = 2.0 * error / count[0]
            bias_grad[0] += fold(back)
            hidden_ref[at, :] = back
            grad_b[at, :] = back.astype(BF16)

        row_blocks(rows, BLOCK, end)
        keep = pltpu.make_async_copy(hidden_ref, grad, keep_sem)
        keep.start()
        transpose_into(grad_b, grad_turned)
        keep.wait()
        gather.end()
        for share in shares:
            share.end()


def feed_back_kernel(
    result_b, result_turned, second_turned, expand, reduce, activ, slope, hidden, result_grad, gain,
    reduce_grad, expand_grad, expand_bias_grad, hidden_grad, hidden_b, hidden_turned, sums,
    total, staging, *scatter_refs,
):
    step, steps = pl.program_id(0), reduce_grad.shape[1] // expand.shape[-1]
    rows, width = result_b.shape
    halves, _, columns = expand.shape
    expand_tile, reduce_tile = side_by_side(expand), side_by_side(reduce)

    scatters = []
    here = Place()
    for p, target in enumerate((reduce_grad, expand_grad)):
        slot = lambda j, p=p: staging.at[lax.rem(j, 2), p]
        part = lambda j, target=target: target.at[:, pl.ds(pl.multiple_of(j * columns, columns), columns)]
        scatters.append(Scatter(here, slot, part, scatter_refs[p * SCATTER_REFS : (p + 1) * SCATTER_REFS]))

    @pl.when(step == 0)
    def _():
        here.greet()
        total[...] = jnp.zeros_like(total)

    def ticks(p, back):
        for stage in range(3, -1, -1):

            @pl.when(step >= stage + back)
            def _(stage=stage):
                scatters[p].tick(step - back - stage, stage)

    def stage_out(p, part):
        for t in range(halves):
            block = part[:, t * columns : (t + 1) * columns].astype(BF16)
            staging[lax.rem(step, 2), p, t] = block.reshape(staging.shape[3:])
        scatters[p].begin(step)

    stage_out(0, dot(result_turned[...], activ[0]))
    ticks(1, 1)
    bias = jnp.zeros((8, halves * columns), F32)
    parts = []
    for i in range(rows // SLOTS):
        at = slice(i * SLOTS, (i + 1) * SLOTS)
        z_grad = (dot(result_b[at, :], reduce_tile) * slope[0, at, :].astype(F32)).astype(BF16)
        bias += fold(z_grad.astype(F32))
        parts.append(z_grad)
        total[at, :] += dot(z_grad, expand_tile, 1, 1)
    expand_bias_grad[0] = jnp.sum(bias, axis=0, keepdims=True)
    ticks(0, 0)
    stage_out(1, dot(second_turned[...], jnp.concatenate(parts, axis=0)))

    @pl.when(step == steps - 1)
    def _():
        sums[...] = jnp.zeros_like(sums)
        size = 128 if rows % 128 == 0 else rows
        blocks = rows // size

        def end(first, h_ref, g_ref, back_ref, back_b_ref, turned_ref):
            block = pl.program_id(0) + first
            for k in range(0, size, 32):
                at = slice(k, k + 32)
                hat, inverse = centred(h_ref[at, :])
                second_grad = total[pl.ds(pl.multiple_of(block * size + k, 32), 32), :]
                back = g_ref[at, :] + norm_back(second_grad, hat, inverse, gain[...])
                sums[0] += fold(second_grad * hat)
                sums[1] += fold(second_grad)
                sums[2] += fold(back)
                back_ref[at, :] = back
                back_b_ref[at, :] = back.astype(BF16)
            turned_ref[...] = back_ref[...].T.astype(BF16)

        def some(first, last):
            row_block = pl.BlockSpec((size, width), lambda i: (i + first, 0))
            pltpu.emit_pipeline(
                partial(end, first),
                grid=(last - first,),
                in_specs=[row_block, row_block],
                out_specs=[row_block, row_block, pl.BlockSpec((width, size), lambda i: (0, i + first))],
            )(hidden, result_grad, hidden_grad, hidden_b, hidden_turned)

        bounds = [blocks * k // 3 for k in range(4)]
        for drain in range(4):
            for stage in range(3, -1, -1):
                for p, first in ((0, drain + 1), (1, drain)):
                    n = steps + first - 1 - stage
                    if stage >= first and n >= 0:
                        scatters[p].tick(n, stage)
            if drain < 3 and bounds[drain + 1] > bounds[drain]:
                some(bounds[drain], bounds[drain + 1])
        for scatter in scatters:
            scatter.end(steps)


def attend_back_kernel(
    lengths, a_turned, hidden_b, hidden_turned, qkv_ref, mixed_ref, log_ref, x_ref, hidden_grad, gain,
    qkv_weight, merge_weight, second_sums, reduce_bias_grad, loss, expand_bias_grad,
    merge_grad, qkv_grad, inputs_grad, early_out, expand_out, late_out, heads_out,
    mixed_grad, heads_grad, total, qkv_held, merge_held, sem, merge_staging, qkv_staging, sums, bias_grad,
    *comm,
):
    now = pl.program_id(0)
    rows = x_ref.shape[0]
    images = rows // SLOTS
    halves = qkv_held.shape[1]
    groups = merge_grad.shape[1] // PAIR
    steps = groups * images
    group, image = lax.div(now, images), lax.rem(now, images)
    here = Place()
    block = lambda c: pl.ds(pl.multiple_of(c * PAIR, PAIR), PAIR)
    merge_scatter = Scatter(here, lambda n: merge_staging, lambda n: merge_grad.at[:, block(n)], comm[:SCATTER_REFS])
    qkv_scatter = Scatter(
        here, lambda n: qkv_staging.at[lax.rem(n, 3)],
        lambda n: qkv_grad.at[lax.rem(n, 3), :, block(lax.div(n, 3))], comm[SCATTER_REFS : 2 * SCATTER_REFS],
    )
    early, expand_sum, late, heads_sum = (
        SmallSum(here, comm[2 * SCATTER_REFS + k * SMALL_REFS :][:SMALL_REFS]) for k in range(4)
    )

    def qkv_tick(c, stage):
        for e in range(3):
            qkv_scatter.tick(3 * c + e, stage)
    columns = pl.ds(pl.multiple_of(group * PAIR, PAIR), PAIR)

    @pl.when(now == 0)
    def _():
        copies = [
            pltpu.make_async_copy(merge_weight, merge_held, sem.at[1]),
            pltpu.make_async_copy(qkv_weight, qkv_held, sem.at[0]),
        ]
        for copy in copies:
            copy.start()
        here.greet()
        total[...] = jnp.zeros_like(total)
        rowsum = lambda ref, k: jnp.sum(ref[k], axis=0, keepdims=True)
        vectors = [rowsum(second_sums, k) for k in range(3)] + [rowsum(reduce_bias_grad, 0)]
        lost = jnp.sum(rowsum(loss, 0), axis=1, keepdims=True)
        vectors.append(jnp.broadcast_to(lost, vectors[0].shape))
        early.start(0, jnp.concatenate(vectors, axis=0))
        expand_sum.start(0, expand_bias_grad[:, 0])
        for copy in copies:
            copy.wait()

    @pl.when(image == 0)
    def _():
        weight = merge_tile(merge_held, columns)
        for i in range(rows // SLOTS):
            part = slice(i * SLOTS, (i + 1) * SLOTS)
            mixed_grad[part, :] = dot(hidden_b[part, :], weight).astype(BF16)
        part = dot(hidden_turned[...], mixed_ref[0]).astype(BF16)
        for t in range(halves):
            merge_staging[t] = part[:, t * PAIR : (t + 1) * PAIR].reshape(merge_staging.shape[1:])
        merge_scatter.begin(group)

        @pl.when(group == 0)
        def _():
            early.tick(0, early_out)
            expand_sum.tick(0, expand_out)

        @pl.when(group > 0)
        def _():
            merge_scatter.tick(group - 1, 2)
            qkv_tick(group - 1, 1)

    length = lengths[image]
    at = pl.ds(pl.multiple_of(image * SLOTS, SLOTS), SLOTS)
    for t in range(halves):
        first = t * 3 * PAIR
        query_stack = two_heads(qkv_ref[0, at, first : first + PAIR])
        keys = qkv_ref[0, at, first + PAIR : first + 2 * PAIR]
        values = qkv_ref[0, at, first + 2 * PAIR : first + 3 * PAIR]
        scores = masked_scores(query_stack, keys, length)
        attend = jnp.exp(scores - log_ref[0, 0, t : t + 1])
        grad_stack = two_heads(mixed_grad[at, t * PAIR : (t + 1) * PAIR])
        attend_grad = dot(values, grad_stack, 1, 1)
        value_grad = dot(attend.astype(BF16), grad_stack).astype(BF16)
        centre = jnp.sum(attend * attend_grad, axis=0, keepdims=True)
        score_grad = (attend * (attend_grad - centre)).astype(BF16)
        key_grad = dot(score_grad, query_stack).astype(BF16)
        query_grad = dot(keys, score_grad, 0, 0)
        query_grad = (one_pair(query_grad.T) * 0.125).astype(BF16)
        heads_grad[at, first : first + PAIR] = query_grad
        heads_grad[at, first + PAIR : first + 2 * PAIR] = key_grad
        heads_grad[at, first + 2 * PAIR : first + 3 * PAIR] = value_grad

    @pl.when(image == images - 1)
    def _():
        @pl.when(group == 0)
        def _():
            early.tick(1, early_out)
            expand_sum.tick(1, expand_out)

        @pl.when(group > 0)
        def _():
            merge_scatter.tick(group - 1, 3)
            qkv_tick(group - 1, 2)

        merge_scatter.tick(group, 0)
        weight = group_weight(qkv_held, columns)
        bias = jnp.zeros((8, halves * 3 * PAIR), F32)
        for i in range(rows // SLOTS):
            part = slice(i * SLOTS, (i + 1) * SLOTS)
            bias += fold(heads_grad[part, :].astype(F32))
        bias_grad[pl.ds(group, 1), :] = jnp.sum(bias, axis=0, keepdims=True)
        part = dot(a_turned[...], heads_grad[...]).astype(BF16)
        for t in range(halves):
            for e in range(3):
                first = (t * 3 + e) * PAIR
                qkv_staging[e, t] = part[:, first : first + PAIR].reshape(qkv_staging.shape[2:])
        for e in range(3):
            qkv_scatter.begin(3 * group + e)
        for i in range(rows // SLOTS):
            part = slice(i * SLOTS, (i + 1) * SLOTS)
            total[part, :] += dot(heads_grad[part, :], weight, 1, 1)

        @pl.when(group == 0)
        def _():
            early.tick(2, early_out)
            expand_sum.tick(2, expand_out)

        @pl.when(group > 0)
        def _():
            qkv_tick(group - 1, 3)

        merge_scatter.tick(group, 1)
        qkv_tick(group, 0)

    @pl.when(now == steps - 1)
    def _():
        heads_sum.start(0, bias_grad[...])
        sums[...] = jnp.zeros_like(sums)

        def end(i, _):
            at = pl.ds(pl.multiple_of(i * BLOCK, BLOCK), BLOCK)
            hat, inverse = centred(x_ref[at, :].astype(F32))
            grad = total[at, :]
            sums[0] += fold(grad * hat)
            sums[1] += fold(grad)
            inputs_grad[at, :] = hidden_grad[at, :] + norm_back(grad, hat, inverse, gain[...])
            return 0

        blocks = rows // BLOCK
        last = groups - 1
        lax.fori_loop(0, blocks // 2, end, 0)
        merge_scatter.tick(last, 2)
        qkv_tick(last, 1)
        early.tick(3, early_out)
        expand_sum.tick(3, expand_out)
        heads_sum.tick(0, heads_out)
        lax.fori_loop(blocks // 2, blocks, end, 0)
        late.start(0, jnp.sum(sums[...], axis=1))
        merge_scatter.tick(last, 3)
        qkv_tick(last, 2)
        heads_sum.tick(1, heads_out)
        late.tick(0, late_out)
        qkv_tick(last, 3)
        heads_sum.tick(2, heads_out)
        late.tick(1, late_out)
        heads_sum.tick(3, heads_out)
        late.tick(2, late_out)
        late.tick(3, late_out)
        merge_scatter.end(groups)
        qkv_scatter.end(3 * groups)


def shape(dims, kind=BF16):
    return jax.ShapeDtypeStruct(dims, kind)


def once(dims):
    return pl.BlockSpec(dims, lambda *_: (0,) * len(dims), pipeline_mode=pl.Buffered(1))


ELSEWHERE = pl.BlockSpec(memory_space=pl.ANY)
SCALARS = pl.BlockSpec(memory_space=pltpu.SMEM)
LIMIT = 63 * 2**20


OFFSETS = (0, 1, 2)


def feed_width(halves):
    return max(PAIR, 512 // halves)


def forward(
    lengths, count, x, teacher, gain, shift, merge_bias, gain_2, shift_2, reduce_bias, heads_bias, expand_bias, parts
):
    rows, width = x.shape
    halves, columns = lax.axis_size("tensor"), parts[0].shape[2]
    groups, images = columns // PAIR, rows // SLOTS
    attention_steps = groups * images
    feed_columns = feed_width(halves)
    feed_steps = parts[2].shape[1] // feed_columns
    pieces = len(pieces_of(parts, columns))
    most = max(sizes().values()) - 1
    line, whole, turned = once((1, width)), once((rows, width)), once((width, rows))
    group_at = lambda s: lax.min(lax.div(s, images), groups - 1)
    feed_at = lambda s: lax.max(s - attention_steps, 0)
    wholes = [whole_shape(part) for part in parts]
    saved = pl.BlockSpec((1, rows, halves * feed_columns), lambda s: (feed_at(s), 0, 0))
    return pl.pallas_call(
        partial(forward_kernel, columns, OFFSETS, feed_columns),
        grid=(attention_steps + feed_steps,),
        in_specs=[SCALARS, SCALARS, whole, whole, *[line] * 6, *[ELSEWHERE] * 6],
        out_specs=[
            turned,
            pl.BlockSpec((1, rows, halves * 3 * PAIR), lambda s: (group_at(s), 0, 0)),
            pl.BlockSpec((1, rows, halves * PAIR), lambda s: (group_at(s), 0, 0)),
            pl.BlockSpec(
                (1, 1, halves, 2 * SLOTS),
                lambda s: (group_at(s), jnp.where(s < attention_steps, lax.rem(s, images), images - 1), 0, 0),
            ),
            turned, saved, saved, whole, whole, turned, once((1, 8, width)), once((1, 8, width)),
            *[ELSEWHERE] * 6,
        ],
        out_shape=[
            shape((width, rows)),
            shape((groups, rows, halves * 3 * PAIR)),
            shape((groups, rows, halves * PAIR)),
            shape((groups, images, halves, 2 * SLOTS), F32),
            shape((width, rows)),
            *[shape((feed_steps, rows, halves * feed_columns))] * 2,
            shape((rows, width)), shape((rows, width)), shape((width, rows)),
            shape((1, 8, width), F32), shape((1, 8, width), F32),
            shape((rows, width), F32), shape((rows, width), F32),
            *[shape(dims) for dims in wholes],
        ],
        scratch_shapes=[
            pltpu.VMEM((rows, width), F32),
            pltpu.VMEM((rows, width), BF16),
            pltpu.VMEM((rows, width), BF16),
            pltpu.VMEM(wholes[0], BF16),
            pltpu.VMEM(wholes[1], BF16),
            pltpu.VMEM((2, 2, *wholes[2][:-1], feed_columns), BF16),
            pltpu.VMEM((halves, *heads_bias.shape), F32),
            pltpu.VMEM((halves, *expand_bias.shape), F32),
            pltpu.SemaphoreType.DMA((pieces, 2, 4, most)),
            pltpu.SemaphoreType.DMA((pieces, 2, 4, most)),
            pltpu.SemaphoreType.DMA((pieces,)),
            pltpu.SemaphoreType.DMA((2, halves)),
            pltpu.SemaphoreType.DMA((2, halves)),
            pltpu.SemaphoreType.DMA((2,)),
            pltpu.SemaphoreType.DMA((4,)),
            pltpu.SemaphoreType.DMA((2, 2)),
            pltpu.SemaphoreType.DMA(()),
        ],
        compiler_params=pltpu.CompilerParams(
            vmem_limit_bytes=LIMIT, collective_id=0, has_side_effects=True
        ),
        name="forward",
    )(
        lengths, count, x, teacher, gain, shift, merge_bias, gain_2, shift_2, reduce_bias,
        heads_bias, expand_bias, *parts,
    )


def feed_back(result_b, result_turned, second_turned, expand, reduce, activ, slope, hidden, result_grad, gain):
    rows, width = result_b.shape
    halves, _, wide = expand.shape
    steps, columns = activ.shape[0], activ.shape[2] // halves
    size = sizes()
    part_rows = width // math.prod(size[a] for a in ("line", "row", "core"))
    tile = pl.BlockSpec((halves, width, columns), lambda j: (0, 0, j))
    saved = pl.BlockSpec((1, rows, halves * columns), lambda j: (j, 0, 0))
    whole, turned, part = once((rows, width)), once((width, rows)), once((part_rows, wide))
    return pl.pallas_call(
        feed_back_kernel,
        grid=(steps,),
        in_specs=[whole, turned, turned, tile, tile, saved, saved, ELSEWHERE, ELSEWHERE, once((1, width))],
        out_specs=[
            part, part, pl.BlockSpec((1, 1, halves * columns), lambda j: (j, 0, 0)),
            ELSEWHERE, ELSEWHERE, ELSEWHERE, once((3, 8, width)),
        ],
        out_shape=[
            shape((part_rows, wide), F32), shape((part_rows, wide), F32),
            shape((steps, 1, halves * columns), F32),
            shape((rows, width), F32), shape((rows, width)), shape((width, rows)), shape((3, 8, width), F32),
        ],
        scratch_shapes=[
            pltpu.VMEM((rows, width), F32),
            pltpu.VMEM((2, 2, *(size[a] for a in AXES), part_rows, columns), BF16),
            *scatter_scratch(steps, part_rows, columns),
            *scatter_scratch(steps, part_rows, columns),
        ],
        compiler_params=pltpu.CompilerParams(
            vmem_limit_bytes=LIMIT, collective_id=1, has_side_effects=True
        ),
        name="feed_back",
    )(result_b, result_turned, second_turned, expand, reduce, activ, slope, hidden, result_grad, gain)


def attend_back(
    lengths, a_turned, hidden_b, hidden_turned, qkv, mixed, log_total, x, hidden_grad, gain,
    qkv_whole, merge_whole, second_sums, reduce_bias_grad, loss, expand_bias_grad,
):
    rows, width = x.shape
    halves, (part_rows, columns) = qkv_whole.shape[1], qkv_whole.shape[-2:]
    groups, images = columns // PAIR, rows // SLOTS
    whole, turned = once((rows, width)), once((width, rows))
    group_at = lambda s: lax.div(s, images)
    size = sizes()
    staging = (*(size[a] for a in AXES), part_rows, PAIR)
    small = [(5, width), (expand_bias_grad.shape[0], expand_bias_grad.shape[2]), (2, width), (groups, halves * 3 * PAIR)]
    vmem = lambda array: once(array.shape)
    return pl.pallas_call(
        attend_back_kernel,
        grid=(groups * images,),
        in_specs=[
            SCALARS, turned, whole, turned,
            pl.BlockSpec((1, rows, halves * 3 * PAIR), lambda s: (group_at(s), 0, 0)),
            pl.BlockSpec((1, rows, halves * PAIR), lambda s: (group_at(s), 0, 0)),
            pl.BlockSpec((1, 1, halves, 2 * SLOTS), lambda s: (group_at(s), lax.rem(s, images), 0, 0)),
            whole, whole, once((1, width)), ELSEWHERE, ELSEWHERE,
            vmem(second_sums), vmem(reduce_bias_grad), vmem(loss), vmem(expand_bias_grad),
        ],
        out_specs=[
            once((part_rows, columns)), once((3, part_rows, columns)), whole, *[once(dims) for dims in small]
        ],
        out_shape=[
            shape((part_rows, columns), F32), shape((3, part_rows, columns), F32), shape((rows, width), F32),
            *[shape(dims, F32) for dims in small],
        ],
        scratch_shapes=[
            pltpu.VMEM((rows, halves * PAIR), BF16),
            pltpu.VMEM((rows, halves * 3 * PAIR), BF16),
            pltpu.VMEM((rows, width), F32),
            pltpu.VMEM(qkv_whole.shape, BF16),
            pltpu.VMEM(merge_whole.shape, BF16),
            pltpu.SemaphoreType.DMA((2,)),
            pltpu.VMEM(staging, BF16),
            pltpu.VMEM((3, *staging), BF16),
            pltpu.VMEM((2, 8, width), F32),
            pltpu.VMEM((groups, halves * 3 * PAIR), F32),
            *scatter_scratch(groups, part_rows, PAIR),
            *scatter_scratch(3 * groups, part_rows, PAIR),
            *[ref for dims in small for ref in SmallSum.scratch(dims)],
        ],
        compiler_params=pltpu.CompilerParams(
            vmem_limit_bytes=LIMIT, collective_id=2, has_side_effects=True
        ),
        name="attend_back",
    )(
        lengths, a_turned, hidden_b, hidden_turned, qkv, mixed, log_total, x, hidden_grad, gain,
        qkv_whole, merge_whole, second_sums, reduce_bias_grad, loss, expand_bias_grad,
    )


def body(
    inputs,
    teacher,
    lengths,
    first_gain,
    first_shift,
    query_key_value_weight,
    heads_bias,
    merge_weight,
    merge_bias,
    second_gain,
    second_shift,
    expand_weight,
    expand_bias,
    reduce_weight,
    reduce_bias,
):
    rows, width = inputs.shape
    images = rows // SLOTS
    halves = lax.axis_size("tensor")
    tensor = lax.axis_index("tensor")
    hidden = expand_weight.shape[1] * halves
    piece_width = query_key_value_weight.shape[-1]
    groups = piece_width // PAIR
    place = lax.axis_index("dp") * halves + tensor
    mine = lax.dynamic_slice_in_dim(lengths, place * images, images)
    count = jnp.sum(lengths).astype(F32)
    line = lambda vector: vector.reshape(1, width)

    (
        a_turned, qkv, mixed, log_total, second_turned, activ, slope, outputs, result_b, result_turned,
        reduce_bias_grad, loss, hidden_state, result_grad, *wholes,
    ) = forward(
        mine, count.reshape(1), inputs, teacher, line(first_gain), line(first_shift), line(merge_bias),
        line(second_gain), line(second_shift), line(reduce_bias), heads_bias, expand_bias.reshape(1, -1),
        [query_key_value_weight, merge_weight, expand_weight, reduce_weight],
    )
    expand_full, reduce_full = (whole.reshape(halves, width, -1) for whole in wholes[2:])
    columns = feed_width(halves)
    steps = hidden // halves // columns
    reduce_grad, expand_grad, expand_bias_grad, hidden_grad, hidden_b, hidden_turned, second_sums = feed_back(
        result_b, result_turned, second_turned, expand_full, reduce_full, activ, slope, hidden_state,
        result_grad, line(second_gain),
    )
    merge_grad, heads_grad, inputs_grad, early, expand_sum, late, heads_sum = attend_back(
        mine, a_turned, hidden_b, hidden_turned, qkv, mixed, log_total, inputs, hidden_grad,
        line(first_gain), wholes[0], wholes[1], second_sums, reduce_bias_grad, loss, expand_bias_grad,
    )
    heads_sum = jnp.moveaxis(heads_sum.reshape(groups, halves, 3, PAIR), 0, 2)
    heads_sum = lax.dynamic_index_in_dim(heads_sum, tensor, 0, False).reshape(3, piece_width)
    expand_sum = jnp.moveaxis(expand_sum.reshape(steps, halves, columns), 0, 1)
    expand_sum = lax.dynamic_index_in_dim(expand_sum, tensor, 0, False).reshape(-1)
    return (
        early[4, 0] / count,
        outputs,
        inputs_grad,
        late[0],
        late[1],
        heads_grad,
        heads_sum[::2],
        merge_grad,
        early[2],
        early[0],
        early[1],
        expand_grad,
        expand_sum,
        reduce_grad,
        early[3],
    )


def solution(mesh):
    return jax.shard_map(
        body,
        mesh=mesh,
        in_specs=(
            P(("dp", "tensor"), None),
            P(("dp", "tensor"), None),
            P(),
            P(),
            P(),
            P(None, "dp", "tensor"),
            P(None, "tensor"),
            P("dp", "tensor"),
            P(),
            P(),
            P(),
            P("dp", "tensor"),
            P("tensor"),
            P("dp", "tensor"),
            P(),
        ),
        out_specs=(
            P(),
            P(("dp", "tensor"), None),
            P(("dp", "tensor"), None),
            P(),
            P(),
            P(None, "dp", "tensor"),
            P(None, "tensor"),
            P("dp", "tensor"),
            P(),
            P(),
            P(),
            P("dp", "tensor"),
            P("tensor"),
            P("dp", "tensor"),
            P(),
        ),
        check_vma=False,
    )
```

```python
from functools import partial
import math

import jax
import jax.numpy as jnp
import numpy as np
from jax import lax
from jax.experimental import pallas as pl
from jax.experimental.pallas import tpu as pltpu
from jax.sharding import PartitionSpec as P

HD = 64
SLOTS = 320
PAIR = 2 * HD
BLOCK = SLOTS // 2

EPSILON = 1e-05
MASKED_SCORE = -1e30
F32 = jnp.float32
BF16 = jnp.bfloat16
CORES = 2
LINE = 4


AXES = ("tensor", "line", "row", "core")
MESH = pl.DeviceIdType.MESH
GATHER_ORDERS = (("line", "tensor", "row", "core"), ("line", "row", "tensor", "core"))


def sizes():
    dp = lax.axis_size("dp")
    return {"tensor": lax.axis_size("tensor"), "line": LINE, "row": dp // (LINE * CORES), "core": CORES}


class Place:
    def __init__(self):
        self.size = sizes()
        index = lax.axis_index("dp")
        self.at = {
            "tensor": lax.axis_index("tensor"),
            "core": lax.rem(index, CORES),
            "row": lax.rem(lax.div(index, CORES), self.size["row"]),
            "line": lax.div(index, CORES * self.size["row"]),
        }

    def steps(self, axis):
        return range(1, self.size[axis])

    def peer(self, axis, step):
        return lax.rem(self.at[axis] + step, self.size[axis])

    def device(self, axis, place):
        at = {**self.at, axis: place}
        return {"dp": (at["line"] * self.size["row"] + at["row"]) * CORES + at["core"], "tensor": at["tensor"]}

    def greet(self):
        barrier = pltpu.get_barrier_semaphore()
        count = 0
        for axis in AXES:
            for step in self.steps(axis):
                pl.semaphore_signal(
                    barrier, inc=1, device_id=self.device(axis, self.peer(axis, step)), device_id_type=MESH
                )
                count += 1
        pl.semaphore_wait(barrier, count)


def pieces_of(shards, width):
    out = []
    for a, shard in enumerate(shards):
        for lead in range(shard.shape[0]) if len(shard.shape) == 3 else (None,):
            for col in range(shard.shape[-1] // width):
                out.append((a, lead, col))
    return out


def piece(refs, which, width):
    a, lead, col = which
    ref = refs[a] if lead is None else refs[a].at[lead]
    spare = (slice(None),) * (len(ref.shape) - 1)
    return ref.at[(*spare, pl.ds(col * width, width))]


def whole_shape(weight):
    size = sizes()
    return (*weight.shape[:-2], *(size[a] for a in AXES), *weight.shape[-2:])


class Gather:
    def __init__(self, pieces, width, offsets, ins, outs, sems):
        self.here = Place()
        self.pieces, self.width, self.offsets, self.ins, self.outs = pieces, width, offsets, ins, outs
        self.send_sem, self.recv_sem, self.own_sem = sems
        self.half = ins[0].shape[-2] // 2
        self.count = len(pieces)

    def region(self, n, h, stage, axis=None, place=None):
        order = GATHER_ORDERS[h]
        index = [
            slice(None) if a in order[:stage] else place if a == axis else self.here.at[a] for a in AXES
        ]
        return piece(self.outs, self.pieces[n], self.width).at[(*index, pl.ds(h * self.half, self.half))]

    def remote(self, n, h, stage, step, coming=False):
        here, axis = self.here, GATHER_ORDERS[h][stage]
        slot = (n, h, stage, step - 1)
        to = source = self.region(n, h, stage)
        if stage == 0:
            source = piece(self.ins, self.pieces[n], self.width).at[pl.ds(h * self.half, self.half)]
        if coming:
            to = self.region(n, h, stage, axis, here.peer(axis, here.size[axis] - step))
        return pltpu.make_async_remote_copy(
            src_ref=source, dst_ref=to, send_sem=self.send_sem.at[slot], recv_sem=self.recv_sem.at[slot],
            device_id=here.device(axis, here.peer(axis, step)), device_id_type=MESH,
        )

    def every(self, n, stage):
        return [(n, h, stage, step) for h in range(2) for step in self.here.steps(GATHER_ORDERS[h][stage])]

    def start(self, n, stage):
        for slot in self.every(n, stage):
            self.remote(*slot).start()

    def arrived(self, n, stage=3):
        for slot in self.every(n, stage):
            self.remote(*slot, coming=True).wait_recv()

    def own(self, n):
        place = tuple(self.here.at[a] for a in AXES)
        return pltpu.make_async_copy(
            piece(self.ins, self.pieces[n], self.width),
            piece(self.outs, self.pieces[n], self.width).at[place], self.own_sem.at[n],
        )

    def begin(self):
        self.here.greet()
        for n in range(self.count):
            self.start(n, 0)
            self.own(n).start()

    def ticks(self):
        return self.count + self.offsets[-1]

    def tick(self, k):
        for stage, offset in enumerate(self.offsets, 1):
            n = k - offset
            if 0 <= n < self.count:
                if stage == 1:
                    self.own(n).wait()
                self.arrived(n, stage - 1)
                self.start(n, stage)

    def end(self):
        for n in range(self.count):
            for stage in range(4):
                for slot in self.every(n, stage):
                    self.remote(*slot).wait_send()


class Share:
    def __init__(self, here, source, target, sems):
        self.here, self.source, self.target = here, source, target
        self.send_sem, self.recv_sem, self.own_sem = sems

    def remote(self, step, coming=False):
        here = self.here
        place = here.peer("tensor", here.size["tensor"] - step) if coming else here.at["tensor"]
        return pltpu.make_async_remote_copy(
            src_ref=self.source, dst_ref=self.target.at[place],
            send_sem=self.send_sem.at[step - 1], recv_sem=self.recv_sem.at[step - 1],
            device_id=here.device("tensor", here.peer("tensor", step)), device_id_type=MESH,
        )

    def own(self):
        return pltpu.make_async_copy(self.source, self.target.at[self.here.at["tensor"]], self.own_sem)

    def begin(self):
        self.own().start()
        for step in self.here.steps("tensor"):
            self.remote(step).start()

    def arrived(self):
        self.own().wait()
        for step in self.here.steps("tensor"):
            self.remote(step, coming=True).wait_recv()

    def end(self):
        for step in self.here.steps("tensor"):
            self.remote(step).wait_send()


SCATTER_ORDERS = (("tensor", "row", "line"), ("row", "tensor", "line"))
THREE = AXES[:3]


def late_shapes(count, rows, columns):
    size, out = sizes(), []
    for order in SCATTER_ORDERS:
        for stage in (1, 2, 3):
            free = [size[a] for a in THREE if a not in order[:stage]]
            out.append((count, size[order[stage - 1]] - 1, *free, rows // 2, columns))
    return out


def scatter_scratch(count, rows, columns):
    size = sizes()
    most = max(size.values()) - 1
    half_piece = (count, *(size[a] for a in THREE), rows, columns)
    return [
        pltpu.VMEM(half_piece, BF16),
        pltpu.VMEM(half_piece, BF16),
        *[pltpu.VMEM(dims, BF16) for dims in late_shapes(count, rows, columns)],
        pltpu.SemaphoreType.DMA((count, 2, 4, most)),
        pltpu.SemaphoreType.DMA((count, 2, 4, most)),
    ]


SCATTER_REFS = 10


def plus(terms):
    if len(terms) == 2:
        return terms[0] + terms[1]
    return sum(term.astype(F32) for term in terms).astype(BF16)


class Scatter:
    def __init__(self, here, staging, out, refs):
        self.here, self.staging, self.out = here, staging, out
        self.own, self.first, *late, self.send_sem, self.recv_sem = refs
        self.late = {(h, s): late[h * 3 + s - 1] for h in range(2) for s in (1, 2, 3)}
        self.half = self.own.shape[-2] // 2

    def to_core(self, n):
        here = self.here
        other = here.peer("core", 1)
        return pltpu.make_async_remote_copy(
            src_ref=self.staging(n).at[:, :, :, other], dst_ref=self.first.at[n],
            send_sem=self.send_sem.at[n, 0, 0, 0], recv_sem=self.recv_sem.at[n, 0, 0, 0],
            device_id=here.device("core", other), device_id_type=MESH,
        )

    def remote(self, n, h, stage, step):
        here, order = self.here, SCATTER_ORDERS[h]
        axis = order[stage - 1]
        to = here.peer(axis, step)
        index = [
            here.at[a] if a in order[: stage - 1] else to if a == axis else slice(None) for a in THREE
        ]
        slot = (n, h, stage, step - 1)
        return pltpu.make_async_remote_copy(
            src_ref=self.own.at[(n, *index, pl.ds(h * self.half, self.half))],
            dst_ref=self.late[h, stage].at[n, step - 1],
            send_sem=self.send_sem.at[slot], recv_sem=self.recv_sem.at[slot],
            device_id=here.device(axis, to), device_id_type=MESH,
        )

    def every(self, n, stage):
        return [
            self.remote(n, h, stage, step)
            for h in range(2)
            for step in self.here.steps(SCATTER_ORDERS[h][stage - 1])
        ]

    def add_core(self, n):
        source, core = self.staging(n), self.here.at["core"]
        for at in np.ndindex(self.own.shape[1:3]):
            self.own[(n, *at)] = plus([source[(*at, slice(None), core)], self.first[(n, *at)]])

    def add(self, n, h, stage):
        here, order = self.here, SCATTER_ORDERS[h]
        buf, steps = self.late[h, stage], here.size[order[stage - 1]] - 1
        free = [a for a in THREE if a not in order[:stage]]
        rows = pl.ds(h * self.half, self.half)
        for free_at in np.ndindex(*(here.size[a] for a in free)):
            at = {**here.at, **dict(zip(free, free_at, strict=True))}
            mine = (n, *(at[a] for a in THREE), rows)
            terms = [self.own[mine]] + [buf[(n, s, *free_at)] for s in range(steps)]
            if stage == 3:
                self.out(n)[rows, :] = sum(term.astype(F32) for term in terms)
            else:
                self.own[mine] = plus(terms)

    def begin(self, n):
        self.to_core(n).start()

    def tick(self, n, stage):
        if stage == 0:
            copy = self.to_core(n)
            copy.wait_recv()
            copy.wait_send()
            self.add_core(n)
        else:
            for copy in self.every(n, stage):
                copy.wait_recv()
            for h in range(2):
                self.add(n, h, stage)
        if stage < 3:
            for copy in self.every(n, stage + 1):
                copy.start()

    def end(self, count):
        def one(n, _):
            for stage in (1, 2, 3):
                for copy in self.every(n, stage):
                    copy.wait_send()
            return 0

        lax.fori_loop(0, count, one, 0)


SUM_AXES = ("core", "tensor", "row", "line")


class SmallSum:
    def __init__(self, here, refs):
        self.here = here
        *self.bufs, self.send_sem, self.recv_sem = refs

    @staticmethod
    def scratch(dims):
        size = sizes()
        most = max(size.values()) - 1
        return [
            *[pltpu.VMEM((size[a], *dims), F32) for a in SUM_AXES],
            pltpu.SemaphoreType.DMA((4, most)),
            pltpu.SemaphoreType.DMA((4, most)),
        ]

    def remote(self, stage, step, coming=False):
        here, axis, buf = self.here, SUM_AXES[stage], self.bufs[stage]
        place = here.peer(axis, here.size[axis] - step) if coming else here.at[axis]
        return pltpu.make_async_remote_copy(
            src_ref=buf.at[here.at[axis]], dst_ref=buf.at[place],
            send_sem=self.send_sem.at[stage, step - 1], recv_sem=self.recv_sem.at[stage, step - 1],
            device_id=here.device(axis, here.peer(axis, step)), device_id_type=MESH,
        )

    def start(self, stage, value):
        self.bufs[stage][self.here.at[SUM_AXES[stage]]] = value
        self.send(stage)

    def send(self, stage):
        for step in self.here.steps(SUM_AXES[stage]):
            self.remote(stage, step).start()

    def finish(self, stage):
        axis = SUM_AXES[stage]
        for step in self.here.steps(axis):
            self.remote(stage, step, coming=True).wait_recv()
            self.remote(stage, step).wait_send()
        total = self.bufs[stage][0]
        for place in range(1, self.here.size[axis]):
            total += self.bufs[stage][place]
        return total

    def tick(self, stage, target):
        total = self.finish(stage)
        if stage < 3:
            self.start(stage + 1, total)
        else:
            target[...] = total


SMALL_REFS = 6


def dot(left, right, left_dim=1, right_dim=0):
    return lax.dot_general(
        left, right, (((left_dim,), (right_dim,)), ((), ())), preferred_element_type=F32
    )


def side_by_side(ref, *lead):
    return jnp.concatenate([ref[(*lead, t)] for t in range(ref.shape[-3])], axis=-1)


def centred(rows):
    off = rows - jnp.mean(rows, axis=-1, keepdims=True)
    inverse = lax.rsqrt(jnp.mean(off * off, axis=-1, keepdims=True) + EPSILON)
    return off * inverse, inverse


def norm_back(grad, hat, inverse, gain):
    scaled = grad * gain
    along = jnp.mean(scaled * hat, axis=-1, keepdims=True)
    return inverse * (scaled - jnp.mean(scaled, axis=-1, keepdims=True) - hat * along)


def fold(rows):
    return jnp.sum(rows.reshape(-1, 8, rows.shape[-1]), axis=0)


def row_blocks(rows, size, one):
    def step(i, _):
        one(i, pl.ds(pl.multiple_of(i * size, size), size))
        return 0

    lax.fori_loop(0, rows // size, step, 0)


def transpose_into(source, target):
    rows = source.shape[0]
    for first in range(0, rows, 128):
        size = min(128, rows - first)
        target[:, first : first + size] = source[first : first + size, :].astype(F32).T.astype(BF16)


def two_heads(pair):
    first = lax.broadcasted_iota(jnp.int32, pair.shape, 1) < HD
    zero = jnp.zeros_like(pair)
    return jnp.concatenate([jnp.where(first, pair, zero), jnp.where(first, zero, pair)], axis=0)


def one_pair(stacked):
    first = lax.broadcasted_iota(jnp.int32, (SLOTS, PAIR), 1) < HD
    return jnp.where(first, stacked[:SLOTS], stacked[SLOTS:])


def masked_scores(query_stack, keys, length):
    scores = dot(keys, query_stack, 1, 1)
    slot = lax.broadcasted_iota(jnp.int32, scores.shape, 0)
    return jnp.where(slot < length, scores, MASKED_SCORE)


def group_weight(qkv_held, columns):
    parts = [qkv_held[e, t, ..., columns] for t in range(qkv_held.shape[1]) for e in range(3)]
    return jnp.concatenate([part.reshape(-1, PAIR) for part in parts], axis=-1)


def merge_tile(merge_held, columns):
    parts = [merge_held[t, ..., columns] for t in range(merge_held.shape[0])]
    return jnp.concatenate([part.reshape(-1, PAIR) for part in parts], axis=-1)


def schedule(ticks, last_piece, needed, steps):
    at = []
    first = needed.index(next(s for s in needed if s > 0), 0) if any(needed) else len(needed)
    early = first + last_piece
    for k in range(ticks):
        piece_done = k - last_piece
        even = 0 if k < early else 1 + (k - early) * (steps - 1) // (ticks - early)
        at.append(min(even, needed[max(piece_done, 0)]))
    for k in range(ticks - 2, -1, -1):
        at[k] = min(at[k], at[k + 1])
    return at


def forward_pieces(parts, width):
    pieces = pieces_of(parts, width)
    return sorted(pieces, key=lambda which: (max(which[0], 0) if which[0] < 2 else 2, which[2], which[0]))


def forward_kernel(
    width_of_piece, offsets, feed_columns,
    lengths, count, x_ref, teacher, gain, shift, merge_bias, gain_2, shift_2, reduce_bias,
    heads_bias, expand_bias, qkv_part, merge_part, expand_part, reduce_part,
    a_turned, qkv_ref, mixed_ref, log_ref, second_turned, activ, slope,
    out, grad_b, grad_turned, bias_grad, loss,
    hidden, grad, qkv_full, merge_full, expand_full, reduce_full,
    hidden_ref, second_ref, a_ref, qkv_held, merge_held, tiles, heads_bias_all, expand_bias_all,
    send_sem, recv_sem, own_sem, share_send, share_recv, share_own, held_sem, tile_sem, keep_sem,
):
    now = pl.program_id(0)
    rows = x_ref.shape[0]
    images = rows // SLOTS
    halves = qkv_held.shape[1]
    groups = width_of_piece // PAIR
    attention_steps = groups * images
    feed_steps = expand_part.shape[1] // feed_columns
    steps = attention_steps + feed_steps
    parts = [qkv_part, merge_part, expand_part, reduce_part]
    pieces = forward_pieces(parts, width_of_piece)
    gather = Gather(
        pieces, width_of_piece, offsets, parts, [qkv_full, merge_full, expand_full, reduce_full],
        (send_sem, recv_sem, own_sem),
    )
    shares = [
        Share(gather.here, source, target, (share_send.at[n], share_recv.at[n], share_own.at[n]))
        for n, (source, target) in enumerate([(heads_bias, heads_bias_all), (expand_bias, expand_bias_all)])
    ]
    tiles_of_piece = width_of_piece // feed_columns
    needed = [
        0 if a == 0 else images - 1 if a == 1 else max(attention_steps + col * tiles_of_piece - 1, 0)
        for a, _, col in pieces
    ]
    when = schedule(gather.ticks(), offsets[-1], needed, steps)
    image = lax.rem(now, images)
    group = lax.min(lax.div(now, images), groups - 1)
    columns = pl.ds(pl.multiple_of(group * PAIR, PAIR), PAIR)

    def hold(n):
        a, lead, _ = pieces[n]
        source, target = (qkv_full.at[lead], qkv_held.at[lead]) if a == 0 else (merge_full, merge_held)
        return pltpu.make_async_copy(source, target, held_sem.at[n])

    def tile_copies(j):
        block = pl.ds(j * feed_columns, feed_columns)
        return [
            pltpu.make_async_copy(
                full.at[:, :, :, :, :, block], tiles.at[j % 2, kind], tile_sem.at[j % 2, kind]
            )
            for kind, full in enumerate((expand_full, reduce_full))
        ]

    def fetch_tiles(j):
        for kind, copy in enumerate(tile_copies(j)):
            if j % tiles_of_piece == 0:
                gather.arrived(4 + 2 * (j // tiles_of_piece) + kind)
            copy.start()

    def keep_hidden():
        return pltpu.make_async_copy(hidden_ref, hidden, keep_sem)

    @pl.when(now == 0)
    def _():
        gather.begin()
        for share in shares:
            share.begin()
        early = [k for k in range(gather.ticks()) if when[k] == 0]
        blocks = rows // BLOCK
        per = -(-blocks // max(len(early), 1))

        def norm(i, _):
            at = pl.ds(pl.multiple_of(i * BLOCK, BLOCK), BLOCK)
            x = x_ref[at, :].astype(F32)
            hidden_ref[at, :] = x + merge_bias[...]
            a_ref[at, :] = (centred(x)[0] * gain[...] + shift[...]).astype(BF16)
            return 0

        done = 0
        for k in early:
            lax.fori_loop(done, min(done + per, blocks), norm, 0)
            done = min(done + per, blocks)
            gather.tick(k)
            n = k - offsets[-1] - 1
            if 0 <= n < 3:
                gather.arrived(n)
                hold(n).start()
        lax.fori_loop(done, blocks, norm, 0)
        transpose_into(a_ref, a_turned)
        for n in range(max(len(early) - offsets[-1] - 1, 0), 3):
            gather.arrived(n)
            hold(n).start()
        for share in shares:
            share.arrived()
        for n in range(3):
            hold(n).wait()

    for k in range(gather.ticks()):
        if when[k] > 0:
            pl.when(now == when[k])(partial(gather.tick, k))

    @pl.when((now < attention_steps) & (image == 0))
    def _():
        weight = group_weight(qkv_held, columns)
        bias = []
        for t in range(halves):
            query = heads_bias_all[t, 0:1, columns]
            bias += [query, jnp.zeros_like(query), heads_bias_all[t, 1:2, columns]]
        bias = jnp.concatenate(bias, axis=-1)
        for i in range(images):
            at = slice(i * SLOTS, (i + 1) * SLOTS)
            out = (dot(a_ref[at, :], weight) + bias).astype(BF16)
            for t in range(halves):
                query = slice(t * 3 * PAIR, (t * 3 + 1) * PAIR)
                qkv_ref[0, at, query] = out[:, query] * 0.125
                rest = slice((t * 3 + 1) * PAIR, (t * 3 + 3) * PAIR)
                qkv_ref[0, at, rest] = out[:, rest]

    @pl.when(now < attention_steps)
    def _():
        length = lengths[image]
        at = pl.ds(pl.multiple_of(image * SLOTS, SLOTS), SLOTS)
        for t in range(halves):
            first = t * 3 * PAIR
            query_stack = two_heads(qkv_ref[0, at, first : first + PAIR])
            scores = masked_scores(query_stack, qkv_ref[0, at, first + PAIR : first + 2 * PAIR], length)
            highest = jnp.max(scores, axis=0, keepdims=True)
            expo = jnp.exp(scores - highest)
            totals = jnp.sum(expo, axis=0, keepdims=True)
            values = qkv_ref[0, at, first + 2 * PAIR : first + 3 * PAIR]
            mixed = dot(values, expo.astype(BF16), 0, 0) * (1.0 / totals)
            mixed_ref[0, at, t * PAIR : (t + 1) * PAIR] = one_pair(mixed.T).astype(BF16)
            log_ref[0, 0, t : t + 1] = highest + jnp.log(totals)

    @pl.when(now == images - 1)
    def _():
        gather.arrived(3)
        hold(3).start()
        hold(3).wait()

    @pl.when((now < attention_steps) & (image == images - 1))
    def _():
        weight = merge_tile(merge_held, columns)
        for i in range(images):
            part = slice(i * SLOTS, (i + 1) * SLOTS)
            hidden_ref[part, :] += dot(mixed_ref[0, part, :], weight, 1, 1)

    @pl.when(now == attention_steps - 1)
    def _():
        keep_hidden().start()
        fetch_tiles(0)

        def norm(_, at):
            hat, _ = centred(hidden_ref[at, :])
            second_ref[at, :] = (hat * gain_2[...] + shift_2[...]).astype(BF16)

        row_blocks(rows, BLOCK, norm)
        transpose_into(second_ref, second_turned)

    for j in range(feed_steps):

        @pl.when(now == attention_steps + j)
        def _(j=j):
            if j == 0:
                keep_hidden().wait()
            for copy in tile_copies(j):
                copy.wait()
            if j + 1 < feed_steps:
                fetch_tiles(j + 1)

    @pl.when(now >= attention_steps)
    def _():
        j = now - attention_steps
        block = pl.ds(pl.multiple_of(j * feed_columns, feed_columns), feed_columns)
        slot = lax.rem(j, 2)
        weight, reduce_tile = (
            jnp.concatenate([tiles[slot, kind, t].reshape(-1, feed_columns) for t in range(halves)], axis=-1)
            for kind in range(2)
        )
        bias = jnp.concatenate([expand_bias_all[t, :, block] for t in range(halves)], axis=-1)
        for i in range(images):
            at = slice(i * SLOTS, (i + 1) * SLOTS)
            z = dot(second_ref[at, :], weight) + bias
            square = z * z
            bend = jnp.tanh(0.7978845608 * z * (1.0 + 0.044715 * square))
            half = 0.5 + 0.5 * bend
            act = (z * half).astype(BF16)
            activ[0, at, :] = act
            inner = 0.7978845608 * z * (1.0 + (3 * 0.044715) * square)
            slope[0, at, :] = (half + 0.5 * inner * (1.0 - bend * bend)).astype(BF16)
            hidden_ref[at, :] += dot(act, reduce_tile, 1, 1)

    @pl.when(now == steps - 1)
    def _():
        bias_grad[...] = jnp.zeros_like(bias_grad)
        loss[...] = jnp.zeros_like(loss)

        def end(i, at):
            image, block = lax.div(i, SLOTS // BLOCK), lax.rem(i, SLOTS // BLOCK)
            slot = block * BLOCK + lax.broadcasted_iota(jnp.int32, (BLOCK, 1), 0)
            valid = slot < lengths[image]
            result = jnp.where(valid, hidden_ref[at, :] + reduce_bias[...], 0.0)
            out[at, :] = result.astype(BF16)
            error = jnp.where(valid, result - teacher[at, :].astype(F32), 0.0)
            loss[0] += fold(error * error)
            back = 2.0 * error / count[0]
            bias_grad[0] += fold(back)
            hidden_ref[at, :] = back
            grad_b[at, :] = back.astype(BF16)

        row_blocks(rows, BLOCK, end)
        keep = pltpu.make_async_copy(hidden_ref, grad, keep_sem)
        keep.start()
        transpose_into(grad_b, grad_turned)
        keep.wait()
        gather.end()
        for share in shares:
            share.end()


def feed_back_kernel(
    result_b, result_turned, second_turned, expand, reduce, activ, slope, hidden, result_grad, gain,
    reduce_grad, expand_grad, expand_bias_grad, hidden_grad, hidden_b, hidden_turned, sums,
    total, staging, *scatter_refs,
):
    step, steps = pl.program_id(0), reduce_grad.shape[1] // expand.shape[-1]
    rows, width = result_b.shape
    halves, _, columns = expand.shape
    expand_tile, reduce_tile = side_by_side(expand), side_by_side(reduce)

    scatters = []
    here = Place()
    for p, target in enumerate((reduce_grad, expand_grad)):
        slot = lambda j, p=p: staging.at[lax.rem(j, 2), p]
        part = lambda j, target=target: target.at[:, pl.ds(pl.multiple_of(j * columns, columns), columns)]
        scatters.append(Scatter(here, slot, part, scatter_refs[p * SCATTER_REFS : (p + 1) * SCATTER_REFS]))

    @pl.when(step == 0)
    def _():
        here.greet()
        total[...] = jnp.zeros_like(total)

    def ticks(p, back):
        for stage in range(3, -1, -1):

            @pl.when(step >= stage + back)
            def _(stage=stage):
                scatters[p].tick(step - back - stage, stage)

    def stage_out(p, part):
        for t in range(halves):
            block = part[:, t * columns : (t + 1) * columns].astype(BF16)
            staging[lax.rem(step, 2), p, t] = block.reshape(staging.shape[3:])
        scatters[p].begin(step)

    stage_out(0, dot(result_turned[...], activ[0]))
    ticks(1, 1)
    bias = jnp.zeros((8, halves * columns), F32)
    parts = []
    for i in range(rows // SLOTS):
        at = slice(i * SLOTS, (i + 1) * SLOTS)
        z_grad = (dot(result_b[at, :], reduce_tile) * slope[0, at, :].astype(F32)).astype(BF16)
        bias += fold(z_grad.astype(F32))
        parts.append(z_grad)
        total[at, :] += dot(z_grad, expand_tile, 1, 1)
    expand_bias_grad[0] = jnp.sum(bias, axis=0, keepdims=True)
    ticks(0, 0)
    stage_out(1, dot(second_turned[...], jnp.concatenate(parts, axis=0)))

    @pl.when(step == steps - 1)
    def _():
        sums[...] = jnp.zeros_like(sums)
        size = 128 if rows % 128 == 0 else rows
        blocks = rows // size

        def end(first, h_ref, g_ref, back_ref, back_b_ref, turned_ref):
            block = pl.program_id(0) + first
            for k in range(0, size, 32):
                at = slice(k, k + 32)
                hat, inverse = centred(h_ref[at, :])
                second_grad = total[pl.ds(pl.multiple_of(block * size + k, 32), 32), :]
                back = g_ref[at, :] + norm_back(second_grad, hat, inverse, gain[...])
                sums[0] += fold(second_grad * hat)
                sums[1] += fold(second_grad)
                sums[2] += fold(back)
                back_ref[at, :] = back
                back_b_ref[at, :] = back.astype(BF16)
            turned_ref[...] = back_ref[...].T.astype(BF16)

        def some(first, last):
            row_block = pl.BlockSpec((size, width), lambda i: (i + first, 0))
            pltpu.emit_pipeline(
                partial(end, first),
                grid=(last - first,),
                in_specs=[row_block, row_block],
                out_specs=[row_block, row_block, pl.BlockSpec((width, size), lambda i: (0, i + first))],
            )(hidden, result_grad, hidden_grad, hidden_b, hidden_turned)

        bounds = [blocks * k // 3 for k in range(4)]
        for drain in range(4):
            for stage in range(3, -1, -1):
                for p, first in ((0, drain + 1), (1, drain)):
                    n = steps + first - 1 - stage
                    if stage >= first and n >= 0:
                        scatters[p].tick(n, stage)
            if drain < 3 and bounds[drain + 1] > bounds[drain]:
                some(bounds[drain], bounds[drain + 1])
        for scatter in scatters:
            scatter.end(steps)


def attend_back_kernel(
    lengths, a_turned, hidden_b, hidden_turned, qkv_ref, mixed_ref, log_ref, x_ref, hidden_grad, gain,
    qkv_weight, merge_weight, second_sums, reduce_bias_grad, loss, expand_bias_grad,
    merge_grad, qkv_grad, inputs_grad, early_out, expand_out, late_out, heads_out,
    mixed_grad, heads_grad, total, qkv_held, merge_held, sem, merge_staging, qkv_staging, sums, bias_grad,
    *comm,
):
    now = pl.program_id(0)
    rows = x_ref.shape[0]
    images = rows // SLOTS
    halves = qkv_held.shape[1]
    groups = merge_grad.shape[1] // PAIR
    steps = groups * images
    group, image = lax.div(now, images), lax.rem(now, images)
    here = Place()
    block = lambda c: pl.ds(pl.multiple_of(c * PAIR, PAIR), PAIR)
    merge_scatter = Scatter(here, lambda n: merge_staging, lambda n: merge_grad.at[:, block(n)], comm[:SCATTER_REFS])
    qkv_scatter = Scatter(
        here, lambda n: qkv_staging.at[lax.rem(n, 3)],
        lambda n: qkv_grad.at[lax.rem(n, 3), :, block(lax.div(n, 3))], comm[SCATTER_REFS : 2 * SCATTER_REFS],
    )
    early, expand_sum, late, heads_sum = (
        SmallSum(here, comm[2 * SCATTER_REFS + k * SMALL_REFS :][:SMALL_REFS]) for k in range(4)
    )

    def qkv_tick(c, stage):
        for e in range(3):
            qkv_scatter.tick(3 * c + e, stage)
    columns = pl.ds(pl.multiple_of(group * PAIR, PAIR), PAIR)

    @pl.when(now == 0)
    def _():
        copies = [
            pltpu.make_async_copy(merge_weight, merge_held, sem.at[1]),
            pltpu.make_async_copy(qkv_weight, qkv_held, sem.at[0]),
        ]
        for copy in copies:
            copy.start()
        here.greet()
        total[...] = jnp.zeros_like(total)
        rowsum = lambda ref, k: jnp.sum(ref[k], axis=0, keepdims=True)
        vectors = [rowsum(second_sums, k) for k in range(3)] + [rowsum(reduce_bias_grad, 0)]
        lost = jnp.sum(rowsum(loss, 0), axis=1, keepdims=True)
        vectors.append(jnp.broadcast_to(lost, vectors[0].shape))
        early.start(0, jnp.concatenate(vectors, axis=0))
        expand_sum.start(0, expand_bias_grad[:, 0])
        for copy in copies:
            copy.wait()

    @pl.when(image == 0)
    def _():
        weight = merge_tile(merge_held, columns)
        for i in range(rows // SLOTS):
            part = slice(i * SLOTS, (i + 1) * SLOTS)
            mixed_grad[part, :] = dot(hidden_b[part, :], weight).astype(BF16)
        part = dot(hidden_turned[...], mixed_ref[0]).astype(BF16)
        for t in range(halves):
            merge_staging[t] = part[:, t * PAIR : (t + 1) * PAIR].reshape(merge_staging.shape[1:])
        merge_scatter.begin(group)

        @pl.when(group == 0)
        def _():
            early.tick(0, early_out)
            expand_sum.tick(0, expand_out)

        @pl.when(group > 0)
        def _():
            merge_scatter.tick(group - 1, 2)
            qkv_tick(group - 1, 1)

    length = lengths[image]
    at = pl.ds(pl.multiple_of(image * SLOTS, SLOTS), SLOTS)
    for t in range(halves):
        first = t * 3 * PAIR
        query_stack = two_heads(qkv_ref[0, at, first : first + PAIR])
        keys = qkv_ref[0, at, first + PAIR : first + 2 * PAIR]
        values = qkv_ref[0, at, first + 2 * PAIR : first + 3 * PAIR]
        scores = masked_scores(query_stack, keys, length)
        attend = jnp.exp(scores - log_ref[0, 0, t : t + 1])
        grad_stack = two_heads(mixed_grad[at, t * PAIR : (t + 1) * PAIR])
        attend_grad = dot(values, grad_stack, 1, 1)
        value_grad = dot(attend.astype(BF16), grad_stack).astype(BF16)
        centre = jnp.sum(attend * attend_grad, axis=0, keepdims=True)
        score_grad = (attend * (attend_grad - centre)).astype(BF16)
        key_grad = dot(score_grad, query_stack).astype(BF16)
        query_grad = dot(keys, score_grad, 0, 0)
        query_grad = (one_pair(query_grad.T) * 0.125).astype(BF16)
        heads_grad[at, first : first + PAIR] = query_grad
        heads_grad[at, first + PAIR : first + 2 * PAIR] = key_grad
        heads_grad[at, first + 2 * PAIR : first + 3 * PAIR] = value_grad

    @pl.when(image == images - 1)
    def _():
        @pl.when(group == 0)
        def _():
            early.tick(1, early_out)
            expand_sum.tick(1, expand_out)

        @pl.when(group > 0)
        def _():
            merge_scatter.tick(group - 1, 3)
            qkv_tick(group - 1, 2)

        merge_scatter.tick(group, 0)
        weight = group_weight(qkv_held, columns)
        bias = jnp.zeros((8, halves * 3 * PAIR), F32)
        for i in range(rows // SLOTS):
            part = slice(i * SLOTS, (i + 1) * SLOTS)
            bias += fold(heads_grad[part, :].astype(F32))
        bias_grad[pl.ds(group, 1), :] = jnp.sum(bias, axis=0, keepdims=True)
        part = dot(a_turned[...], heads_grad[...]).astype(BF16)
        for t in range(halves):
            for e in range(3):
                first = (t * 3 + e) * PAIR
                qkv_staging[e, t] = part[:, first : first + PAIR].reshape(qkv_staging.shape[2:])
        for e in range(3):
            qkv_scatter.begin(3 * group + e)
        for i in range(rows // SLOTS):
            part = slice(i * SLOTS, (i + 1) * SLOTS)
            total[part, :] += dot(heads_grad[part, :], weight, 1, 1)

        @pl.when(group == 0)
        def _():
            early.tick(2, early_out)
            expand_sum.tick(2, expand_out)

        @pl.when(group > 0)
        def _():
            qkv_tick(group - 1, 3)

        merge_scatter.tick(group, 1)
        qkv_tick(group, 0)

    @pl.when(now == steps - 1)
    def _():
        heads_sum.start(0, bias_grad[...])
        sums[...] = jnp.zeros_like(sums)

        def end(i, _):
            at = pl.ds(pl.multiple_of(i * BLOCK, BLOCK), BLOCK)
            hat, inverse = centred(x_ref[at, :].astype(F32))
            grad = total[at, :]
            sums[0] += fold(grad * hat)
            sums[1] += fold(grad)
            inputs_grad[at, :] = hidden_grad[at, :] + norm_back(grad, hat, inverse, gain[...])
            return 0

        blocks = rows // BLOCK
        last = groups - 1
        lax.fori_loop(0, blocks // 2, end, 0)
        merge_scatter.tick(last, 2)
        qkv_tick(last, 1)
        early.tick(3, early_out)
        expand_sum.tick(3, expand_out)
        heads_sum.tick(0, heads_out)
        lax.fori_loop(blocks // 2, blocks, end, 0)
        late.start(0, jnp.sum(sums[...], axis=1))
        merge_scatter.tick(last, 3)
        qkv_tick(last, 2)
        heads_sum.tick(1, heads_out)
        late.tick(0, late_out)
        qkv_tick(last, 3)
        heads_sum.tick(2, heads_out)
        late.tick(1, late_out)
        heads_sum.tick(3, heads_out)
        late.tick(2, late_out)
        late.tick(3, late_out)
        merge_scatter.end(groups)
        qkv_scatter.end(3 * groups)


def shape(dims, kind=BF16):
    return jax.ShapeDtypeStruct(dims, kind)


def once(dims):
    return pl.BlockSpec(dims, lambda *_: (0,) * len(dims), pipeline_mode=pl.Buffered(1))


ELSEWHERE = pl.BlockSpec(memory_space=pl.ANY)
SCALARS = pl.BlockSpec(memory_space=pltpu.SMEM)
LIMIT = 63 * 2**20


OFFSETS = (0, 1, 2)


def feed_width(halves):
    return max(PAIR, 512 // halves)


def forward(
    lengths, count, x, teacher, gain, shift, merge_bias, gain_2, shift_2, reduce_bias, heads_bias, expand_bias, parts
):
    rows, width = x.shape
    halves, columns = lax.axis_size("tensor"), parts[0].shape[2]
    groups, images = columns // PAIR, rows // SLOTS
    attention_steps = groups * images
    feed_columns = feed_width(halves)
    feed_steps = parts[2].shape[1] // feed_columns
    pieces = len(pieces_of(parts, columns))
    most = max(sizes().values()) - 1
    line, whole, turned = once((1, width)), once((rows, width)), once((width, rows))
    group_at = lambda s: lax.min(lax.div(s, images), groups - 1)
    feed_at = lambda s: lax.max(s - attention_steps, 0)
    wholes = [whole_shape(part) for part in parts]
    saved = pl.BlockSpec((1, rows, halves * feed_columns), lambda s: (feed_at(s), 0, 0))
    return pl.pallas_call(
        partial(forward_kernel, columns, OFFSETS, feed_columns),
        grid=(attention_steps + feed_steps,),
        in_specs=[
            SCALARS, SCALARS, whole, whole, *[line] * 6, *[ELSEWHERE] * 2, *[once(part.shape) for part in parts]
        ],
        out_specs=[
            turned,
            pl.BlockSpec((1, rows, halves * 3 * PAIR), lambda s: (group_at(s), 0, 0)),
            pl.BlockSpec((1, rows, halves * PAIR), lambda s: (group_at(s), 0, 0)),
            pl.BlockSpec(
                (1, 1, halves, 2 * SLOTS),
                lambda s: (group_at(s), jnp.where(s < attention_steps, lax.rem(s, images), images - 1), 0, 0),
            ),
            turned, saved, saved, whole, whole, turned, once((1, 8, width)), once((1, 8, width)),
            *[ELSEWHERE] * 6,
        ],
        out_shape=[
            shape((width, rows)),
            shape((groups, rows, halves * 3 * PAIR)),
            shape((groups, rows, halves * PAIR)),
            shape((groups, images, halves, 2 * SLOTS), F32),
            shape((width, rows)),
            *[shape((feed_steps, rows, halves * feed_columns))] * 2,
            shape((rows, width)), shape((rows, width)), shape((width, rows)),
            shape((1, 8, width), F32), shape((1, 8, width), F32),
            shape((rows, width), F32), shape((rows, width), F32),
            *[shape(dims) for dims in wholes],
        ],
        scratch_shapes=[
            pltpu.VMEM((rows, width), F32),
            pltpu.VMEM((rows, width), BF16),
            pltpu.VMEM((rows, width), BF16),
            pltpu.VMEM(wholes[0], BF16),
            pltpu.VMEM(wholes[1], BF16),
            pltpu.VMEM((2, 2, *wholes[2][:-1], feed_columns), BF16),
            pltpu.VMEM((halves, *heads_bias.shape), F32),
            pltpu.VMEM((halves, *expand_bias.shape), F32),
            pltpu.SemaphoreType.DMA((pieces, 2, 4, most)),
            pltpu.SemaphoreType.DMA((pieces, 2, 4, most)),
            pltpu.SemaphoreType.DMA((pieces,)),
            pltpu.SemaphoreType.DMA((2, halves)),
            pltpu.SemaphoreType.DMA((2, halves)),
            pltpu.SemaphoreType.DMA((2,)),
            pltpu.SemaphoreType.DMA((4,)),
            pltpu.SemaphoreType.DMA((2, 2)),
            pltpu.SemaphoreType.DMA(()),
        ],
        compiler_params=pltpu.CompilerParams(
            vmem_limit_bytes=LIMIT, collective_id=0, has_side_effects=True
        ),
        name="forward",
    )(
        lengths, count, x, teacher, gain, shift, merge_bias, gain_2, shift_2, reduce_bias,
        heads_bias, expand_bias, *parts,
    )


def feed_back(result_b, result_turned, second_turned, expand, reduce, activ, slope, hidden, result_grad, gain):
    rows, width = result_b.shape
    halves, _, wide = expand.shape
    steps, columns = activ.shape[0], activ.shape[2] // halves
    size = sizes()
    part_rows = width // math.prod(size[a] for a in ("line", "row", "core"))
    tile = pl.BlockSpec((halves, width, columns), lambda j: (0, 0, j))
    saved = pl.BlockSpec((1, rows, halves * columns), lambda j: (j, 0, 0))
    whole, turned, part = once((rows, width)), once((width, rows)), once((part_rows, wide))
    return pl.pallas_call(
        feed_back_kernel,
        grid=(steps,),
        in_specs=[whole, turned, turned, tile, tile, saved, saved, ELSEWHERE, ELSEWHERE, once((1, width))],
        out_specs=[
            part, part, pl.BlockSpec((1, 1, halves * columns), lambda j: (j, 0, 0)),
            ELSEWHERE, ELSEWHERE, ELSEWHERE, once((3, 8, width)),
        ],
        out_shape=[
            shape((part_rows, wide), F32), shape((part_rows, wide), F32),
            shape((steps, 1, halves * columns), F32),
            shape((rows, width), F32), shape((rows, width)), shape((width, rows)), shape((3, 8, width), F32),
        ],
        scratch_shapes=[
            pltpu.VMEM((rows, width), F32),
            pltpu.VMEM((2, 2, *(size[a] for a in AXES), part_rows, columns), BF16),
            *scatter_scratch(steps, part_rows, columns),
            *scatter_scratch(steps, part_rows, columns),
        ],
        compiler_params=pltpu.CompilerParams(
            vmem_limit_bytes=LIMIT, collective_id=1, has_side_effects=True
        ),
        name="feed_back",
    )(result_b, result_turned, second_turned, expand, reduce, activ, slope, hidden, result_grad, gain)


def attend_back(
    lengths, a_turned, hidden_b, hidden_turned, qkv, mixed, log_total, x, hidden_grad, gain,
    qkv_whole, merge_whole, second_sums, reduce_bias_grad, loss, expand_bias_grad,
):
    rows, width = x.shape
    halves, (part_rows, columns) = qkv_whole.shape[1], qkv_whole.shape[-2:]
    groups, images = columns // PAIR, rows // SLOTS
    whole, turned = once((rows, width)), once((width, rows))
    group_at = lambda s: lax.div(s, images)
    size = sizes()
    staging = (*(size[a] for a in AXES), part_rows, PAIR)
    small = [(5, width), (expand_bias_grad.shape[0], expand_bias_grad.shape[2]), (2, width), (groups, halves * 3 * PAIR)]
    vmem = lambda array: once(array.shape)
    return pl.pallas_call(
        attend_back_kernel,
        grid=(groups * images,),
        in_specs=[
            SCALARS, turned, whole, turned,
            pl.BlockSpec((1, rows, halves * 3 * PAIR), lambda s: (group_at(s), 0, 0)),
            pl.BlockSpec((1, rows, halves * PAIR), lambda s: (group_at(s), 0, 0)),
            pl.BlockSpec((1, 1, halves, 2 * SLOTS), lambda s: (group_at(s), lax.rem(s, images), 0, 0)),
            whole, whole, once((1, width)), ELSEWHERE, ELSEWHERE,
            vmem(second_sums), vmem(reduce_bias_grad), vmem(loss), vmem(expand_bias_grad),
        ],
        out_specs=[
            once((part_rows, columns)), once((3, part_rows, columns)), whole, *[once(dims) for dims in small]
        ],
        out_shape=[
            shape((part_rows, columns), F32), shape((3, part_rows, columns), F32), shape((rows, width), F32),
            *[shape(dims, F32) for dims in small],
        ],
        scratch_shapes=[
            pltpu.VMEM((rows, halves * PAIR), BF16),
            pltpu.VMEM((rows, halves * 3 * PAIR), BF16),
            pltpu.VMEM((rows, width), F32),
            pltpu.VMEM(qkv_whole.shape, BF16),
            pltpu.VMEM(merge_whole.shape, BF16),
            pltpu.SemaphoreType.DMA((2,)),
            pltpu.VMEM(staging, BF16),
            pltpu.VMEM((3, *staging), BF16),
            pltpu.VMEM((2, 8, width), F32),
            pltpu.VMEM((groups, halves * 3 * PAIR), F32),
            *scatter_scratch(groups, part_rows, PAIR),
            *scatter_scratch(3 * groups, part_rows, PAIR),
            *[ref for dims in small for ref in SmallSum.scratch(dims)],
        ],
        compiler_params=pltpu.CompilerParams(
            vmem_limit_bytes=LIMIT, collective_id=2, has_side_effects=True
        ),
        name="attend_back",
    )(
        lengths, a_turned, hidden_b, hidden_turned, qkv, mixed, log_total, x, hidden_grad, gain,
        qkv_whole, merge_whole, second_sums, reduce_bias_grad, loss, expand_bias_grad,
    )


def finish_kernel(count, early, late, expand_sum, heads_sum, *refs):
    arrays = (len(refs) - 10) // 2
    sources, targets = refs[:arrays], refs[arrays : 2 * arrays]
    loss, first_gain, first_shift, second_gain, second_shift, merge_bias, reduce_bias, heads_bias, expand_bias, sem = (
        refs[2 * arrays :]
    )
    copies = [
        pltpu.make_async_copy(source, target, sem.at[n])
        for n, (source, target) in enumerate(zip(sources, targets, strict=True))
    ]
    for copy in copies:
        copy.start()
    tensor = lax.axis_index("tensor")
    loss[...] = early[4:5, 0:1] / count[0]
    for k, target in enumerate((second_gain, second_shift, merge_bias, reduce_bias)):
        target[...] = early[k : k + 1]
    first_gain[...] = late[0:1]
    first_shift[...] = late[1:2]
    for k, e in enumerate((0, 2)):
        columns = pl.ds(pl.multiple_of((tensor * 3 + e) * PAIR, PAIR), PAIR)
        for group in range(heads_sum.shape[0]):
            heads_bias[k : k + 1, group * PAIR : (group + 1) * PAIR] = heads_sum[group : group + 1, columns]
    wide = expand_bias.shape[1] // expand_sum.shape[0]
    columns = pl.ds(pl.multiple_of(tensor * wide, wide), wide)
    for step in range(expand_sum.shape[0]):
        expand_bias[:, step * wide : (step + 1) * wide] = expand_sum[step : step + 1, columns]
    for copy in copies:
        copy.wait()


def finish(count, early, late, expand_sum, heads_sum, arrays):
    width, halves = early.shape[1], lax.axis_size("tensor")
    small = [(1, 1), *[(1, width)] * 6, (2, heads_sum.shape[0] * PAIR), (1, expand_sum.size // halves)]
    vmem = pl.BlockSpec(memory_space=pltpu.VMEM)
    return pl.pallas_call(
        finish_kernel,
        in_specs=[SCALARS, *[vmem] * (4 + len(arrays))],
        out_specs=[*[ELSEWHERE] * len(arrays), *[vmem] * len(small)],
        out_shape=[*[shape(a.shape, a.dtype) for a in arrays], *[shape(dims, F32) for dims in small]],
        scratch_shapes=[pltpu.SemaphoreType.DMA((len(arrays),))],
        compiler_params=pltpu.CompilerParams(vmem_limit_bytes=LIMIT),
        name="finish",
    )(count, early, late, expand_sum, heads_sum, *arrays)


def body(
    inputs,
    teacher,
    lengths,
    first_gain,
    first_shift,
    query_key_value_weight,
    heads_bias,
    merge_weight,
    merge_bias,
    second_gain,
    second_shift,
    expand_weight,
    expand_bias,
    reduce_weight,
    reduce_bias,
):
    rows, width = inputs.shape
    images = rows // SLOTS
    halves = lax.axis_size("tensor")
    tensor = lax.axis_index("tensor")
    hidden = expand_weight.shape[1] * halves
    piece_width = query_key_value_weight.shape[-1]
    groups = piece_width // PAIR
    place = lax.axis_index("dp") * halves + tensor
    mine = lax.dynamic_slice_in_dim(lengths, place * images, images)
    count = jnp.sum(lengths).astype(F32).reshape(1)
    line = lambda vector: vector.reshape(1, width)

    (
        a_turned, qkv, mixed, log_total, second_turned, activ, slope, outputs, result_b, result_turned,
        reduce_bias_grad, loss, hidden_state, result_grad, *wholes,
    ) = forward(
        mine, count, inputs, teacher, line(first_gain), line(first_shift), line(merge_bias),
        line(second_gain), line(second_shift), line(reduce_bias), heads_bias, expand_bias.reshape(1, -1),
        [query_key_value_weight, merge_weight, expand_weight, reduce_weight],
    )
    expand_full, reduce_full = (whole.reshape(halves, width, -1) for whole in wholes[2:])
    columns = feed_width(halves)
    steps = hidden // halves // columns
    reduce_grad, expand_grad, expand_bias_grad, hidden_grad, hidden_b, hidden_turned, second_sums = feed_back(
        result_b, result_turned, second_turned, expand_full, reduce_full, activ, slope, hidden_state,
        result_grad, line(second_gain),
    )
    merge_grad, heads_grad, inputs_grad, early, expand_sum, late, heads_sum = attend_back(
        mine, a_turned, hidden_b, hidden_turned, qkv, mixed, log_total, inputs, hidden_grad,
        line(first_gain), wholes[0], wholes[1], second_sums, reduce_bias_grad, loss, expand_bias_grad,
    )
    outputs, inputs_grad, heads_grad, merge_grad, expand_grad, reduce_grad, loss, *vectors, heads_sum, expand_sum = finish(
        count, early, late, expand_sum, heads_sum,
        [outputs, inputs_grad, heads_grad, merge_grad, expand_grad, reduce_grad],
    )
    first_gain_grad, first_shift_grad, second_gain_grad, second_shift_grad, merge_bias_grad, reduce_bias_grad = (
        vector.reshape(width) for vector in vectors
    )
    return (
        loss.reshape(()),
        outputs,
        inputs_grad,
        first_gain_grad,
        first_shift_grad,
        heads_grad,
        heads_sum,
        merge_grad,
        merge_bias_grad,
        second_gain_grad,
        second_shift_grad,
        expand_grad,
        expand_sum.reshape(-1),
        reduce_grad,
        reduce_bias_grad,
    )


def solution(mesh):
    return jax.shard_map(
        body,
        mesh=mesh,
        in_specs=(
            P(("dp", "tensor"), None),
            P(("dp", "tensor"), None),
            P(),
            P(),
            P(),
            P(None, "dp", "tensor"),
            P(None, "tensor"),
            P("dp", "tensor"),
            P(),
            P(),
            P(),
            P("dp", "tensor"),
            P("tensor"),
            P("dp", "tensor"),
            P(),
        ),
        out_specs=(
            P(),
            P(("dp", "tensor"), None),
            P(("dp", "tensor"), None),
            P(),
            P(),
            P(None, "dp", "tensor"),
            P(None, "tensor"),
            P("dp", "tensor"),
            P(),
            P(),
            P(),
            P("dp", "tensor"),
            P("tensor"),
            P("dp", "tensor"),
            P(),
        ),
        check_vma=False,
    )
```

```python
from functools import partial
import math

import jax
import jax.numpy as jnp
import numpy as np
from jax import lax
from jax.experimental import pallas as pl
from jax.experimental.pallas import tpu as pltpu
from jax.sharding import PartitionSpec as P

HD = 64
SLOTS = 320
PAIR = 2 * HD
BLOCK = SLOTS // 2

EPSILON = 1e-05
MASKED_SCORE = -1e30
F32 = jnp.float32
BF16 = jnp.bfloat16
CORES = 2
LINE = 4


AXES = ("tensor", "line", "row", "core")
MESH = pl.DeviceIdType.MESH
GATHER_ORDERS = (("line", "tensor", "row", "core"), ("line", "row", "tensor", "core"))


def sizes():
    dp = lax.axis_size("dp")
    return {"tensor": lax.axis_size("tensor"), "line": LINE, "row": dp // (LINE * CORES), "core": CORES}


class Place:
    def __init__(self):
        self.size = sizes()
        index = lax.axis_index("dp")
        self.at = {
            "tensor": lax.axis_index("tensor"),
            "core": lax.rem(index, CORES),
            "row": lax.rem(lax.div(index, CORES), self.size["row"]),
            "line": lax.div(index, CORES * self.size["row"]),
        }

    def steps(self, axis):
        return range(1, self.size[axis])

    def peer(self, axis, step):
        return lax.rem(self.at[axis] + step, self.size[axis])

    def device(self, axis, place):
        at = {**self.at, axis: place}
        return {"dp": (at["line"] * self.size["row"] + at["row"]) * CORES + at["core"], "tensor": at["tensor"]}

    def greet(self):
        barrier = pltpu.get_barrier_semaphore()
        count = 0
        for axis in AXES:
            for step in self.steps(axis):
                pl.semaphore_signal(
                    barrier, inc=1, device_id=self.device(axis, self.peer(axis, step)), device_id_type=MESH
                )
                count += 1
        pl.semaphore_wait(barrier, count)


def pieces_of(shards, width):
    out = []
    for a, shard in enumerate(shards):
        for lead in range(shard.shape[0]) if len(shard.shape) == 3 else (None,):
            for col in range(shard.shape[-1] // width):
                out.append((a, lead, col))
    return out


def piece(refs, which, width):
    a, lead, col = which
    ref = refs[a] if lead is None else refs[a].at[lead]
    spare = (slice(None),) * (len(ref.shape) - 1)
    return ref.at[(*spare, pl.ds(col * width, width))]


def whole_shape(weight):
    size = sizes()
    return (*weight.shape[:-2], *(size[a] for a in AXES), *weight.shape[-2:])


LEAD = 4


class Gather:
    def __init__(self, pieces, width, offsets, ins, outs, sems):
        self.here = Place()
        self.pieces, self.width, self.offsets, self.ins, self.outs = pieces, width, offsets, ins, outs
        self.send_sem, self.recv_sem, self.own_sem = sems
        self.half = ins[0].shape[-2] // 2
        self.count = len(pieces)

    def region(self, n, h, stage, axis=None, place=None):
        order = GATHER_ORDERS[h]
        index = [
            slice(None) if a in order[:stage] else place if a == axis else self.here.at[a] for a in AXES
        ]
        return piece(self.outs, self.pieces[n], self.width).at[(*index, pl.ds(h * self.half, self.half))]

    def remote(self, n, h, stage, step, coming=False):
        here, axis = self.here, GATHER_ORDERS[h][stage]
        slot = (n, h, stage, step - 1)
        to = source = self.region(n, h, stage)
        if stage == 0:
            source = piece(self.ins, self.pieces[n], self.width).at[pl.ds(h * self.half, self.half)]
        if coming:
            to = self.region(n, h, stage, axis, here.peer(axis, here.size[axis] - step))
        return pltpu.make_async_remote_copy(
            src_ref=source, dst_ref=to, send_sem=self.send_sem.at[slot], recv_sem=self.recv_sem.at[slot],
            device_id=here.device(axis, here.peer(axis, step)), device_id_type=MESH,
        )

    def every(self, n, stage):
        return [(n, h, stage, step) for h in range(2) for step in self.here.steps(GATHER_ORDERS[h][stage])]

    def start(self, n, stage):
        for slot in self.every(n, stage):
            self.remote(*slot).start()

    def arrived(self, n, stage=3):
        for slot in self.every(n, stage):
            self.remote(*slot, coming=True).wait_recv()

    def own(self, n):
        place = tuple(self.here.at[a] for a in AXES)
        return pltpu.make_async_copy(
            piece(self.ins, self.pieces[n], self.width),
            piece(self.outs, self.pieces[n], self.width).at[place], self.own_sem.at[n],
        )

    def begin(self):
        self.here.greet()
        for n in range(min(LEAD, self.count)):
            self.start(n, 0)
        for n in range(self.count):
            self.own(n).start()

    def ticks(self):
        return self.count + self.offsets[-1]

    def tick(self, k):
        if k + LEAD < self.count:
            self.start(k + LEAD, 0)
        for stage, offset in enumerate(self.offsets, 1):
            n = k - offset
            if 0 <= n < self.count:
                if stage == 1:
                    self.own(n).wait()
                self.arrived(n, stage - 1)
                self.start(n, stage)

    def end(self):
        for n in range(self.count):
            for stage in range(4):
                for slot in self.every(n, stage):
                    self.remote(*slot).wait_send()


class Share:
    def __init__(self, here, source, target, sems):
        self.here, self.source, self.target = here, source, target
        self.send_sem, self.recv_sem, self.own_sem = sems

    def remote(self, step, coming=False):
        here = self.here
        place = here.peer("tensor", here.size["tensor"] - step) if coming else here.at["tensor"]
        return pltpu.make_async_remote_copy(
            src_ref=self.source, dst_ref=self.target.at[place],
            send_sem=self.send_sem.at[step - 1], recv_sem=self.recv_sem.at[step - 1],
            device_id=here.device("tensor", here.peer("tensor", step)), device_id_type=MESH,
        )

    def own(self):
        return pltpu.make_async_copy(self.source, self.target.at[self.here.at["tensor"]], self.own_sem)

    def begin(self):
        self.own().start()
        for step in self.here.steps("tensor"):
            self.remote(step).start()

    def arrived(self):
        self.own().wait()
        for step in self.here.steps("tensor"):
            self.remote(step, coming=True).wait_recv()

    def end(self):
        for step in self.here.steps("tensor"):
            self.remote(step).wait_send()


SCATTER_ORDERS = (("tensor", "row", "line"), ("row", "tensor", "line"))
THREE = AXES[:3]


def late_shapes(count, rows, columns):
    size, out = sizes(), []
    for order in SCATTER_ORDERS:
        for stage in (1, 2, 3):
            free = [size[a] for a in THREE if a not in order[:stage]]
            out.append((count, size[order[stage - 1]] - 1, *free, rows // 2, columns))
    return out


def scatter_scratch(count, rows, columns):
    size = sizes()
    most = max(size.values()) - 1
    half_piece = (count, *(size[a] for a in THREE), rows, columns)
    return [
        pltpu.VMEM(half_piece, BF16),
        pltpu.VMEM(half_piece, BF16),
        *[pltpu.VMEM(dims, BF16) for dims in late_shapes(count, rows, columns)],
        pltpu.SemaphoreType.DMA((count, 2, 4, most)),
        pltpu.SemaphoreType.DMA((count, 2, 4, most)),
    ]


SCATTER_REFS = 10


def plus(terms):
    if len(terms) == 2:
        return terms[0] + terms[1]
    return sum(term.astype(F32) for term in terms).astype(BF16)


class Scatter:
    def __init__(self, here, staging, out, refs):
        self.here, self.staging, self.out = here, staging, out
        self.own, self.first, *late, self.send_sem, self.recv_sem = refs
        self.late = {(h, s): late[h * 3 + s - 1] for h in range(2) for s in (1, 2, 3)}
        self.half = self.own.shape[-2] // 2

    def to_core(self, n):
        here = self.here
        other = here.peer("core", 1)
        return pltpu.make_async_remote_copy(
            src_ref=self.staging(n).at[:, :, :, other], dst_ref=self.first.at[n],
            send_sem=self.send_sem.at[n, 0, 0, 0], recv_sem=self.recv_sem.at[n, 0, 0, 0],
            device_id=here.device("core", other), device_id_type=MESH,
        )

    def remote(self, n, h, stage, step):
        here, order = self.here, SCATTER_ORDERS[h]
        axis = order[stage - 1]
        to = here.peer(axis, step)
        index = [
            here.at[a] if a in order[: stage - 1] else to if a == axis else slice(None) for a in THREE
        ]
        slot = (n, h, stage, step - 1)
        return pltpu.make_async_remote_copy(
            src_ref=self.own.at[(n, *index, pl.ds(h * self.half, self.half))],
            dst_ref=self.late[h, stage].at[n, step - 1],
            send_sem=self.send_sem.at[slot], recv_sem=self.recv_sem.at[slot],
            device_id=here.device(axis, to), device_id_type=MESH,
        )

    def every(self, n, stage):
        return [
            self.remote(n, h, stage, step)
            for h in range(2)
            for step in self.here.steps(SCATTER_ORDERS[h][stage - 1])
        ]

    def add_core(self, n):
        source, core = self.staging(n), self.here.at["core"]
        for at in np.ndindex(self.own.shape[1:3]):
            self.own[(n, *at)] = plus([source[(*at, slice(None), core)], self.first[(n, *at)]])

    def add(self, n, h, stage):
        here, order = self.here, SCATTER_ORDERS[h]
        buf, steps = self.late[h, stage], here.size[order[stage - 1]] - 1
        free = [a for a in THREE if a not in order[:stage]]
        rows = pl.ds(h * self.half, self.half)
        for free_at in np.ndindex(*(here.size[a] for a in free)):
            at = {**here.at, **dict(zip(free, free_at, strict=True))}
            mine = (n, *(at[a] for a in THREE), rows)
            terms = [self.own[mine]] + [buf[(n, s, *free_at)] for s in range(steps)]
            if stage == 3:
                self.out(n)[rows, :] = sum(term.astype(F32) for term in terms)
            else:
                self.own[mine] = plus(terms)

    def begin(self, n):
        self.to_core(n).start()

    def tick(self, n, stage):
        if stage == 0:
            copy = self.to_core(n)
            copy.wait_recv()
            copy.wait_send()
            self.add_core(n)
        else:
            for copy in self.every(n, stage):
                copy.wait_recv()
            for h in range(2):
                self.add(n, h, stage)
        if stage < 3:
            for copy in self.every(n, stage + 1):
                copy.start()

    def end(self, count):
        def one(n, _):
            for stage in (1, 2, 3):
                for copy in self.every(n, stage):
                    copy.wait_send()
            return 0

        lax.fori_loop(0, count, one, 0)


SUM_AXES = ("core", "tensor", "row", "line")


class SmallSum:
    def __init__(self, here, refs):
        self.here = here
        *self.bufs, self.send_sem, self.recv_sem = refs

    @staticmethod
    def scratch(dims):
        size = sizes()
        most = max(size.values()) - 1
        return [
            *[pltpu.VMEM((size[a], *dims), F32) for a in SUM_AXES],
            pltpu.SemaphoreType.DMA((4, most)),
            pltpu.SemaphoreType.DMA((4, most)),
        ]

    def remote(self, stage, step, coming=False):
        here, axis, buf = self.here, SUM_AXES[stage], self.bufs[stage]
        place = here.peer(axis, here.size[axis] - step) if coming else here.at[axis]
        return pltpu.make_async_remote_copy(
            src_ref=buf.at[here.at[axis]], dst_ref=buf.at[place],
            send_sem=self.send_sem.at[stage, step - 1], recv_sem=self.recv_sem.at[stage, step - 1],
            device_id=here.device(axis, here.peer(axis, step)), device_id_type=MESH,
        )

    def start(self, stage, value):
        self.bufs[stage][self.here.at[SUM_AXES[stage]]] = value
        self.send(stage)

    def send(self, stage):
        for step in self.here.steps(SUM_AXES[stage]):
            self.remote(stage, step).start()

    def finish(self, stage):
        axis = SUM_AXES[stage]
        for step in self.here.steps(axis):
            self.remote(stage, step, coming=True).wait_recv()
            self.remote(stage, step).wait_send()
        total = self.bufs[stage][0]
        for place in range(1, self.here.size[axis]):
            total += self.bufs[stage][place]
        return total

    def tick(self, stage, target):
        total = self.finish(stage)
        if stage < 3:
            self.start(stage + 1, total)
        else:
            target[...] = total


SMALL_REFS = 6


def dot(left, right, left_dim=1, right_dim=0):
    return lax.dot_general(
        left, right, (((left_dim,), (right_dim,)), ((), ())), preferred_element_type=F32
    )


def side_by_side(ref, *lead):
    return jnp.concatenate([ref[(*lead, t)] for t in range(ref.shape[-3])], axis=-1)


def centred(rows):
    off = rows - jnp.mean(rows, axis=-1, keepdims=True)
    inverse = lax.rsqrt(jnp.mean(off * off, axis=-1, keepdims=True) + EPSILON)
    return off * inverse, inverse


def norm_back(grad, hat, inverse, gain):
    scaled = grad * gain
    along = jnp.mean(scaled * hat, axis=-1, keepdims=True)
    return inverse * (scaled - jnp.mean(scaled, axis=-1, keepdims=True) - hat * along)


def fold(rows):
    return jnp.sum(rows.reshape(-1, 8, rows.shape[-1]), axis=0)


def row_blocks(rows, size, one):
    def step(i, _):
        one(i, pl.ds(pl.multiple_of(i * size, size), size))
        return 0

    lax.fori_loop(0, rows // size, step, 0)


def transpose_into(source, target):
    rows = source.shape[0]
    for first in range(0, rows, 128):
        size = min(128, rows - first)
        target[:, first : first + size] = source[first : first + size, :].astype(F32).T.astype(BF16)


def two_heads(pair):
    first = lax.broadcasted_iota(jnp.int32, pair.shape, 1) < HD
    zero = jnp.zeros_like(pair)
    return jnp.concatenate([jnp.where(first, pair, zero), jnp.where(first, zero, pair)], axis=0)


def one_pair(stacked):
    first = lax.broadcasted_iota(jnp.int32, (SLOTS, PAIR), 1) < HD
    return jnp.where(first, stacked[:SLOTS], stacked[SLOTS:])


def masked_scores(query_stack, keys, length):
    scores = dot(keys, query_stack, 1, 1)
    slot = lax.broadcasted_iota(jnp.int32, scores.shape, 0)
    return jnp.where(slot < length, scores, MASKED_SCORE)


def group_weight(qkv_held, columns):
    parts = [qkv_held[e, t, ..., columns] for t in range(qkv_held.shape[1]) for e in range(3)]
    return jnp.concatenate([part.reshape(-1, PAIR) for part in parts], axis=-1)


def merge_tile(merge_held, columns):
    parts = [merge_held[t, ..., columns] for t in range(merge_held.shape[0])]
    return jnp.concatenate([part.reshape(-1, PAIR) for part in parts], axis=-1)


def schedule(ticks, last_piece, needed, steps):
    at = []
    first = needed.index(next(s for s in needed if s > 0), 0) if any(needed) else len(needed)
    early = first + last_piece
    for k in range(ticks):
        piece_done = k - last_piece
        even = 0 if k < early else 1 + (k - early) * (steps - 1) // (ticks - early)
        at.append(min(even, needed[max(piece_done, 0)]))
    for k in range(ticks - 2, -1, -1):
        at[k] = min(at[k], at[k + 1])
    return at


def forward_pieces(parts, width):
    pieces = pieces_of(parts, width)
    return sorted(pieces, key=lambda which: (max(which[0], 0) if which[0] < 2 else 2, which[2], which[0]))


def forward_kernel(
    width_of_piece, offsets, feed_columns,
    lengths, count, x_ref, teacher, gain, shift, merge_bias, gain_2, shift_2, reduce_bias,
    heads_bias, expand_bias, qkv_part, merge_part, expand_part, reduce_part,
    a_turned, qkv_ref, mixed_ref, log_ref, second_turned, activ, slope,
    out, grad_b, grad_turned, bias_grad, loss,
    hidden, grad, qkv_full, merge_full, expand_full, reduce_full,
    hidden_ref, second_ref, a_ref, qkv_held, merge_held, tiles, heads_bias_all, expand_bias_all,
    send_sem, recv_sem, own_sem, share_send, share_recv, share_own, held_sem, tile_sem, keep_sem,
):
    now = pl.program_id(0)
    rows = x_ref.shape[0]
    images = rows // SLOTS
    halves = qkv_held.shape[1]
    groups = width_of_piece // PAIR
    attention_steps = groups * images
    feed_steps = expand_part.shape[1] // feed_columns
    steps = attention_steps + feed_steps
    parts = [qkv_part, merge_part, expand_part, reduce_part]
    pieces = forward_pieces(parts, width_of_piece)
    gather = Gather(
        pieces, width_of_piece, offsets, parts, [qkv_full, merge_full, expand_full, reduce_full],
        (send_sem, recv_sem, own_sem),
    )
    shares = [
        Share(gather.here, source, target, (share_send.at[n], share_recv.at[n], share_own.at[n]))
        for n, (source, target) in enumerate([(heads_bias, heads_bias_all), (expand_bias, expand_bias_all)])
    ]
    tiles_of_piece = width_of_piece // feed_columns
    needed = [
        0 if a == 0 else images - 1 if a == 1 else max(attention_steps + col * tiles_of_piece - 1, 0)
        for a, _, col in pieces
    ]
    when = schedule(gather.ticks(), offsets[-1], needed, steps)
    image = lax.rem(now, images)
    group = lax.min(lax.div(now, images), groups - 1)
    columns = pl.ds(pl.multiple_of(group * PAIR, PAIR), PAIR)

    def hold(n):
        a, lead, _ = pieces[n]
        source, target = (qkv_full.at[lead], qkv_held.at[lead]) if a == 0 else (merge_full, merge_held)
        return pltpu.make_async_copy(source, target, held_sem.at[n])

    def tile_copies(j):
        block = pl.ds(j * feed_columns, feed_columns)
        return [
            pltpu.make_async_copy(
                full.at[:, :, :, :, :, block], tiles.at[j % 2, kind], tile_sem.at[j % 2, kind]
            )
            for kind, full in enumerate((expand_full, reduce_full))
        ]

    def fetch_tiles(j):
        for kind, copy in enumerate(tile_copies(j)):
            if j % tiles_of_piece == 0:
                gather.arrived(4 + 2 * (j // tiles_of_piece) + kind)
            copy.start()

    def keep_hidden():
        return pltpu.make_async_copy(hidden_ref, hidden, keep_sem)

    @pl.when(now == 0)
    def _():
        gather.begin()
        for share in shares:
            share.begin()
        early = [k for k in range(gather.ticks()) if when[k] == 0]
        blocks = rows // BLOCK
        per = -(-blocks // max(len(early), 1))

        def norm(i, _):
            at = pl.ds(pl.multiple_of(i * BLOCK, BLOCK), BLOCK)
            x = x_ref[at, :].astype(F32)
            hidden_ref[at, :] = x + merge_bias[...]
            a_ref[at, :] = (centred(x)[0] * gain[...] + shift[...]).astype(BF16)
            return 0

        done = 0
        for k in early:
            lax.fori_loop(done, min(done + per, blocks), norm, 0)
            done = min(done + per, blocks)
            gather.tick(k)
            n = k - offsets[-1] - 1
            if 0 <= n < 3:
                gather.arrived(n)
                hold(n).start()
        lax.fori_loop(done, blocks, norm, 0)
        transpose_into(a_ref, a_turned)
        for n in range(max(len(early) - offsets[-1] - 1, 0), 3):
            gather.arrived(n)
            hold(n).start()
        for share in shares:
            share.arrived()
        for n in range(3):
            hold(n).wait()

    for k in range(gather.ticks()):
        if when[k] > 0:
            pl.when(now == when[k])(partial(gather.tick, k))

    @pl.when((now < attention_steps) & (image == 0))
    def _():
        weight = group_weight(qkv_held, columns)
        bias = []
        for t in range(halves):
            query = heads_bias_all[t, 0:1, columns]
            bias += [query, jnp.zeros_like(query), heads_bias_all[t, 1:2, columns]]
        bias = jnp.concatenate(bias, axis=-1)
        for i in range(images):
            at = slice(i * SLOTS, (i + 1) * SLOTS)
            out = (dot(a_ref[at, :], weight) + bias).astype(BF16)
            for t in range(halves):
                query = slice(t * 3 * PAIR, (t * 3 + 1) * PAIR)
                qkv_ref[0, at, query] = out[:, query] * 0.125
                rest = slice((t * 3 + 1) * PAIR, (t * 3 + 3) * PAIR)
                qkv_ref[0, at, rest] = out[:, rest]

    @pl.when(now < attention_steps)
    def _():
        length = lengths[image]
        at = pl.ds(pl.multiple_of(image * SLOTS, SLOTS), SLOTS)
        for t in range(halves):
            first = t * 3 * PAIR
            query_stack = two_heads(qkv_ref[0, at, first : first + PAIR])
            scores = masked_scores(query_stack, qkv_ref[0, at, first + PAIR : first + 2 * PAIR], length)
            highest = jnp.max(scores, axis=0, keepdims=True)
            expo = jnp.exp(scores - highest)
            totals = jnp.sum(expo, axis=0, keepdims=True)
            values = qkv_ref[0, at, first + 2 * PAIR : first + 3 * PAIR]
            mixed = dot(values, expo.astype(BF16), 0, 0) * (1.0 / totals)
            mixed_ref[0, at, t * PAIR : (t + 1) * PAIR] = one_pair(mixed.T).astype(BF16)
            log_ref[0, 0, t : t + 1] = highest + jnp.log(totals)

    @pl.when(now == images - 1)
    def _():
        gather.arrived(3)
        hold(3).start()
        hold(3).wait()

    @pl.when((now < attention_steps) & (image == images - 1))
    def _():
        weight = merge_tile(merge_held, columns)
        for i in range(images):
            part = slice(i * SLOTS, (i + 1) * SLOTS)
            hidden_ref[part, :] += dot(mixed_ref[0, part, :], weight, 1, 1)

    @pl.when(now == attention_steps - 1)
    def _():
        keep_hidden().start()
        fetch_tiles(0)

        def norm(_, at):
            hat, _ = centred(hidden_ref[at, :])
            second_ref[at, :] = (hat * gain_2[...] + shift_2[...]).astype(BF16)

        row_blocks(rows, BLOCK, norm)
        transpose_into(second_ref, second_turned)

    for j in range(feed_steps):

        @pl.when(now == attention_steps + j)
        def _(j=j):
            if j == 0:
                keep_hidden().wait()
            for copy in tile_copies(j):
                copy.wait()
            if j + 1 < feed_steps:
                fetch_tiles(j + 1)

    @pl.when(now >= attention_steps)
    def _():
        j = now - attention_steps
        block = pl.ds(pl.multiple_of(j * feed_columns, feed_columns), feed_columns)
        slot = lax.rem(j, 2)
        weight, reduce_tile = (
            jnp.concatenate([tiles[slot, kind, t].reshape(-1, feed_columns) for t in range(halves)], axis=-1)
            for kind in range(2)
        )
        bias = jnp.concatenate([expand_bias_all[t, :, block] for t in range(halves)], axis=-1)
        for i in range(images):
            at = slice(i * SLOTS, (i + 1) * SLOTS)
            z = dot(second_ref[at, :], weight) + bias
            square = z * z
            bend = jnp.tanh(0.7978845608 * z * (1.0 + 0.044715 * square))
            half = 0.5 + 0.5 * bend
            act = (z * half).astype(BF16)
            activ[0, at, :] = act
            inner = 0.7978845608 * z * (1.0 + (3 * 0.044715) * square)
            slope[0, at, :] = (half + 0.5 * inner * (1.0 - bend * bend)).astype(BF16)
            hidden_ref[at, :] += dot(act, reduce_tile, 1, 1)

    @pl.when(now == steps - 1)
    def _():
        bias_grad[...] = jnp.zeros_like(bias_grad)
        loss[...] = jnp.zeros_like(loss)

        def end(i, at):
            image, block = lax.div(i, SLOTS // BLOCK), lax.rem(i, SLOTS // BLOCK)
            slot = block * BLOCK + lax.broadcasted_iota(jnp.int32, (BLOCK, 1), 0)
            valid = slot < lengths[image]
            result = jnp.where(valid, hidden_ref[at, :] + reduce_bias[...], 0.0)
            out[at, :] = result.astype(BF16)
            error = jnp.where(valid, result - teacher[at, :].astype(F32), 0.0)
            loss[0] += fold(error * error)
            back = 2.0 * error / count[0]
            bias_grad[0] += fold(back)
            hidden_ref[at, :] = back
            grad_b[at, :] = back.astype(BF16)

        row_blocks(rows, BLOCK, end)
        keep = pltpu.make_async_copy(hidden_ref, grad, keep_sem)
        keep.start()
        transpose_into(grad_b, grad_turned)
        keep.wait()
        gather.end()
        for share in shares:
            share.end()


def feed_back_kernel(
    result_b, result_turned, second_turned, expand, reduce, activ, slope, hidden, result_grad, gain,
    reduce_grad, expand_grad, expand_bias_grad, hidden_grad, hidden_b, hidden_turned, sums,
    total, staging, *scatter_refs,
):
    step, steps = pl.program_id(0), reduce_grad.shape[1] // expand.shape[-1]
    rows, width = result_b.shape
    halves, _, columns = expand.shape
    expand_tile, reduce_tile = side_by_side(expand), side_by_side(reduce)

    scatters = []
    here = Place()
    for p, target in enumerate((reduce_grad, expand_grad)):
        slot = lambda j, p=p: staging.at[lax.rem(j, 2), p]
        part = lambda j, target=target: target.at[:, pl.ds(pl.multiple_of(j * columns, columns), columns)]
        scatters.append(Scatter(here, slot, part, scatter_refs[p * SCATTER_REFS : (p + 1) * SCATTER_REFS]))

    @pl.when(step == 0)
    def _():
        here.greet()
        total[...] = jnp.zeros_like(total)

    def ticks(p, back):
        for stage in range(3, -1, -1):

            @pl.when(step >= stage + back)
            def _(stage=stage):
                scatters[p].tick(step - back - stage, stage)

    def stage_out(p, part):
        for t in range(halves):
            block = part[:, t * columns : (t + 1) * columns].astype(BF16)
            staging[lax.rem(step, 2), p, t] = block.reshape(staging.shape[3:])
        scatters[p].begin(step)

    stage_out(0, dot(result_turned[...], activ[0]))
    ticks(1, 1)
    bias = jnp.zeros((8, halves * columns), F32)
    parts = []
    for i in range(rows // SLOTS):
        at = slice(i * SLOTS, (i + 1) * SLOTS)
        z_grad = (dot(result_b[at, :], reduce_tile) * slope[0, at, :].astype(F32)).astype(BF16)
        bias += fold(z_grad.astype(F32))
        parts.append(z_grad)
        total[at, :] += dot(z_grad, expand_tile, 1, 1)
    expand_bias_grad[0] = jnp.sum(bias, axis=0, keepdims=True)
    ticks(0, 0)
    stage_out(1, dot(second_turned[...], jnp.concatenate(parts, axis=0)))

    @pl.when(step == steps - 1)
    def _():
        sums[...] = jnp.zeros_like(sums)
        size = 128 if rows % 128 == 0 else rows
        blocks = rows // size

        def end(first, h_ref, g_ref, back_ref, back_b_ref, turned_ref):
            block = pl.program_id(0) + first
            for k in range(0, size, 32):
                at = slice(k, k + 32)
                hat, inverse = centred(h_ref[at, :])
                second_grad = total[pl.ds(pl.multiple_of(block * size + k, 32), 32), :]
                back = g_ref[at, :] + norm_back(second_grad, hat, inverse, gain[...])
                sums[0] += fold(second_grad * hat)
                sums[1] += fold(second_grad)
                sums[2] += fold(back)
                back_ref[at, :] = back
                back_b_ref[at, :] = back.astype(BF16)
            turned_ref[...] = back_ref[...].T.astype(BF16)

        def some(first, last):
            row_block = pl.BlockSpec((size, width), lambda i: (i + first, 0))
            pltpu.emit_pipeline(
                partial(end, first),
                grid=(last - first,),
                in_specs=[row_block, row_block],
                out_specs=[row_block, row_block, pl.BlockSpec((width, size), lambda i: (0, i + first))],
            )(hidden, result_grad, hidden_grad, hidden_b, hidden_turned)

        bounds = [blocks * k // 3 for k in range(4)]
        for drain in range(4):
            for stage in range(3, -1, -1):
                for p, first in ((0, drain + 1), (1, drain)):
                    n = steps + first - 1 - stage
                    if stage >= first and n >= 0:
                        scatters[p].tick(n, stage)
            if drain < 3 and bounds[drain + 1] > bounds[drain]:
                some(bounds[drain], bounds[drain + 1])
        for scatter in scatters:
            scatter.end(steps)


def attend_back_kernel(
    lengths, a_turned, hidden_b, hidden_turned, qkv_ref, mixed_ref, log_ref, x_ref, hidden_grad, gain,
    qkv_weight, merge_weight, second_sums, reduce_bias_grad, loss, expand_bias_grad,
    merge_grad, qkv_grad, inputs_grad, early_out, expand_out, late_out, heads_out,
    mixed_grad, heads_grad, total, qkv_held, merge_held, sem, merge_staging, qkv_staging, sums, bias_grad,
    *comm,
):
    now = pl.program_id(0)
    rows = x_ref.shape[0]
    images = rows // SLOTS
    halves = qkv_held.shape[1]
    groups = merge_grad.shape[1] // PAIR
    steps = groups * images
    group, image = lax.div(now, images), lax.rem(now, images)
    here = Place()
    block = lambda c: pl.ds(pl.multiple_of(c * PAIR, PAIR), PAIR)
    merge_scatter = Scatter(here, lambda n: merge_staging, lambda n: merge_grad.at[:, block(n)], comm[:SCATTER_REFS])
    qkv_scatter = Scatter(
        here, lambda n: qkv_staging.at[lax.rem(n, 3)],
        lambda n: qkv_grad.at[lax.rem(n, 3), :, block(lax.div(n, 3))], comm[SCATTER_REFS : 2 * SCATTER_REFS],
    )
    early, expand_sum, late, heads_sum = (
        SmallSum(here, comm[2 * SCATTER_REFS + k * SMALL_REFS :][:SMALL_REFS]) for k in range(4)
    )

    def qkv_tick(c, stage):
        for e in range(3):
            qkv_scatter.tick(3 * c + e, stage)
    columns = pl.ds(pl.multiple_of(group * PAIR, PAIR), PAIR)

    @pl.when(now == 0)
    def _():
        copies = [
            pltpu.make_async_copy(merge_weight, merge_held, sem.at[1]),
            pltpu.make_async_copy(qkv_weight, qkv_held, sem.at[0]),
        ]
        for copy in copies:
            copy.start()
        here.greet()
        total[...] = jnp.zeros_like(total)
        rowsum = lambda ref, k: jnp.sum(ref[k], axis=0, keepdims=True)
        vectors = [rowsum(second_sums, k) for k in range(3)] + [rowsum(reduce_bias_grad, 0)]
        lost = jnp.sum(rowsum(loss, 0), axis=1, keepdims=True)
        vectors.append(jnp.broadcast_to(lost, vectors[0].shape))
        early.start(0, jnp.concatenate(vectors, axis=0))
        expand_sum.start(0, expand_bias_grad[:, 0])
        for copy in copies:
            copy.wait()

    @pl.when(image == 0)
    def _():
        weight = merge_tile(merge_held, columns)
        for i in range(rows // SLOTS):
            part = slice(i * SLOTS, (i + 1) * SLOTS)
            mixed_grad[part, :] = dot(hidden_b[part, :], weight).astype(BF16)
        part = dot(hidden_turned[...], mixed_ref[0]).astype(BF16)
        for t in range(halves):
            merge_staging[t] = part[:, t * PAIR : (t + 1) * PAIR].reshape(merge_staging.shape[1:])
        merge_scatter.begin(group)

        @pl.when(group == 0)
        def _():
            early.tick(0, early_out)
            expand_sum.tick(0, expand_out)

        @pl.when(group > 0)
        def _():
            merge_scatter.tick(group - 1, 2)
            qkv_tick(group - 1, 1)

    length = lengths[image]
    at = pl.ds(pl.multiple_of(image * SLOTS, SLOTS), SLOTS)
    for t in range(halves):
        first = t * 3 * PAIR
        query_stack = two_heads(qkv_ref[0, at, first : first + PAIR])
        keys = qkv_ref[0, at, first + PAIR : first + 2 * PAIR]
        values = qkv_ref[0, at, first + 2 * PAIR : first + 3 * PAIR]
        scores = masked_scores(query_stack, keys, length)
        attend = jnp.exp(scores - log_ref[0, 0, t : t + 1])
        grad_stack = two_heads(mixed_grad[at, t * PAIR : (t + 1) * PAIR])
        attend_grad = dot(values, grad_stack, 1, 1)
        value_grad = dot(attend.astype(BF16), grad_stack).astype(BF16)
        centre = jnp.sum(attend * attend_grad, axis=0, keepdims=True)
        score_grad = (attend * (attend_grad - centre)).astype(BF16)
        key_grad = dot(score_grad, query_stack).astype(BF16)
        query_grad = dot(keys, score_grad, 0, 0)
        query_grad = (one_pair(query_grad.T) * 0.125).astype(BF16)
        heads_grad[at, first : first + PAIR] = query_grad
        heads_grad[at, first + PAIR : first + 2 * PAIR] = key_grad
        heads_grad[at, first + 2 * PAIR : first + 3 * PAIR] = value_grad

    @pl.when(image == images - 1)
    def _():
        @pl.when(group == 0)
        def _():
            early.tick(1, early_out)
            expand_sum.tick(1, expand_out)

        @pl.when(group > 0)
        def _():
            merge_scatter.tick(group - 1, 3)
            qkv_tick(group - 1, 2)

        merge_scatter.tick(group, 0)
        weight = group_weight(qkv_held, columns)
        bias = jnp.zeros((8, halves * 3 * PAIR), F32)
        for i in range(rows // SLOTS):
            part = slice(i * SLOTS, (i + 1) * SLOTS)
            bias += fold(heads_grad[part, :].astype(F32))
        bias_grad[pl.ds(group, 1), :] = jnp.sum(bias, axis=0, keepdims=True)
        part = dot(a_turned[...], heads_grad[...]).astype(BF16)
        for t in range(halves):
            for e in range(3):
                first = (t * 3 + e) * PAIR
                qkv_staging[e, t] = part[:, first : first + PAIR].reshape(qkv_staging.shape[2:])
        for e in range(3):
            qkv_scatter.begin(3 * group + e)
        for i in range(rows // SLOTS):
            part = slice(i * SLOTS, (i + 1) * SLOTS)
            total[part, :] += dot(heads_grad[part, :], weight, 1, 1)

        @pl.when(group == 0)
        def _():
            early.tick(2, early_out)
            expand_sum.tick(2, expand_out)

        @pl.when(group > 0)
        def _():
            qkv_tick(group - 1, 3)

        merge_scatter.tick(group, 1)
        qkv_tick(group, 0)

    @pl.when(now == steps - 1)
    def _():
        heads_sum.start(0, bias_grad[...])
        sums[...] = jnp.zeros_like(sums)

        def end(i, _):
            at = pl.ds(pl.multiple_of(i * BLOCK, BLOCK), BLOCK)
            hat, inverse = centred(x_ref[at, :].astype(F32))
            grad = total[at, :]
            sums[0] += fold(grad * hat)
            sums[1] += fold(grad)
            inputs_grad[at, :] = hidden_grad[at, :] + norm_back(grad, hat, inverse, gain[...])
            return 0

        blocks = rows // BLOCK
        last = groups - 1
        lax.fori_loop(0, blocks // 2, end, 0)
        merge_scatter.tick(last, 2)
        qkv_tick(last, 1)
        early.tick(3, early_out)
        expand_sum.tick(3, expand_out)
        heads_sum.tick(0, heads_out)
        lax.fori_loop(blocks // 2, blocks, end, 0)
        late.start(0, jnp.sum(sums[...], axis=1))
        merge_scatter.tick(last, 3)
        qkv_tick(last, 2)
        heads_sum.tick(1, heads_out)
        late.tick(0, late_out)
        qkv_tick(last, 3)
        heads_sum.tick(2, heads_out)
        late.tick(1, late_out)
        heads_sum.tick(3, heads_out)
        late.tick(2, late_out)
        late.tick(3, late_out)
        merge_scatter.end(groups)
        qkv_scatter.end(3 * groups)


def shape(dims, kind=BF16):
    return jax.ShapeDtypeStruct(dims, kind)


def once(dims):
    return pl.BlockSpec(dims, lambda *_: (0,) * len(dims), pipeline_mode=pl.Buffered(1))


ELSEWHERE = pl.BlockSpec(memory_space=pl.ANY)
SCALARS = pl.BlockSpec(memory_space=pltpu.SMEM)
LIMIT = 63 * 2**20


OFFSETS = (0, 1, 2)


def feed_width(halves):
    return max(PAIR, 512 // halves)


def forward(
    lengths, count, x, teacher, gain, shift, merge_bias, gain_2, shift_2, reduce_bias, heads_bias, expand_bias, parts
):
    rows, width = x.shape
    halves, columns = lax.axis_size("tensor"), parts[0].shape[2]
    groups, images = columns // PAIR, rows // SLOTS
    attention_steps = groups * images
    feed_columns = feed_width(halves)
    feed_steps = parts[2].shape[1] // feed_columns
    pieces = len(pieces_of(parts, columns))
    most = max(sizes().values()) - 1
    line, whole, turned = once((1, width)), once((rows, width)), once((width, rows))
    group_at = lambda s: lax.min(lax.div(s, images), groups - 1)
    feed_at = lambda s: lax.max(s - attention_steps, 0)
    wholes = [whole_shape(part) for part in parts]
    saved = pl.BlockSpec((1, rows, halves * feed_columns), lambda s: (feed_at(s), 0, 0))
    return pl.pallas_call(
        partial(forward_kernel, columns, OFFSETS, feed_columns),
        grid=(attention_steps + feed_steps,),
        in_specs=[
            SCALARS, SCALARS, whole, whole, *[line] * 6, *[ELSEWHERE] * 2, *[once(part.shape) for part in parts]
        ],
        out_specs=[
            turned,
            pl.BlockSpec((1, rows, halves * 3 * PAIR), lambda s: (group_at(s), 0, 0)),
            pl.BlockSpec((1, rows, halves * PAIR), lambda s: (group_at(s), 0, 0)),
            pl.BlockSpec(
                (1, 1, halves, 2 * SLOTS),
                lambda s: (group_at(s), jnp.where(s < attention_steps, lax.rem(s, images), images - 1), 0, 0),
            ),
            turned, saved, saved, whole, whole, turned, once((1, 8, width)), once((1, 8, width)),
            *[ELSEWHERE] * 6,
        ],
        out_shape=[
            shape((width, rows)),
            shape((groups, rows, halves * 3 * PAIR)),
            shape((groups, rows, halves * PAIR)),
            shape((groups, images, halves, 2 * SLOTS), F32),
            shape((width, rows)),
            *[shape((feed_steps, rows, halves * feed_columns))] * 2,
            shape((rows, width)), shape((rows, width)), shape((width, rows)),
            shape((1, 8, width), F32), shape((1, 8, width), F32),
            shape((rows, width), F32), shape((rows, width), F32),
            *[shape(dims) for dims in wholes],
        ],
        scratch_shapes=[
            pltpu.VMEM((rows, width), F32),
            pltpu.VMEM((rows, width), BF16),
            pltpu.VMEM((rows, width), BF16),
            pltpu.VMEM(wholes[0], BF16),
            pltpu.VMEM(wholes[1], BF16),
            pltpu.VMEM((2, 2, *wholes[2][:-1], feed_columns), BF16),
            pltpu.VMEM((halves, *heads_bias.shape), F32),
            pltpu.VMEM((halves, *expand_bias.shape), F32),
            pltpu.SemaphoreType.DMA((pieces, 2, 4, most)),
            pltpu.SemaphoreType.DMA((pieces, 2, 4, most)),
            pltpu.SemaphoreType.DMA((pieces,)),
            pltpu.SemaphoreType.DMA((2, halves)),
            pltpu.SemaphoreType.DMA((2, halves)),
            pltpu.SemaphoreType.DMA((2,)),
            pltpu.SemaphoreType.DMA((4,)),
            pltpu.SemaphoreType.DMA((2, 2)),
            pltpu.SemaphoreType.DMA(()),
        ],
        compiler_params=pltpu.CompilerParams(
            vmem_limit_bytes=LIMIT, collective_id=0, has_side_effects=True
        ),
        name="forward",
    )(
        lengths, count, x, teacher, gain, shift, merge_bias, gain_2, shift_2, reduce_bias,
        heads_bias, expand_bias, *parts,
    )


def feed_back(result_b, result_turned, second_turned, expand, reduce, activ, slope, hidden, result_grad, gain):
    rows, width = result_b.shape
    halves, _, wide = expand.shape
    steps, columns = activ.shape[0], activ.shape[2] // halves
    size = sizes()
    part_rows = width // math.prod(size[a] for a in ("line", "row", "core"))
    tile = pl.BlockSpec((halves, width, columns), lambda j: (0, 0, j))
    saved = pl.BlockSpec((1, rows, halves * columns), lambda j: (j, 0, 0))
    whole, turned, part = once((rows, width)), once((width, rows)), once((part_rows, wide))
    return pl.pallas_call(
        feed_back_kernel,
        grid=(steps,),
        in_specs=[whole, turned, turned, tile, tile, saved, saved, ELSEWHERE, ELSEWHERE, once((1, width))],
        out_specs=[
            part, part, pl.BlockSpec((1, 1, halves * columns), lambda j: (j, 0, 0)),
            ELSEWHERE, ELSEWHERE, ELSEWHERE, once((3, 8, width)),
        ],
        out_shape=[
            shape((part_rows, wide), F32), shape((part_rows, wide), F32),
            shape((steps, 1, halves * columns), F32),
            shape((rows, width), F32), shape((rows, width)), shape((width, rows)), shape((3, 8, width), F32),
        ],
        scratch_shapes=[
            pltpu.VMEM((rows, width), F32),
            pltpu.VMEM((2, 2, *(size[a] for a in AXES), part_rows, columns), BF16),
            *scatter_scratch(steps, part_rows, columns),
            *scatter_scratch(steps, part_rows, columns),
        ],
        compiler_params=pltpu.CompilerParams(
            vmem_limit_bytes=LIMIT, collective_id=1, has_side_effects=True
        ),
        name="feed_back",
    )(result_b, result_turned, second_turned, expand, reduce, activ, slope, hidden, result_grad, gain)


def attend_back(
    lengths, a_turned, hidden_b, hidden_turned, qkv, mixed, log_total, x, hidden_grad, gain,
    qkv_whole, merge_whole, second_sums, reduce_bias_grad, loss, expand_bias_grad,
):
    rows, width = x.shape
    halves, (part_rows, columns) = qkv_whole.shape[1], qkv_whole.shape[-2:]
    groups, images = columns // PAIR, rows // SLOTS
    whole, turned = once((rows, width)), once((width, rows))
    group_at = lambda s: lax.div(s, images)
    size = sizes()
    staging = (*(size[a] for a in AXES), part_rows, PAIR)
    small = [(5, width), (expand_bias_grad.shape[0], expand_bias_grad.shape[2]), (2, width), (groups, halves * 3 * PAIR)]
    vmem = lambda array: once(array.shape)
    return pl.pallas_call(
        attend_back_kernel,
        grid=(groups * images,),
        in_specs=[
            SCALARS, turned, whole, turned,
            pl.BlockSpec((1, rows, halves * 3 * PAIR), lambda s: (group_at(s), 0, 0)),
            pl.BlockSpec((1, rows, halves * PAIR), lambda s: (group_at(s), 0, 0)),
            pl.BlockSpec((1, 1, halves, 2 * SLOTS), lambda s: (group_at(s), lax.rem(s, images), 0, 0)),
            whole, whole, once((1, width)), ELSEWHERE, ELSEWHERE,
            vmem(second_sums), vmem(reduce_bias_grad), vmem(loss), vmem(expand_bias_grad),
        ],
        out_specs=[
            once((part_rows, columns)), once((3, part_rows, columns)), whole, *[once(dims) for dims in small]
        ],
        out_shape=[
            shape((part_rows, columns), F32), shape((3, part_rows, columns), F32), shape((rows, width), F32),
            *[shape(dims, F32) for dims in small],
        ],
        scratch_shapes=[
            pltpu.VMEM((rows, halves * PAIR), BF16),
            pltpu.VMEM((rows, halves * 3 * PAIR), BF16),
            pltpu.VMEM((rows, width), F32),
            pltpu.VMEM(qkv_whole.shape, BF16),
            pltpu.VMEM(merge_whole.shape, BF16),
            pltpu.SemaphoreType.DMA((2,)),
            pltpu.VMEM(staging, BF16),
            pltpu.VMEM((3, *staging), BF16),
            pltpu.VMEM((2, 8, width), F32),
            pltpu.VMEM((groups, halves * 3 * PAIR), F32),
            *scatter_scratch(groups, part_rows, PAIR),
            *scatter_scratch(3 * groups, part_rows, PAIR),
            *[ref for dims in small for ref in SmallSum.scratch(dims)],
        ],
        compiler_params=pltpu.CompilerParams(
            vmem_limit_bytes=LIMIT, collective_id=2, has_side_effects=True
        ),
        name="attend_back",
    )(
        lengths, a_turned, hidden_b, hidden_turned, qkv, mixed, log_total, x, hidden_grad, gain,
        qkv_whole, merge_whole, second_sums, reduce_bias_grad, loss, expand_bias_grad,
    )


def finish_kernel(count, early, late, expand_sum, heads_sum, *refs):
    arrays = (len(refs) - 10) // 2
    sources, targets = refs[:arrays], refs[arrays : 2 * arrays]
    loss, first_gain, first_shift, second_gain, second_shift, merge_bias, reduce_bias, heads_bias, expand_bias, sem = (
        refs[2 * arrays :]
    )
    copies = [
        pltpu.make_async_copy(source, target, sem.at[n])
        for n, (source, target) in enumerate(zip(sources, targets, strict=True))
    ]
    for copy in copies:
        copy.start()
    tensor = lax.axis_index("tensor")
    loss[...] = early[4:5, 0:1] / count[0]
    for k, target in enumerate((second_gain, second_shift, merge_bias, reduce_bias)):
        target[...] = early[k : k + 1]
    first_gain[...] = late[0:1]
    first_shift[...] = late[1:2]
    for k, e in enumerate((0, 2)):
        columns = pl.ds(pl.multiple_of((tensor * 3 + e) * PAIR, PAIR), PAIR)
        for group in range(heads_sum.shape[0]):
            heads_bias[k : k + 1, group * PAIR : (group + 1) * PAIR] = heads_sum[group : group + 1, columns]
    wide = expand_bias.shape[1] // expand_sum.shape[0]
    columns = pl.ds(pl.multiple_of(tensor * wide, wide), wide)
    for step in range(expand_sum.shape[0]):
        expand_bias[:, step * wide : (step + 1) * wide] = expand_sum[step : step + 1, columns]
    for copy in copies:
        copy.wait()


def finish(count, early, late, expand_sum, heads_sum, arrays):
    width, halves = early.shape[1], lax.axis_size("tensor")
    small = [(1, 1), *[(1, width)] * 6, (2, heads_sum.shape[0] * PAIR), (1, expand_sum.size // halves)]
    vmem = pl.BlockSpec(memory_space=pltpu.VMEM)
    return pl.pallas_call(
        finish_kernel,
        in_specs=[SCALARS, *[vmem] * (4 + len(arrays))],
        out_specs=[*[ELSEWHERE] * len(arrays), *[vmem] * len(small)],
        out_shape=[*[shape(a.shape, a.dtype) for a in arrays], *[shape(dims, F32) for dims in small]],
        scratch_shapes=[pltpu.SemaphoreType.DMA((len(arrays),))],
        compiler_params=pltpu.CompilerParams(vmem_limit_bytes=LIMIT),
        name="finish",
    )(count, early, late, expand_sum, heads_sum, *arrays)


def body(
    inputs,
    teacher,
    lengths,
    first_gain,
    first_shift,
    query_key_value_weight,
    heads_bias,
    merge_weight,
    merge_bias,
    second_gain,
    second_shift,
    expand_weight,
    expand_bias,
    reduce_weight,
    reduce_bias,
):
    rows, width = inputs.shape
    images = rows // SLOTS
    halves = lax.axis_size("tensor")
    tensor = lax.axis_index("tensor")
    hidden = expand_weight.shape[1] * halves
    piece_width = query_key_value_weight.shape[-1]
    groups = piece_width // PAIR
    place = lax.axis_index("dp") * halves + tensor
    mine = lax.dynamic_slice_in_dim(lengths, place * images, images)
    count = jnp.sum(lengths).astype(F32).reshape(1)
    line = lambda vector: vector.reshape(1, width)

    (
        a_turned, qkv, mixed, log_total, second_turned, activ, slope, outputs, result_b, result_turned,
        reduce_bias_grad, loss, hidden_state, result_grad, *wholes,
    ) = forward(
        mine, count, inputs, teacher, line(first_gain), line(first_shift), line(merge_bias),
        line(second_gain), line(second_shift), line(reduce_bias), heads_bias, expand_bias.reshape(1, -1),
        [query_key_value_weight, merge_weight, expand_weight, reduce_weight],
    )
    expand_full, reduce_full = (whole.reshape(halves, width, -1) for whole in wholes[2:])
    columns = feed_width(halves)
    steps = hidden // halves // columns
    reduce_grad, expand_grad, expand_bias_grad, hidden_grad, hidden_b, hidden_turned, second_sums = feed_back(
        result_b, result_turned, second_turned, expand_full, reduce_full, activ, slope, hidden_state,
        result_grad, line(second_gain),
    )
    merge_grad, heads_grad, inputs_grad, early, expand_sum, late, heads_sum = attend_back(
        mine, a_turned, hidden_b, hidden_turned, qkv, mixed, log_total, inputs, hidden_grad,
        line(first_gain), wholes[0], wholes[1], second_sums, reduce_bias_grad, loss, expand_bias_grad,
    )
    outputs, inputs_grad, heads_grad, merge_grad, expand_grad, reduce_grad, loss, *vectors, heads_sum, expand_sum = finish(
        count, early, late, expand_sum, heads_sum,
        [outputs, inputs_grad, heads_grad, merge_grad, expand_grad, reduce_grad],
    )
    first_gain_grad, first_shift_grad, second_gain_grad, second_shift_grad, merge_bias_grad, reduce_bias_grad = (
        vector.reshape(width) for vector in vectors
    )
    return (
        loss.reshape(()),
        outputs,
        inputs_grad,
        first_gain_grad,
        first_shift_grad,
        heads_grad,
        heads_sum,
        merge_grad,
        merge_bias_grad,
        second_gain_grad,
        second_shift_grad,
        expand_grad,
        expand_sum.reshape(-1),
        reduce_grad,
        reduce_bias_grad,
    )


def solution(mesh):
    return jax.shard_map(
        body,
        mesh=mesh,
        in_specs=(
            P(("dp", "tensor"), None),
            P(("dp", "tensor"), None),
            P(),
            P(),
            P(),
            P(None, "dp", "tensor"),
            P(None, "tensor"),
            P("dp", "tensor"),
            P(),
            P(),
            P(),
            P("dp", "tensor"),
            P("tensor"),
            P("dp", "tensor"),
            P(),
        ),
        out_specs=(
            P(),
            P(("dp", "tensor"), None),
            P(("dp", "tensor"), None),
            P(),
            P(),
            P(None, "dp", "tensor"),
            P(None, "tensor"),
            P("dp", "tensor"),
            P(),
            P(),
            P(),
            P("dp", "tensor"),
            P("tensor"),
            P("dp", "tensor"),
            P(),
        ),
        check_vma=False,
    )
```
